32 devices in a mesh: dp: 8 (over z, x), fsdp: 4 (over y, core).
Axes of the slice: x: 2, y: 2, z: 4, core: 2. Of those that a mesh axis runs over, the one named last changes fastest.
Arguments:
- tokens: bfloat16 [128, 128, 768], P(('dp', 'fsdp')), may hold values from -6 to 6
- memory: bfloat16 [128, 1024, 768], P(('dp', 'fsdp')), may hold values from -6 to 6
- tgt_len: int32 [128], P(('dp', 'fsdp')), may hold values from 58 to 114
- enc_len: int32 [128], P(('dp', 'fsdp')), may hold values from 256 to 1024, as said below
- ex_count: int32 [32], P(('dp', 'fsdp')), may hold values from 2 to 4, as said below
- self_gain: bfloat16 [768], P('fsdp'), may hold values from 0.5 to 1.5
- self_q: bfloat16 [768, 768], P('fsdp'), may hold values from -0.0546875 to 0.0546875
- self_k: bfloat16 [768, 768], P('fsdp'), may hold values from -0.21875 to 0.21875
- self_v: bfloat16 [768, 768], P('fsdp'), may hold values from -0.21875 to 0.21875
- self_out: bfloat16 [768, 768], P('fsdp'), may hold values from -0.625 to 0.625
- rel_bias: bfloat16 [32, 12], P('fsdp'), may hold values from -4 to 4
- cross_gain: bfloat16 [768], P('fsdp'), may hold values from 0.5 to 1.5
- cross_q: bfloat16 [768, 768], P('fsdp'), may hold values from -0.0546875 to 0.0546875
- cross_k: bfloat16 [768, 768], P('fsdp'), may hold values from -0.21875 to 0.21875
- cross_v: bfloat16 [768, 768], P('fsdp'), may hold values from -0.21875 to 0.21875
- cross_out: bfloat16 [768, 768], P('fsdp'), may hold values from -0.625 to 0.625
- ff_gain: bfloat16 [768], P('fsdp'), may hold values from 0.5 to 1.5
- ff_in: bfloat16 [768, 3072], P('fsdp'), may hold values from -0.21875 to 0.21875
- ff_out: bfloat16 [3072, 768], P('fsdp'), may hold values from -0.15625 to 0.15625
- cotangent: bfloat16 [128, 128, 768], P(('dp', 'fsdp')), may hold values from -6 to 6
Outputs:
- output: bfloat16 [128, 128, 768], P(('dp', 'fsdp'))
- tokens_grad: float32 [128, 128, 768], P(('dp', 'fsdp'))
- memory_grad: float32 [128, 1024, 768], P(('dp', 'fsdp'))
- self_gain_grad: float32 [768], P('fsdp')
- self_q_grad: float32 [768, 768], P('fsdp')
- self_k_grad: float32 [768, 768], P('fsdp')
- self_v_grad: float32 [768, 768], P('fsdp')
- self_out_grad: float32 [768, 768], P('fsdp')
- rel_bias_grad: float32 [32, 12], P('fsdp')
- cross_gain_grad: float32 [768], P('fsdp')
- cross_q_grad: float32 [768, 768], P('fsdp')
- cross_k_grad: float32 [768, 768], P('fsdp')
- cross_v_grad: float32 [768, 768], P('fsdp')
- cross_out_grad: float32 [768, 768], P('fsdp')
- ff_gain_grad: float32 [768], P('fsdp')
- ff_in_grad: float32 [768, 3072], P('fsdp')
- ff_out_grad: float32 [3072, 768], P('fsdp')
The draws below stay inside these ranges and needn't reach their ends.
Inputs may be any that keep to these rules, and one draw needn't show every extreme that they name: `enc_len`: the 4 slots of one device share a bucket: their encoder lengths lie between half and all of a bucket top of 512, 768 or 1024. `ex_count`: slots of a device at or beyond its count hold no example.
All inputs are finite; a program needn't handle non-finite values.
Results may differ from the reference program's by a relative error of at most 0.025.
The reference program's roundings to bfloat16 on the way count: a program that leaves them out, or rounds other values in their place, can miss the bound.
Values may be sent and summed in bfloat16 or wider, within the bound.
No kernel may reach another device: no remote copies, remote signals or barrier semaphores. Data moves between devices by JAX's collectives and lax.ppermute only.
A program may use at most 256 MiB of HBM per device.

```python
import math
import jax
import jax.numpy as jnp
from jax import lax

D = 768
H = 12
DH = 64
FF = 3072
NB = 32
B_DEV = 4
LT = 128
TMAX = 114
LE = 1024
SLOTS = 128
GROUPS = 32


def draw_tgt_len(key, part):
    lengths = jax.random.randint(key, (SLOTS,), TMAX // 2 + 1, TMAX + 1)
    longest_at = jax.random.randint(jax.random.fold_in(key, 7), (), 0, SLOTS)
    return lengths.at[longest_at].set(TMAX).astype(jnp.int32)


def draw_enc_len(key, part):
    groups_count = SLOTS // B_DEV
    bucket_top = LE * jax.random.randint(jax.random.fold_in(key, 3), (groups_count, 1), 2, 5) // 4
    fullest_group = jax.random.randint(jax.random.fold_in(key, 9), (), 0, groups_count)
    bucket_top = bucket_top.at[fullest_group, 0].set(LE)
    lengths = jax.random.randint(jax.random.fold_in(key, 5), (groups_count, B_DEV), bucket_top // 2, bucket_top + 1)
    fullest_slot = jax.random.randint(jax.random.fold_in(key, 13), (), 0, B_DEV)
    lengths = lengths.at[fullest_group, fullest_slot].set(LE)
    return lengths.reshape(SLOTS).astype(jnp.int32)


def draw_ex_count(key, part):
    counts = jax.random.randint(key, (GROUPS,), B_DEV // 2, B_DEV + 1)
    fullest_at = jax.random.randint(jax.random.fold_in(key, 11), (), 0, GROUPS)
    return counts.at[fullest_at].set(B_DEV).astype(jnp.int32)


def level_of(rng, shape, cuts, least, largest):
    loudness = 1.0
    for axis_at, blocks in cuts:
        heights = jax.random.uniform(jax.random.fold_in(jax.random.fold_in(rng, 6), axis_at), (blocks,), jnp.float32, least / len(cuts), largest / len(cuts))
        loudness = loudness * jnp.repeat(jnp.exp(heights), shape[axis_at] // blocks).reshape((-1,) + (1,) * (len(shape) - 1 - axis_at))
    return loudness


def normal_values(rng, dims, deviation, most, pieces=(), kind=jnp.bfloat16):
    drawn = jax.random.normal(rng, dims, jnp.float32) * deviation
    if len(pieces) > 0:
        drawn = level_of(rng, dims, pieces, -0.22, 0.18) * drawn
    return jnp.clip(drawn, min=-most, max=most).astype(kind)


def setup_inputs(seed: int = 0) -> dict:
    arg_keys = jax.random.split(jax.random.key(seed), 21)
    tokens = normal_values(arg_keys[0], (SLOTS, LT, D), 1.0, 6.0, ((0, 32),))
    memory = normal_values(arg_keys[1], (SLOTS, LE, D), 1.0, 6.0, ((0, 32),))
    tgt_len = draw_tgt_len(jax.random.fold_in(arg_keys[20], 71), 0)
    enc_len = draw_enc_len(jax.random.fold_in(arg_keys[20], 71), 0)
    ex_count = draw_ex_count(jax.random.fold_in(arg_keys[20], 71), 0)
    self_gain = jnp.clip(1.0 + 0.1 * jax.random.normal(arg_keys[5], (D,), jnp.float32), 0.5, 1.5).astype(jnp.bfloat16)
    self_q = normal_values(arg_keys[6], (D, D), (16 * D) ** -0.5, 0.0546875, ((0, 4),))
    self_k = normal_values(arg_keys[7], (D, D), D ** -0.5, 0.21875, ((0, 4),))
    self_v = normal_values(arg_keys[8], (D, D), D ** -0.5, 0.21875, ((0, 4),))
    self_out = normal_values(arg_keys[9], (D, D), (D // 8) ** -0.5, 0.625, ((0, 4),))
    rel_bias = normal_values(arg_keys[10], (NB, H), 1.0, 4.0, ((0, 4),))
    cross_gain = jnp.clip(1.0 + 0.1 * jax.random.normal(arg_keys[11], (D,), jnp.float32), 0.5, 1.5).astype(jnp.bfloat16)
    cross_q = normal_values(arg_keys[12], (D, D), (16 * D) ** -0.5, 0.0546875, ((0, 4),))
    cross_k = normal_values(arg_keys[13], (D, D), D ** -0.5, 0.21875, ((0, 4),))
    cross_v = normal_values(arg_keys[14], (D, D), D ** -0.5, 0.21875, ((0, 4),))
    cross_out = normal_values(arg_keys[15], (D, D), (D // 8) ** -0.5, 0.625, ((0, 4),))
    ff_gain = jnp.clip(1.0 + 0.1 * jax.random.normal(arg_keys[16], (D,), jnp.float32), 0.5, 1.5).astype(jnp.bfloat16)
    ff_in = normal_values(arg_keys[17], (D, FF), D ** -0.5, 0.21875, ((0, 4),))
    ff_out = normal_values(arg_keys[18], (FF, D), (FF // 2) ** -0.5, 0.15625, ((0, 4),))
    cotangent = normal_values(arg_keys[19], (SLOTS, LT, D), 1.0, 6.0, ((0, 32),))
    return {"tokens": tokens, "memory": memory, "tgt_len": tgt_len, "enc_len": enc_len, "ex_count": ex_count, "self_gain": self_gain, "self_q": self_q, "self_k": self_k, "self_v": self_v, "self_out": self_out, "rel_bias": rel_bias, "cross_gain": cross_gain, "cross_q": cross_q, "cross_k": cross_k, "cross_v": cross_v, "cross_out": cross_out, "ff_gain": ff_gain, "ff_in": ff_in, "ff_out": ff_out, "cotangent": cotangent}


bucket_edges = [math.ceil(16 * 8 ** (exponent / 16)) for exponent in range(1, 16)]
highest = lax.Precision.HIGHEST

@jax.custom_vjp
def low(v):
    return lax.optimization_barrier(v.astype(jnp.bfloat16)).astype(jnp.float32)

@jax.custom_vjp
def low_back(v):
    return v

def low_keep(v):
    return (low(v), None)

def low_pass(kept, grad):
    return (grad,)

def back_keep(v):
    return (v, None)

def back_low(kept, grad):
    return (low(grad),)
low.defvjp(low_keep, low_pass)
low_back.defvjp(back_keep, back_low)

def bucket_ids(length):
    positions = jnp.arange(length, dtype=jnp.int32)
    distance = jnp.maximum(positions[:, None] - positions[None, :], 0)
    buckets = jnp.minimum(distance, 16)
    for bucket_edge in bucket_edges:
        buckets = buckets + (distance >= bucket_edge).astype(jnp.int32)
    return buckets

def rms_norm(hidden, gain_vec):
    return hidden * lax.rsqrt(lax.optimization_barrier(jnp.mean(hidden * hidden, axis=-1, keepdims=True)) + 1e-06) * gain_vec

def split_heads(values):
    return values.reshape(values.shape[0], values.shape[1], H, DH).transpose(0, 2, 1, 3)

def join_heads(values):
    return values.transpose(0, 2, 1, 3).reshape(values.shape[0], values.shape[2], H * DH)

def project(values, matrix):
    return jnp.einsum('bld,de->ble', values, matrix, precision=highest)

def attend(queries, keys_in, values, allowed, pos_bias):
    scores = jnp.einsum('bhid,bhjd->bhij', split_heads(queries), split_heads(keys_in), precision=highest) + pos_bias
    scores = low_back(jnp.where(allowed, scores, -1000000000.0))
    weights = low(jax.nn.softmax(scores, axis=-1))
    mixed_heads = jnp.einsum('bhij,bhjd->bhid', weights, split_heads(values), precision=highest)
    return low(low_back(join_heads(mixed_heads)))

def layer(params, tokens, memory, self_ok, cross_ok, row_live, onehot):
    self_gain, self_q, self_k, self_v, self_out, rel_bias, cross_gain, cross_q, cross_k, cross_v, cross_out, ff_gain, ff_in, ff_out = params
    pos_bias = jnp.einsum('ijn,nh->hij', onehot, rel_bias, precision=highest)[None]
    normed = low(rms_norm(tokens, self_gain))
    queries = low(low_back(project(normed, self_q)))
    keys_self = low(low_back(project(normed, self_k)))
    values_self = low(low_back(project(normed, self_v)))
    first = tokens + low_back(project(attend(queries, keys_self, values_self, self_ok, pos_bias), self_out))
    normed = low(rms_norm(first, cross_gain))
    queries = low(low_back(project(normed, cross_q)))
    keys_cross = low(low_back(project(memory, cross_k)))
    values_cross = low(low_back(project(memory, cross_v)))
    second = first + low_back(project(attend(queries, keys_cross, values_cross, cross_ok, 0.0), cross_out))
    normed = low(rms_norm(second, ff_gain))
    hidden_units = low(jax.nn.gelu(low_back(project(normed, ff_in)), approximate=True))
    third = second + low_back(project(hidden_units, ff_out))
    return third * row_live[:, :, None]

def reference(tokens, memory, tgt_len, enc_len, ex_count, self_gain, self_q, self_k, self_v, self_out, rel_bias, cross_gain, cross_q, cross_k, cross_v, cross_out, ff_gain, ff_in, ff_out, cotangent):
    params = tuple((weight.astype(jnp.float32) for weight in (self_gain, self_q, self_k, self_v, self_out, rel_bias, cross_gain, cross_q, cross_k, cross_v, cross_out, ff_gain, ff_in, ff_out)))
    groups_count = ex_count.shape[0]
    positions = jnp.arange(LT, dtype=jnp.int32)
    enc_positions = jnp.arange(LE, dtype=jnp.int32)
    onehot = (bucket_ids(LT)[:, :, None] == jnp.arange(NB, dtype=jnp.int32)).astype(jnp.float32)

    def by_group(values):
        return values.reshape((groups_count, B_DEV) + values.shape[1:])

    def one_group(summed, group_item):
        tok_group, mem_group, tgt_group, enc_group, count_group, cot_group = group_item
        slot_live = jnp.arange(B_DEV, dtype=jnp.int32) < count_group
        row_live = (slot_live[:, None] & (positions[None, :] < tgt_group[:, None])).astype(jnp.float32)
        self_ok = ((positions[None, None, :] <= positions[None, :, None]) & (positions[None, None, :] < tgt_group[:, None, None]))[:, None]
        cross_ok = (enc_positions[None, :] < enc_group[:, None])[:, None, None, :]

        def forward(prm, inputs, mem):
            return layer(prm, inputs, mem, self_ok, cross_ok, row_live, onehot)
        result, pullback = jax.vjp(forward, params, tok_group.astype(jnp.float32), mem_group.astype(jnp.float32))
        grad_params, grad_tokens, grad_memory = pullback(cot_group.astype(jnp.float32))
        summed = tuple((left + right for left, right in zip(summed, grad_params)))
        return (summed, (result.astype(jnp.bfloat16), grad_tokens, grad_memory))
    zeros = tuple((jnp.zeros_like(weight) for weight in params))
    summed, (results, grad_tokens, grad_memory) = lax.scan(one_group, zeros, (by_group(tokens), by_group(memory), by_group(tgt_len), by_group(enc_len), ex_count, by_group(cotangent)))
    output = results.reshape(tokens.shape)
    tokens_grad = grad_tokens.reshape(tokens.shape)
    memory_grad = grad_memory.reshape(memory.shape)
    return (output, tokens_grad, memory_grad, summed[0], summed[1], summed[2], summed[3], summed[4], summed[5], summed[6], summed[7], summed[8], summed[9], summed[10], summed[11], summed[12], summed[13])
```

```python
import math

import jax
import jax.numpy as jnp
from jax import lax
from jax.sharding import PartitionSpec as P

H = 12
DH = 64


bucket_edges = [math.ceil(16 * 8 ** (exponent / 16)) for exponent in range(1, 16)]
highest = lax.Precision.HIGHEST


def bucket_ids(length):
    positions = jnp.arange(length, dtype=jnp.int32)
    distance = jnp.maximum(positions[:, None] - positions[None, :], 0)
    buckets = jnp.minimum(distance, 16)
    for bucket_edge in bucket_edges:
        buckets = buckets + (distance >= bucket_edge).astype(jnp.int32)
    return buckets


def rms_norm(hidden, gain_vec):
    return hidden * lax.rsqrt(jnp.mean(hidden * hidden, axis=-1, keepdims=True) + 1e-06) * gain_vec


def norm_back(hidden, gain_vec, upstream):
    _, pullback = jax.vjp(rms_norm, hidden, gain_vec)
    return pullback(upstream)


def smooth_gate(values):
    return jax.nn.gelu(values, approximate=True)


def smooth_back(values, upstream):
    _, pullback = jax.vjp(smooth_gate, values)
    return pullback(upstream)[0]


def flip(values, axis, bit):
    size = lax.axis_size(axis)
    return lax.ppermute(values, axis, [(i, i ^ bit) for i in range(size)])


def pick(values, index):
    return lax.dynamic_index_in_dim(values, index, 0, keepdims=False)


def gather_rows(own):
    shard = lax.axis_index("fsdp")
    side = lax.axis_index("dp") % 2
    halves = own.reshape((2, own.shape[0] // 2) + own.shape[1:])
    beside = flip(own, "fsdp", 1)
    direct = flip(pick(halves, side), "fsdp", 2)
    passed = flip(direct, "dp", 1)
    far = jnp.where(side == 0, jnp.stack([direct, passed]), jnp.stack([passed, direct])).reshape(own.shape)
    far_beside = flip(far, "fsdp", 1)
    relative = jnp.stack([own, beside, far, far_beside])
    return [pick(relative, shard ^ j) for j in range(4)]


def add_low(left, right):
    return (left.astype(jnp.float32) + right.astype(jnp.float32)).astype(jnp.bfloat16)


def reduce_rows(full):
    shard = lax.axis_index("fsdp")
    mine, other, far, far_other = (pick(full, shard ^ j) for j in range(4))
    got_mine = flip(other, "fsdp", 1)
    got_far = flip(far_other, "fsdp", 1)
    part = add_low(add_low(mine, got_mine), flip(add_low(far, got_far), "fsdp", 2))
    place = lax.axis_index("dp")
    count = lax.axis_size("dp")
    bit = 1
    while bit < count:
        side = (place // bit) % 2
        halves = part.reshape((2, part.shape[0] // 2) + part.shape[1:])
        part = add_low(pick(halves, side), flip(pick(halves, 1 - side), "dp", bit))
        bit *= 2
    while bit > 1:
        bit //= 2
        side = (place // bit) % 2
        got = flip(part, "dp", bit)
        part = jnp.where(side == 0, jnp.concatenate([part, got]), jnp.concatenate([got, part]))
    return part.astype(jnp.float32)


def sum_small(values):
    for axis in ("fsdp", "dp"):
        bit = 1
        while bit < lax.axis_size(axis):
            values = values + flip(values, axis, bit)
            bit *= 2
    return values


def by_shard(gradient):
    return gradient.astype(jnp.bfloat16).reshape((4, gradient.shape[0] // 4, gradient.shape[1]))


def split_heads(values):
    return values.reshape(values.shape[0], values.shape[1], H, DH).transpose(0, 2, 1, 3)


def join_heads(values):
    return values.transpose(0, 2, 1, 3).reshape(values.shape[0], values.shape[2], H * DH)


def project(values, matrix):
    return jnp.einsum("bld,de->ble", values, matrix, preferred_element_type=jnp.float32)


def project_back(grads_in, matrix):
    return jnp.einsum("ble,de->bld", grads_in, matrix, preferred_element_type=jnp.float32)


def matrix_grad(values, grads_in):
    return jnp.einsum("bld,ble->de", values, grads_in, preferred_element_type=jnp.float32)


def attn_scores(queries, keys_in, allowed, pos_bias):
    scores = (
        jnp.einsum(
            "bhid,bhjd->bhij",
            split_heads(queries),
            split_heads(keys_in),
            preferred_element_type=jnp.float32,
        )
        + pos_bias
    )
    return jnp.where(allowed, scores, -1000000000.0)


def attend_forward(queries, keys_in, values, allowed, pos_bias):
    scores = attn_scores(queries, keys_in, allowed, pos_bias)
    row_max = jnp.max(scores, axis=-1, keepdims=True)
    log_total = row_max + jnp.log(jnp.sum(jnp.exp(scores - row_max), axis=-1, keepdims=True))
    weights = jnp.exp(scores - log_total).astype(jnp.bfloat16)
    mixed_heads = jnp.einsum(
        "bhij,bhjd->bhid", weights, split_heads(values), preferred_element_type=jnp.float32
    )
    return (join_heads(mixed_heads).astype(jnp.bfloat16), log_total)


def attend_backward(queries, keys_in, values, allowed, pos_bias, log_total, grad_mixed):
    scores = attn_scores(queries, keys_in, allowed, pos_bias)
    probability = jnp.exp(scores - log_total)
    grad_heads = split_heads(grad_mixed)
    grad_probs = jnp.einsum(
        "bhid,bhjd->bhij", grad_heads, split_heads(values), preferred_element_type=jnp.float32
    )
    grad_values = jnp.einsum(
        "bhij,bhid->bhjd",
        probability.astype(jnp.bfloat16),
        grad_heads,
        preferred_element_type=jnp.float32,
    )
    grad_scores = (
        probability * (grad_probs - jnp.sum(probability * grad_probs, axis=-1, keepdims=True))
    ).astype(jnp.bfloat16)
    grad_queries = jnp.einsum(
        "bhij,bhjd->bhid", grad_scores, split_heads(keys_in), preferred_element_type=jnp.float32
    )
    grad_keys = jnp.einsum(
        "bhij,bhid->bhjd", grad_scores, split_heads(queries), preferred_element_type=jnp.float32
    )
    return (
        join_heads(grad_queries).astype(jnp.bfloat16),
        join_heads(grad_keys).astype(jnp.bfloat16),
        join_heads(grad_values).astype(jnp.bfloat16),
        grad_scores,
    )


def on_device(
    tokens,
    memory,
    tgt_len,
    enc_len,
    ex_count,
    self_gain,
    self_q,
    self_k,
    self_v,
    self_out,
    rel_bias,
    cross_gain,
    cross_q,
    cross_k,
    cross_v,
    cross_out,
    ff_gain,
    ff_in,
    ff_out,
    cotangent,
):
    rows = self_q.shape[0]
    model = tokens.shape[2]

    def bundle(*weights):
        blocks = gather_rows(jnp.stack(weights, axis=1).reshape(rows, len(weights) * model))
        whole = jnp.concatenate(blocks, axis=0).reshape(4 * rows, len(weights), model)
        return [whole[:, i] for i in range(len(weights))]

    key_cross, value_cross = bundle(cross_k, cross_v)
    query_self, key_self, value_self, out_self, query_cross, out_cross = bundle(
        self_q, self_k, self_v, self_out, cross_q, cross_out
    )
    ff_wide = jnp.concatenate(gather_rows(ff_in), axis=0)
    ff_narrow = jnp.concatenate(gather_rows(ff_out), axis=0)
    packed = jnp.concatenate([self_gain, cross_gain, ff_gain, rel_bias.reshape(-1)])
    packed = jnp.pad(packed, (0, model - packed.shape[0]))[None]
    shard = lax.axis_index("fsdp")
    near = jnp.stack([packed] + [flip(packed, "fsdp", j) for j in (1, 2, 3)])
    small = jnp.concatenate([pick(near, shard ^ j) for j in range(4)], axis=0)
    gain_one = small[:, :rows].reshape(-1)
    gain_two = small[:, rows : 2 * rows].reshape(-1)
    gain_three = small[:, 2 * rows : 3 * rows].reshape(-1)
    bias_table = small[:, 3 * rows : 3 * rows + rel_bias.size].reshape(-1, H)
    gain_one = gain_one.astype(jnp.float32)
    gain_two = gain_two.astype(jnp.float32)
    gain_three = gain_three.astype(jnp.float32)
    positions = jnp.arange(tokens.shape[1], dtype=jnp.int32)
    slot_live = jnp.arange(tokens.shape[0], dtype=jnp.int32) < ex_count[0]
    row_live = (slot_live[:, None] & (positions[None, :] < tgt_len[:, None])).astype(jnp.float32)
    self_ok = (
        (positions[None, None, :] <= positions[None, :, None])
        & (positions[None, None, :] < tgt_len[:, None, None])
    )[:, None]
    cross_ok = (jnp.arange(memory.shape[1], dtype=jnp.int32)[None, :] < enc_len[:, None])[
        :, None, None, :
    ]
    onehot = (
        bucket_ids(tokens.shape[1])[:, :, None] == jnp.arange(bias_table.shape[0], dtype=jnp.int32)
    ).astype(jnp.float32)
    pos_bias = jnp.einsum("ijn,nh->hij", onehot, bias_table.astype(jnp.float32), precision=highest)[
        None
    ]
    inputs = tokens.astype(jnp.float32)
    normed_one = rms_norm(inputs, gain_one).astype(jnp.bfloat16)
    queries_one = project(normed_one, query_self).astype(jnp.bfloat16)
    keys_one = project(normed_one, key_self).astype(jnp.bfloat16)
    values_one = project(normed_one, value_self).astype(jnp.bfloat16)
    attended_one, log_one = attend_forward(queries_one, keys_one, values_one, self_ok, pos_bias)
    first = inputs + project(attended_one, out_self)
    normed_two = rms_norm(first, gain_two).astype(jnp.bfloat16)
    queries_two = project(normed_two, query_cross).astype(jnp.bfloat16)
    keys_two = project(memory, key_cross).astype(jnp.bfloat16)
    values_two = project(memory, value_cross).astype(jnp.bfloat16)
    attended_two, log_two = attend_forward(queries_two, keys_two, values_two, cross_ok, 0.0)
    second = first + project(attended_two, out_cross)
    normed_three = rms_norm(second, gain_three).astype(jnp.bfloat16)
    ff_pre = project(normed_three, ff_wide)
    hidden_units = smooth_gate(ff_pre).astype(jnp.bfloat16)
    third = second + project(hidden_units, ff_narrow)
    output = (third * row_live[:, :, None]).astype(jnp.bfloat16)
    back_sq, back_sk, back_sv, back_so = query_self, key_self, value_self, out_self
    back_cq, back_ck, back_cv, back_co = query_cross, key_cross, value_cross, out_cross
    back_wide, back_narrow = ff_wide, ff_narrow
    grad_third = cotangent.astype(jnp.float32) * row_live[:, :, None]
    grad_ffout = grad_third.astype(jnp.bfloat16)
    grad_narrow = matrix_grad(hidden_units, grad_ffout)
    grad_hidden = project_back(grad_ffout, back_narrow)
    grad_pre = smooth_back(ff_pre, grad_hidden).astype(jnp.bfloat16)
    grad_wide = matrix_grad(normed_three, grad_pre)
    grad_normed = project_back(grad_pre, back_wide)
    grad_back, grad_gthree = norm_back(second, gain_three, grad_normed)
    grad_second = grad_third + grad_back
    grad_crossout = grad_second.astype(jnp.bfloat16)
    grad_co = matrix_grad(attended_two, grad_crossout)
    grad_att_two = project_back(grad_crossout, back_co).astype(jnp.bfloat16)
    grad_qtwo, grad_ktwo, grad_vtwo, _ = attend_backward(
        queries_two, keys_two, values_two, cross_ok, 0.0, log_two, grad_att_two
    )
    grad_cq = matrix_grad(normed_two, grad_qtwo)
    grad_ck = matrix_grad(memory, grad_ktwo)
    grad_cv = matrix_grad(memory, grad_vtwo)
    memory_grad = project_back(grad_ktwo, back_ck) + project_back(grad_vtwo, back_cv)
    grad_normed = project_back(grad_qtwo, back_cq)
    grad_back, grad_gtwo = norm_back(first, gain_two, grad_normed)
    grad_first = grad_second + grad_back
    grad_selfout = grad_first.astype(jnp.bfloat16)
    grad_so = matrix_grad(attended_one, grad_selfout)
    grad_att_one = project_back(grad_selfout, back_so).astype(jnp.bfloat16)
    grad_qone, grad_kone, grad_vone, grad_scores = attend_backward(
        queries_one, keys_one, values_one, self_ok, pos_bias, log_one, grad_att_one
    )
    grad_rel = jnp.einsum(
        "ijn,hij->nh", onehot, jnp.sum(grad_scores.astype(jnp.float32), axis=0), precision=highest
    )
    grad_sq = matrix_grad(normed_one, grad_qone)
    grad_sk = matrix_grad(normed_one, grad_kone)
    grad_sv = matrix_grad(normed_one, grad_vone)
    grad_normed = (
        project_back(grad_qone, back_sq)
        + project_back(grad_kone, back_sk)
        + project_back(grad_vone, back_sv)
    )
    grad_back, grad_gone = norm_back(inputs, gain_one, grad_normed)
    tokens_grad = grad_first + grad_back
    sum_narrow = reduce_rows(by_shard(grad_narrow))
    sum_wide = reduce_rows(by_shard(grad_wide))

    def reduce_four(*gradients):
        total = reduce_rows(jnp.concatenate([by_shard(g) for g in gradients], axis=1))
        return [total[i * rows : (i + 1) * rows] for i in range(len(gradients))]

    sum_co, sum_ck, sum_cv, sum_cq = reduce_four(grad_co, grad_ck, grad_cv, grad_cq)
    sum_so, sum_sq, sum_sk, sum_sv = reduce_four(grad_so, grad_sq, grad_sk, grad_sv)
    tiny = jnp.concatenate(
        [g.reshape(4, -1) for g in (grad_gone, grad_gtwo, grad_gthree, grad_rel)], axis=1
    )
    tiny = pick(sum_small(tiny), shard)
    return (
        output,
        tokens_grad,
        memory_grad,
        tiny[:rows],
        sum_sq,
        sum_sk,
        sum_sv,
        sum_so,
        tiny[3 * rows :].reshape(rel_bias.shape),
        tiny[rows : 2 * rows],
        sum_cq,
        sum_ck,
        sum_cv,
        sum_co,
        tiny[2 * rows : 3 * rows],
        sum_wide,
        sum_narrow,
    )


def solution(mesh):
    in_specs = (
        P(("dp", "fsdp"), None, None),
        P(("dp", "fsdp"), None, None),
        P(("dp", "fsdp")),
        P(("dp", "fsdp")),
        P(("dp", "fsdp")),
        P("fsdp"),
        P("fsdp", None),
        P("fsdp", None),
        P("fsdp", None),
        P("fsdp", None),
        P("fsdp", None),
        P("fsdp"),
        P("fsdp", None),
        P("fsdp", None),
        P("fsdp", None),
        P("fsdp", None),
        P("fsdp"),
        P("fsdp", None),
        P("fsdp", None),
        P(("dp", "fsdp"), None, None),
    )
    out_specs = (
        P(("dp", "fsdp"), None, None),
        P(("dp", "fsdp"), None, None),
        P(("dp", "fsdp"), None, None),
        P("fsdp"),
        P("fsdp", None),
        P("fsdp", None),
        P("fsdp", None),
        P("fsdp", None),
        P("fsdp", None),
        P("fsdp"),
        P("fsdp", None),
        P("fsdp", None),
        P("fsdp", None),
        P("fsdp", None),
        P("fsdp"),
        P("fsdp", None),
        P("fsdp", None),
    )
    return jax.shard_map(
        on_device, mesh=mesh, in_specs=in_specs, out_specs=out_specs, check_vma=False
    )
```

```python
import functools
import math

import jax
import jax.numpy as jnp
from jax import lax
from jax.experimental import pallas as pl
from jax.experimental.pallas import tpu as pltpu
from jax.sharding import PartitionSpec as P

H = 12
DH = 64
QUAD = 4
QUADS = H // QUAD
WIDE = QUAD * DH
CHUNK = 256
MASKED = -1000000000.0

bucket_edges = [math.ceil(16 * 8 ** (exponent / 16)) for exponent in range(1, 16)]
highest = lax.Precision.HIGHEST
f32 = jnp.float32
bf16 = jnp.bfloat16


def bucket_ids(length):
    positions = jnp.arange(length, dtype=jnp.int32)
    distance = jnp.maximum(positions[:, None] - positions[None, :], 0)
    buckets = jnp.minimum(distance, 16)
    for bucket_edge in bucket_edges:
        buckets = buckets + (distance >= bucket_edge).astype(jnp.int32)
    return buckets


def flip(values, axis, bit):
    size = lax.axis_size(axis)
    return lax.ppermute(values, axis, [(i, i ^ bit) for i in range(size)])


def pick(values, index):
    return lax.dynamic_index_in_dim(values, index, 0, keepdims=False)


def gather_pieces(own, side):
    half = own.shape[1] // 2
    beside = flip(own, "fsdp", 1)
    direct = flip(lax.dynamic_slice_in_dim(own, side * half, half, 1), "fsdp", 2)
    passed = flip(direct, "dp", 1)
    return (own, beside, direct, passed, flip(direct, "fsdp", 1), flip(passed, "fsdp", 1))


def add_low(left, right):
    return (left.astype(f32) + right.astype(f32)).astype(bf16)


def reduce_rows(keep, send):
    near = add_low(keep, flip(send, "fsdp", 1))
    part = add_low(near[0], flip(near[1], "fsdp", 2))
    place = lax.axis_index("dp")
    count = lax.axis_size("dp")
    bit = 1
    while bit < count:
        side = (place // bit) % 2
        halves = part.reshape((2, part.shape[0] // 2) + part.shape[1:])
        part = add_low(pick(halves, side), flip(pick(halves, 1 - side), "dp", bit))
        bit *= 2
    while bit > 1:
        bit //= 2
        side = (place // bit) % 2
        got = flip(part, "dp", bit)
        part = jnp.where(side == 0, jnp.concatenate([part, got]), jnp.concatenate([got, part]))
    return part.astype(f32)


def sum_small(values):
    for axis in ("fsdp", "dp"):
        bit = 1
        while bit < lax.axis_size(axis):
            values = values + flip(values, axis, bit)
            bit *= 2
    return values


def mm(left, right):
    return jnp.dot(left, right, preferred_element_type=f32)


def mm_nt(left, right):
    return lax.dot_general(left, right, (((1,), (1,)), ((), ())), preferred_element_type=f32)


def mm_tn(left, right):
    return lax.dot_general(left, right, (((0,), (0,)), ((), ())), preferred_element_type=f32)


def copies_in(meta, pieces, whole, sems, only=slice(None)):
    shard, side = meta[0], meta[1]
    rows = pieces[0].shape[1]
    half = rows // 2
    starts = (
        shard * rows,
        (shard ^ 1) * rows,
        (shard ^ 2) * rows + side * half,
        (shard ^ 2) * rows + (1 - side) * half,
        (shard ^ 3) * rows + side * half,
        (shard ^ 3) * rows + (1 - side) * half,
    )
    return [
        pltpu.make_async_copy(
            piece.at[only],
            whole.at[:, pl.ds(pl.multiple_of(start, 32), piece.shape[1])],
            sems.at[i],
        )
        for i, (piece, start) in enumerate(zip(pieces, starts))
    ]


def start_all(copies):
    for copy in copies:
        copy.start()


def wait_all(copies):
    for copy in copies:
        copy.wait()


def copies_out(meta, whole, keep, send, at, sems):
    shard = meta[0]
    rows = whole.shape[0] // 4
    return [
        pltpu.make_async_copy(
            whole.at[pl.ds(pl.multiple_of((shard ^ j) * rows, 32), rows)],
            (send if j % 2 else keep).at[j // 2, pl.ds(at * rows, rows)],
            sems.at[j],
        )
        for j in range(4)
    ]


def norm_rho(hidden):
    return lax.rsqrt(jnp.mean(hidden * hidden, axis=-1, keepdims=True) + 1e-06)


def norm_back(hidden, gain, upstream):
    rho = norm_rho(hidden)
    scaled = upstream * gain
    inner = jnp.mean(scaled * hidden, axis=-1, keepdims=True)
    grad = rho * scaled - hidden * (rho * rho * rho * inner)
    return grad, jnp.sum(upstream * hidden * rho, axis=0, keepdims=True)


def head_masks():
    lane = lax.broadcasted_iota(jnp.int32, (1, WIDE), 1) // DH
    return [(lane == h).astype(f32).astype(bf16) for h in range(QUAD)]


def stack_heads(values, masks):
    return jnp.concatenate([values * mask for mask in masks], axis=0)


def own_heads(mixed):
    rows = mixed.shape[1] // QUAD
    own = [mixed[h * DH : (h + 1) * DH, h * rows : (h + 1) * rows] for h in range(QUAD)]
    return jnp.concatenate(own, axis=0).T


def head_sums(product):
    high = product.astype(bf16)
    low = (product - high.astype(f32)).astype(bf16)
    ones = jnp.ones((8, WIDE), bf16)
    return (mm_nt(ones, high) + mm_nt(ones, low))[0:1]


def fold(values, op):
    return op(values.reshape(values.shape[0] // 8, 8, values.shape[1]), axis=0)


def quad_at(quad):
    return pl.ds(quad * WIDE, WIDE)


def memory_kernel(meta, memory, *refs):
    pieces, (keys, values, whole, sems) = refs[:6], refs[6:]
    slot = pl.program_id(0)

    @pl.when(slot == 0)
    def _():
        copies = copies_in(meta, pieces, whole, sems)
        start_all(copies)
        wait_all(copies)

    def chunk(c, carry):
        rows = pl.ds(c * CHUNK, CHUNK)
        block = memory[0, rows, :]
        keys[0, rows, :] = mm(block, whole[0]).astype(bf16)
        values[0, rows, :] = mm(block, whole[1]).astype(bf16)
        return carry

    lax.fori_loop(0, meta[12 + slot], chunk, 0)


def self_kernel(meta, tokens, gains, bias, *refs):
    pieces = refs[:6]
    normed_out, q_out, k_out, v_out, mixed_out, h1_out, normed2_out, q2_out, lse_out, whole, sems = refs[6:]
    copies = copies_in(meta, pieces, whole, sems)
    start_all(copies)
    hidden = tokens[...].astype(f32)
    normed = (hidden * norm_rho(hidden) * gains[0:1]).astype(bf16)
    normed_out[...] = normed
    wait_all(copies)
    q_out[...] = mm(normed, whole[0]).astype(bf16)
    k_out[...] = mm(normed, whole[1]).astype(bf16)
    v_out[...] = mm(normed, whole[2]).astype(bf16)
    mixed_out[...] = jnp.zeros(mixed_out.shape, bf16)
    lse_out[...] = jnp.zeros(lse_out.shape, f32)
    length = bias.shape[1]

    def slot(b, carry):
        rows = pl.ds(pl.multiple_of(b * length, length), length)
        masks = head_masks()
        key_at = lax.broadcasted_iota(jnp.int32, (length, QUAD * length), 0)
        query_at = lax.broadcasted_iota(jnp.int32, (length, QUAD * length), 1) % length
        ok = (key_at <= query_at) & (key_at < meta[4 + b])
        for quad in range(QUADS):
            at = quad_at(quad)
            scores = mm_nt(k_out[rows, at], stack_heads(q_out[rows, at], masks)) + bias[quad]
            scores = jnp.where(ok, scores, MASKED)
            top = jnp.max(scores, axis=0, keepdims=True)
            raised = jnp.exp(scores - top)
            total = jnp.sum(raised, axis=0, keepdims=True)
            weights = (raised * (1.0 / total)).astype(bf16)
            mixed_out[rows, at] = own_heads(mm_tn(v_out[rows, at], weights)).astype(bf16)
            lse_out[b, quad : quad + 1, :] = top + jnp.log(total)
        return carry

    lax.fori_loop(0, meta[2], slot, 0)
    first = hidden + mm(mixed_out[...], whole[3])
    h1_out[...] = first
    normed2 = (first * norm_rho(first) * gains[1:2]).astype(bf16)
    normed2_out[...] = normed2
    q2_out[...] = mm(normed2, whole[4]).astype(bf16)


def cross_kernel(meta, queries, keys, values, mixed_out, lse_out, stacked, scores):
    slot = pl.program_id(0)
    count = meta[12 + slot]
    length = queries.shape[1]

    @pl.when(count == 0)
    def _():
        mixed_out[...] = jnp.zeros(mixed_out.shape, bf16)
        lse_out[...] = jnp.zeros(lse_out.shape, f32)

    @pl.when(count > 0)
    def _():
        masks = head_masks()
        limit = meta[8 + slot]
        for quad in range(QUADS):
            stacked[quad] = stack_heads(queries[0, :, quad_at(quad)], masks)

        def score(c, tops):
            rows = pl.ds(c * CHUNK, CHUNK)
            ok = lax.broadcasted_iota(jnp.int32, (CHUNK, 1), 0) + c * CHUNK < limit
            new = []
            for quad in range(QUADS):
                block = jnp.where(ok, mm_nt(keys[0, rows, quad_at(quad)], stacked[quad]), MASKED)
                scores[quad, rows, :] = block
                new.append(jnp.maximum(tops[quad], fold(block, jnp.max)))
            return tuple(new)

        start = tuple(jnp.full((8, QUAD * length), -jnp.inf, f32) for _ in range(QUADS))
        tops = lax.fori_loop(0, count, score, start)
        tops = [jnp.max(top, axis=0, keepdims=True) for top in tops]

        def mix(c, carry):
            rows = pl.ds(c * CHUNK, CHUNK)
            totals, mixes = [], []
            for quad in range(QUADS):
                raised = jnp.exp(scores[quad, rows, :] - tops[quad])
                totals.append(carry[0][quad] + fold(raised, jnp.sum))
                mixes.append(carry[1][quad] + mm_tn(values[0, rows, quad_at(quad)], raised.astype(bf16)))
            return tuple(totals), tuple(mixes)

        start = (
            tuple(jnp.zeros((8, QUAD * length), f32) for _ in range(QUADS)),
            tuple(jnp.zeros((WIDE, QUAD * length), f32) for _ in range(QUADS)),
        )
        totals, mixes = lax.fori_loop(0, count, mix, start)
        for quad in range(QUADS):
            total = jnp.sum(totals[quad], axis=0, keepdims=True)
            mixed_out[0, :, quad_at(quad)] = own_heads(mixes[quad] * (1.0 / total)).astype(bf16)
            lse_out[0, quad : quad + 1, :] = tops[quad] + jnp.log(total)


def gelu_both(values):
    scale = math.sqrt(2.0 / math.pi)
    square = values * values
    slope = jnp.tanh(scale * values * (1.0 + 0.044715 * square))
    half = 0.5 * (1.0 + slope)
    back = half + 0.5 * values * (1.0 - slope * slope) * (scale * (1.0 + 3 * 0.044715 * square))
    return values * half, back


def ff_kernel(meta, h1, mixed, cotangent, gains, *refs):
    square, wide, narrow, refs = refs[:6], refs[6:12], refs[12:18], refs[18:]
    (output, g2_out, ga2_out, gain_out, keep_n, send_n, keep_w, send_w, keep_o, send_o, refs) = refs[:10] + (refs[10:],)
    (co, w_in, w_out, gf, normed, grad_n, grad_w, grad_o, second, third, back, in_sems, n_sems, w_sems, o_sems) = refs
    rows_in = wide[0].shape[1]
    model = h1.shape[1]
    co_in = copies_in(meta, square, co, in_sems.at[0], pl.ds(5, 1))
    in_in = copies_in(meta, wide, w_in, in_sems.at[1])
    out_in = copies_in(meta, narrow, w_out, in_sems.at[2])
    start_all(co_in)
    start_all(in_in)
    start_all(out_in)
    positions = lax.broadcasted_iota(jnp.int32, (cotangent.shape[1], 1), 0)
    live = jnp.concatenate(
        [
            ((positions < meta[4 + b]) & (b < meta[2])).astype(f32)
            for b in range(cotangent.shape[0])
        ],
        axis=0,
    )
    g3 = cotangent[...].reshape(h1.shape).astype(f32) * live
    gf[...] = g3.astype(bf16)
    wait_all(co_in)
    second[...] = h1[...] + mm(mixed[...], co[0])
    hidden = second[...]
    normed[...] = (hidden * norm_rho(hidden) * gains[2:3]).astype(bf16)
    third[...] = hidden
    wait_all(in_in)
    wait_all(out_in)
    shard = meta[0]
    waits = []
    for j in range(4):
        cols = pl.ds(pl.multiple_of((shard ^ j) * model, model), model)
        units, slope = gelu_both(mm(normed[...], w_in[0, :, cols]))
        low = units.astype(bf16)
        third[...] += mm(low, w_out[0, cols, :])
        grad_n[j] = mm_tn(low, gf[...]).astype(bf16)
        waits.append(pltpu.make_async_copy(grad_n.at[j], (send_n if j % 2 else keep_n).at[j // 2], n_sems.at[j]))
        waits[-1].start()
        grad_units = (mm_nt(gf[...], w_out[0, cols, :]) * slope).astype(bf16)
        grad_w[j] = mm_tn(normed[...], grad_units).astype(bf16)
        for i in range(4):
            waits.append(
                pltpu.make_async_copy(
                    grad_w.at[j, pl.ds(pl.multiple_of((shard ^ i) * rows_in, 32), rows_in)],
                    (send_w if i % 2 else keep_w).at[i // 2, :, cols],
                    w_sems.at[4 * j + i],
                )
            )
            waits[-1].start()
        grad_normed = mm_nt(grad_units, w_in[0, :, cols])
        if j == 0:
            back[...] = grad_normed
        else:
            back[...] += grad_normed
    output[...] = (third[...] * live).astype(bf16)
    grad, gain = norm_back(second[...], gains[2:3], back[...])
    gain_out[...] = jnp.broadcast_to(gain, gain_out.shape)
    g2 = g3 + grad
    g2_out[...] = g2
    go2 = g2.astype(bf16)
    ga2_out[...] = mm_nt(go2, co[0]).astype(bf16)
    grad_o[...] = mm_tn(mixed[...], go2).astype(bf16)
    out = copies_out(meta, grad_o, keep_o, send_o, 0, o_sems)
    start_all(out)
    wait_all(waits)
    wait_all(out)


def cross_back_kernel(meta, queries, grads, mixed, lse, keys, values, gq_out, gk_out, gv_out, q_stack, g_stack, deltas, total):
    slot = pl.program_id(0)
    count = meta[12 + slot]

    @pl.when(count == 0)
    def _():
        gq_out[...] = jnp.zeros(gq_out.shape, bf16)

    @pl.when(count > 0)
    def _():
        masks = head_masks()
        limit = meta[8 + slot]
        for quad in range(QUADS):
            at = quad_at(quad)
            q_stack[quad] = stack_heads(queries[0, :, at], masks)
            stacked = stack_heads(grads[0, :, at], masks)
            g_stack[quad] = stacked
            tiled = jnp.concatenate([mixed[0, :, at].astype(f32)] * QUAD, axis=0)
            deltas[quad : quad + 1, :] = head_sums(stacked.astype(f32) * tiled)
        total[...] = jnp.zeros(total.shape, f32)

        def chunk(c, carry):
            rows = pl.ds(c * CHUNK, CHUNK)
            ok = lax.broadcasted_iota(jnp.int32, (CHUNK, 1), 0) + c * CHUNK < limit
            for quad in range(QUADS):
                at = quad_at(quad)
                block = keys[0, rows, at]
                scores = jnp.where(ok, mm_nt(block, q_stack[quad]), MASKED)
                share = jnp.exp(scores - lse[0, quad : quad + 1, :])
                grad_share = mm_nt(values[0, rows, at], g_stack[quad])
                grad_scores = (share * (grad_share - deltas[quad : quad + 1, :])).astype(bf16)
                gv_out[0, rows, at] = mm(share.astype(bf16), g_stack[quad]).astype(bf16)
                gk_out[0, rows, at] = mm(grad_scores, q_stack[quad]).astype(bf16)
                total[quad] += mm_tn(block, grad_scores)
            return carry

        lax.fori_loop(0, count, chunk, 0)
        for quad in range(QUADS):
            gq_out[0, :, quad_at(quad)] = own_heads(total[quad]).astype(bf16)


def self_back_kernel(meta, gq2, normed2, h1, g2, mixed, q, k, v, lse, normed, tokens, gains, bias, *refs):
    pieces, refs = refs[:6], refs[6:]
    grad_out, gain_out, bias_out, keep, send, whole, grads, ga1, gq, gk, gv, in_sems, sems = refs
    copies = copies_in(meta, pieces, whole, in_sems)
    start_all(copies)
    wait_all(copies)
    outs = []

    def emit(index, value):
        grads[index] = value.astype(bf16)
        outs.extend(copies_out(meta, grads.at[index], keep, send, index, sems.at[index]))
        start_all(outs[-4:])

    emit(0, mm_tn(normed2[...], gq2[...]))
    grad, gain_two = norm_back(h1[...], gains[1:2], mm_nt(gq2[...], whole[4]))
    g1 = g2[...] + grad
    grad_out[...] = g1
    go1 = g1.astype(bf16)
    emit(1, mm_tn(mixed[...], go1))
    ga1[...] = mm_nt(go1, whole[3]).astype(bf16)
    gq[...] = jnp.zeros(gq.shape, bf16)
    gk[...] = jnp.zeros(gk.shape, bf16)
    gv[...] = jnp.zeros(gv.shape, bf16)
    bias_out[...] = jnp.zeros(bias_out.shape, f32)
    length = bias.shape[1]

    def slot(b, carry):
        rows = pl.ds(pl.multiple_of(b * length, length), length)
        masks = head_masks()
        key_at = lax.broadcasted_iota(jnp.int32, (length, QUAD * length), 0)
        query_at = lax.broadcasted_iota(jnp.int32, (length, QUAD * length), 1) % length
        ok = (key_at <= query_at) & (key_at < meta[4 + b])
        for quad in range(QUADS):
            at = quad_at(quad)
            q_stack = stack_heads(q[rows, at], masks)
            g_stack = stack_heads(ga1[rows, at], masks)
            tiled = jnp.concatenate([mixed[rows, at].astype(f32)] * QUAD, axis=0)
            delta = head_sums(g_stack.astype(f32) * tiled)
            block = k[rows, at]
            scores = jnp.where(ok, mm_nt(block, q_stack) + bias[quad], MASKED)
            share = jnp.exp(scores - lse[b, quad : quad + 1, :])
            grad_share = mm_nt(v[rows, at], g_stack)
            grad_scores = (share * (grad_share - delta)).astype(bf16)
            gv[rows, at] = mm(share.astype(bf16), g_stack).astype(bf16)
            gk[rows, at] = mm(grad_scores, q_stack).astype(bf16)
            gq[rows, at] = own_heads(mm_tn(block, grad_scores)).astype(bf16)
            bias_out[quad] += grad_scores.astype(f32)
        return carry

    lax.fori_loop(0, meta[2], slot, 0)
    emit(2, mm_tn(normed[...], gq[...]))
    emit(3, mm_tn(normed[...], gk[...]))
    emit(4, mm_tn(normed[...], gv[...]))
    grad_normed = mm_nt(gq[...], whole[0]) + mm_nt(gk[...], whole[1]) + mm_nt(gv[...], whole[2])
    grad, gain_one = norm_back(tokens[...].astype(f32), gains[0:1], grad_normed)
    grad_out[...] += grad
    gain_out[0:1] = gain_one
    gain_out[1:2] = gain_two
    wait_all(outs)


def memory_weight_kernel(meta, memory, gk, gv, keep, send, total, low, sems):
    slot = pl.program_id(0)
    count = meta[12 + slot]

    @pl.when(slot == 0)
    def _():
        total[...] = jnp.zeros(total.shape, f32)

    for n in range(1, memory.shape[1] // CHUNK + 1):

        @pl.when(count == n)
        def _(n=n):
            block = memory[0, : n * CHUNK, :]
            total[0] += mm_tn(block, gk[0, : n * CHUNK, :])
            total[1] += mm_tn(block, gv[0, : n * CHUNK, :])

    @pl.when(slot == pl.num_programs(0) - 1)
    def _():
        low[...] = total[...].astype(bf16)
        outs = copies_out(meta, low.at[0], keep, send, 0, sems.at[0]) + copies_out(
            meta, low.at[1], keep, send, 1, sems.at[1]
        )
        start_all(outs)
        wait_all(outs)


def memory_grad_kernel(meta, gk, gv, *refs):
    pieces, (out, whole, sems) = refs[:6], refs[6:]
    slot = pl.program_id(0)

    @pl.when(slot == 0)
    def _():
        copies = copies_in(meta, pieces, whole, sems)
        start_all(copies)
        wait_all(copies)

    for c in range(out.shape[1] // CHUNK):
        rows = pl.ds(c * CHUNK, CHUNK)

        @pl.when(c < meta[12 + slot])
        def _(rows=rows):
            out[0, rows, :] = mm_nt(gk[0, rows, :], whole[0]) + mm_nt(gv[0, rows, :], whole[1])

        @pl.when(c >= meta[12 + slot])
        def _(rows=rows):
            out[0, rows, :] = jnp.zeros((CHUNK, out.shape[2]), f32)


VMEM = pl.BlockSpec(memory_space=pltpu.VMEM)
ANY = pl.BlockSpec(memory_space=pl.ANY)


def params():
    return pltpu.CompilerParams(vmem_limit_bytes=56 * 1024 * 1024)


def cost(flops, moved, raised=0):
    return pl.CostEstimate(flops=int(flops), bytes_accessed=int(moved), transcendentals=int(raised))


def shape(dims, dtype):
    return jax.ShapeDtypeStruct(tuple(dims), dtype)


def live_slot(b, meta):
    return jnp.where(meta[12 + b] > 0, b, jnp.maximum(meta[2] - 1, 0))


def by_slot(rows, model, held=False):
    if held:
        return pl.BlockSpec((1, rows, model), lambda b, meta: (live_slot(b, meta), 0, 0))
    return pl.BlockSpec((1, rows, model), lambda b, meta: (b, 0, 0))


def call(kernel, out_shape, in_specs, out_specs, scratch, estimate, grid=()):
    return pl.pallas_call(
        kernel,
        out_shape=out_shape,
        grid_spec=pltpu.PrefetchScalarGridSpec(
            num_scalar_prefetch=1, grid=grid, in_specs=in_specs, out_specs=out_specs, scratch_shapes=scratch
        ),
        compiler_params=params(),
        cost_estimate=estimate,
    )


def on_device(
    tokens,
    memory,
    tgt_len,
    enc_len,
    ex_count,
    self_gain,
    self_q,
    self_k,
    self_v,
    self_out,
    rel_bias,
    cross_gain,
    cross_q,
    cross_k,
    cross_v,
    cross_out,
    ff_gain,
    ff_in,
    ff_out,
    cotangent,
):
    slots, length, model = tokens.shape
    enc = memory.shape[1]
    hidden = ff_in.shape[1]
    rows = self_q.shape[0]
    total = slots * length
    shard = lax.axis_index("fsdp")
    side = lax.axis_index("dp") % 2
    live = jnp.arange(slots, dtype=jnp.int32) < ex_count[0]
    chunks = jnp.where(live, (enc_len + CHUNK - 1) // CHUNK, 0)
    zero = jnp.zeros((), jnp.int32)
    meta = jnp.concatenate([jnp.stack([shard, side, ex_count[0], zero]), tgt_len, enc_len, chunks])

    cross_pieces = gather_pieces(jnp.stack([cross_k, cross_v]), side)
    square_pieces = gather_pieces(jnp.stack([self_q, self_k, self_v, self_out, cross_q, cross_out]), side)
    wide_pieces = gather_pieces(ff_in[None], side)
    narrow_pieces = gather_pieces(ff_out[None], side)
    packed = jnp.concatenate([self_gain, cross_gain, ff_gain, rel_bias.reshape(-1)])
    packed = jnp.pad(packed, (0, model - packed.shape[0]))[None]
    near = jnp.stack([packed] + [flip(packed, "fsdp", j) for j in (1, 2, 3)])
    small = jnp.concatenate([pick(near, shard ^ j) for j in range(4)], axis=0)
    gains = small[:, : 3 * rows].reshape(4, 3, rows).transpose(1, 0, 2).reshape(3, model).astype(f32)
    gains = jnp.pad(gains, ((0, 5), (0, 0)))
    table = small[:, 3 * rows : 3 * rows + rel_bias.size].reshape(-1, H)
    onehot = (bucket_ids(length)[:, :, None] == jnp.arange(table.shape[0], dtype=jnp.int32)).astype(f32)
    bias = jnp.einsum("ijn,nh->hij", onehot, table.astype(f32), precision=highest)
    bias = bias.reshape(QUADS, QUAD, length, length).transpose(0, 3, 1, 2).reshape(QUADS, length, QUAD * length)

    stacked = QUAD * length
    slot_rows = by_slot(length, model)
    enc_rows = by_slot(enc, model, held=True)
    unit = 2 * total * model * model
    enc_unit = 2 * slots * enc * model * model
    attend_unit = 2 * slots * enc * length * model * QUAD

    keys, values = call(
        memory_kernel,
        (shape(memory.shape, bf16), shape(memory.shape, bf16)),
        [enc_rows] + [ANY] * 6,
        (enc_rows, enc_rows),
        [pltpu.VMEM((2, model, model), bf16), pltpu.SemaphoreType.DMA((6,))],
        cost(2 * enc_unit, 6 * memory.size),
        grid=(slots,),
    )(meta, memory, *cross_pieces)

    flat = tokens.reshape(total, model)
    low = shape((total, model), bf16)
    normed1, q1, k1, v1, a1, h1, normed2, q2, lse1 = call(
        self_kernel,
        (low, low, low, low, low, shape((total, model), f32), low, low, shape((slots, 8, stacked), f32)),
        [VMEM] * 3 + [ANY] * 6,
        (VMEM,) * 9,
        [pltpu.VMEM((6, model, model), bf16), pltpu.SemaphoreType.DMA((6,))],
        cost(5 * unit + attend_unit / 4, 16 * total * model, slots * H * length * length),
    )(meta, flat, gains, bias, *square_pieces)

    by_slots = (slots, length, model)
    lse_spec = by_slot(8, stacked)
    a2, lse2 = call(
        cross_kernel,
        (shape(by_slots, bf16), shape((slots, 8, stacked), f32)),
        [slot_rows, enc_rows, enc_rows],
        (slot_rows, lse_spec),
        [pltpu.VMEM((QUADS, stacked, WIDE), bf16), pltpu.VMEM((QUADS, enc, stacked), f32)],
        cost(2 * attend_unit, 4 * memory.size, slots * H * length * enc),
        grid=(slots,),
    )(meta, q2.reshape(by_slots), keys, values)

    far_rows = hidden // 4
    output, g2, ga2, gain_three, keep_n, send_n, keep_w, send_w, keep_o, send_o = call(
        ff_kernel,
        (
            low,
            shape((total, model), f32),
            low,
            shape((8, model), f32),
            shape((2, far_rows, model), bf16),
            shape((2, far_rows, model), bf16),
            shape((2, rows, hidden), bf16),
            shape((2, rows, hidden), bf16),
            shape((2, rows, model), bf16),
            shape((2, rows, model), bf16),
        ),
        [VMEM] * 4 + [ANY] * 18,
        (VMEM,) * 4 + (ANY,) * 6,
        [
            pltpu.VMEM((1, model, model), bf16),
            pltpu.VMEM((1, model, hidden), bf16),
            pltpu.VMEM((1, hidden, model), bf16),
            pltpu.VMEM((total, model), bf16),
            pltpu.VMEM((total, model), bf16),
            pltpu.VMEM((4, far_rows, model), bf16),
            pltpu.VMEM((4, model, far_rows), bf16),
            pltpu.VMEM((model, model), bf16),
            pltpu.VMEM((total, model), f32),
            pltpu.VMEM((total, model), f32),
            pltpu.VMEM((total, model), f32),
            pltpu.SemaphoreType.DMA((3, 6)),
            pltpu.SemaphoreType.DMA((4,)),
            pltpu.SemaphoreType.DMA((16,)),
            pltpu.SemaphoreType.DMA((4,)),
        ],
        cost(27 * unit, 40e6, total * hidden),
    )(meta, h1, a2.reshape(total, model), cotangent, gains, *square_pieces, *wide_pieces, *narrow_pieces)
    sum_narrow = reduce_rows(keep_n, send_n)
    sum_wide = reduce_rows(keep_w, send_w)

    gq2, gk2, gv2 = call(
        cross_back_kernel,
        (shape(by_slots, bf16), shape(memory.shape, bf16), shape(memory.shape, bf16)),
        [slot_rows, slot_rows, slot_rows, lse_spec, enc_rows, enc_rows],
        (slot_rows, enc_rows, enc_rows),
        [
            pltpu.VMEM((QUADS, stacked, WIDE), bf16),
            pltpu.VMEM((QUADS, stacked, WIDE), bf16),
            pltpu.VMEM((8, stacked), f32),
            pltpu.VMEM((QUADS, WIDE, stacked), f32),
        ],
        cost(5 * attend_unit, 8 * memory.size, slots * H * length * enc),
        grid=(slots,),
    )(meta, q2.reshape(by_slots), ga2.reshape(by_slots), a2, lse2, keys, values)

    tokens_grad, gain_low, bias_grad, keep_s, send_s = call(
        self_back_kernel,
        (
            shape((total, model), f32),
            shape((8, model), f32),
            shape((QUADS, length, stacked), f32),
            shape((2, 5 * rows, model), bf16),
            shape((2, 5 * rows, model), bf16),
        ),
        [VMEM] * 13 + [ANY] * 6,
        (VMEM,) * 3 + (ANY,) * 2,
        [
            pltpu.VMEM((6, model, model), bf16),
            pltpu.VMEM((5, model, model), bf16),
            pltpu.VMEM((total, model), bf16),
            pltpu.VMEM((total, model), bf16),
            pltpu.VMEM((total, model), bf16),
            pltpu.VMEM((total, model), bf16),
            pltpu.SemaphoreType.DMA((6,)),
            pltpu.SemaphoreType.DMA((5, 4)),
        ],
        cost(10 * unit + attend_unit, 40 * total * model, slots * H * length * length),
    )(
        meta, gq2.reshape(total, model), normed2, h1, g2, a1, q1, k1, v1, lse1, normed1, flat, gains, bias,
        *square_pieces,
    )

    keep_m, send_m = call(
        memory_weight_kernel,
        (shape((2, 2 * rows, model), bf16), shape((2, 2 * rows, model), bf16)),
        [enc_rows, enc_rows, enc_rows],
        (ANY, ANY),
        [
            pltpu.VMEM((2, model, model), f32),
            pltpu.VMEM((2, model, model), bf16),
            pltpu.SemaphoreType.DMA((2, 4)),
        ],
        cost(2 * enc_unit, 6 * memory.size),
        grid=(slots,),
    )(meta, memory, gk2, gv2)

    memory_grad = call(
        memory_grad_kernel,
        shape(memory.shape, f32),
        [enc_rows, enc_rows] + [ANY] * 6,
        by_slot(enc, model),
        [pltpu.VMEM((2, model, model), bf16), pltpu.SemaphoreType.DMA((6,))],
        cost(2 * enc_unit, 8 * memory.size),
        grid=(slots,),
    )(meta, gk2, gv2, *cross_pieces)

    keep_c = jnp.concatenate([keep_o, keep_m, keep_s], axis=1)
    send_c = jnp.concatenate([send_o, send_m, send_s], axis=1)
    sums = reduce_rows(keep_c, send_c)
    sum_co, sum_ck, sum_cv, sum_cq, sum_so, sum_sq, sum_sk, sum_sv = (
        sums[i * rows : (i + 1) * rows] for i in range(8)
    )
    by_head = bias_grad.reshape(QUADS, length, QUAD, length).transpose(0, 2, 3, 1).reshape(H, length, length)
    rel = jnp.einsum("ijn,hij->nh", onehot, by_head, precision=highest)
    tiny = jnp.concatenate(
        [g.reshape(4, -1) for g in (gain_low[0], gain_low[1], gain_three[0], rel)], axis=1
    )
    tiny = pick(sum_small(tiny), shard)
    return (
        output.reshape(tokens.shape),
        tokens_grad.reshape(tokens.shape),
        memory_grad,
        tiny[:rows],
        sum_sq,
        sum_sk,
        sum_sv,
        sum_so,
        tiny[3 * rows :].reshape(rel_bias.shape),
        tiny[rows : 2 * rows],
        sum_cq,
        sum_ck,
        sum_cv,
        sum_co,
        tiny[2 * rows : 3 * rows],
        sum_wide,
        sum_narrow,
    )


def solution(mesh):
    in_specs = (
        P(("dp", "fsdp"), None, None),
        P(("dp", "fsdp"), None, None),
        P(("dp", "fsdp")),
        P(("dp", "fsdp")),
        P(("dp", "fsdp")),
        P("fsdp"),
        P("fsdp", None),
        P("fsdp", None),
        P("fsdp", None),
        P("fsdp", None),
        P("fsdp", None),
        P("fsdp"),
        P("fsdp", None),
        P("fsdp", None),
        P("fsdp", None),
        P("fsdp", None),
        P("fsdp"),
        P("fsdp", None),
        P("fsdp", None),
        P(("dp", "fsdp"), None, None),
    )
    out_specs = (
        P(("dp", "fsdp"), None, None),
        P(("dp", "fsdp"), None, None),
        P(("dp", "fsdp"), None, None),
        P("fsdp"),
        P("fsdp", None),
        P("fsdp", None),
        P("fsdp", None),
        P("fsdp", None),
        P("fsdp", None),
        P("fsdp"),
        P("fsdp", None),
        P("fsdp", None),
        P("fsdp", None),
        P("fsdp", None),
        P("fsdp"),
        P("fsdp", None),
        P("fsdp", None),
    )
    return jax.shard_map(
        on_device, mesh=mesh, in_specs=in_specs, out_specs=out_specs, check_vma=False
    )
```

```python
import functools
import math

import jax
import jax.numpy as jnp
from jax import lax
from jax.experimental import pallas as pl
from jax.experimental.pallas import tpu as pltpu
from jax.sharding import PartitionSpec as P

H = 12
DH = 64
QUAD = 4
QUADS = H // QUAD
WIDE = QUAD * DH
CHUNK = 256
MASKED = -1000000000.0
WAY_X, WAY_Z, PLACE = 1, 3, 16
BUCKETS = 32
TINY = 64

bucket_edges = [math.ceil(16 * 8 ** (exponent / 16)) for exponent in range(1, 16)]
highest = lax.Precision.HIGHEST
f32 = jnp.float32
bf16 = jnp.bfloat16


def bucket_ids(length):
    positions = jnp.arange(length, dtype=jnp.int32)
    distance = jnp.maximum(positions[:, None] - positions[None, :], 0)
    buckets = jnp.minimum(distance, 16)
    for bucket_edge in bucket_edges:
        buckets = buckets + (distance >= bucket_edge).astype(jnp.int32)
    return buckets


def flip(values, axis, bit):
    size = lax.axis_size(axis)
    return lax.ppermute(values, axis, [(i, i ^ bit) for i in range(size)])


def pick(values, index):
    return lax.dynamic_index_in_dim(values, index, 0, keepdims=False)


def add_low(left, right):
    return (left.astype(f32) + right.astype(f32)).astype(bf16)


def mm(left, right):
    return jnp.dot(left, right, preferred_element_type=f32)


def mm_nt(left, right):
    return lax.dot_general(left, right, (((1,), (1,)), ((), ())), preferred_element_type=f32)


def mm_tn(left, right):
    return lax.dot_general(left, right, (((0,), (0,)), ((), ())), preferred_element_type=f32)


def piece_starts(meta, pieces, way):
    shard, side = meta[0], meta[way]
    rows = pieces[0].shape[1]
    half = rows // 2
    return (
        shard * rows,
        (shard ^ 1) * rows,
        (shard ^ 2) * rows + side * half,
        (shard ^ 2) * rows + (1 - side) * half,
        (shard ^ 3) * rows + side * half,
        (shard ^ 3) * rows + (1 - side) * half,
    )


def copies_in(meta, pieces, whole, sems, way, only=slice(None), cols=slice(None)):
    return [
        pltpu.make_async_copy(
            piece.at[only, :, cols],
            whole.at[:, pl.ds(pl.multiple_of(start, 32), piece.shape[1])],
            sems.at[i],
        )
        for i, (piece, start) in enumerate(zip(pieces, piece_starts(meta, pieces, way)))
    ]


def start_all(copies):
    for copy in copies:
        copy.start()


def wait_all(copies):
    for copy in copies:
        copy.wait()


def copies_out(meta, whole, keep, send, at, sems):
    shard = meta[0]
    rows = whole.shape[0] // 4
    return [
        pltpu.make_async_copy(
            whole.at[pl.ds(pl.multiple_of((shard ^ j) * rows, 32), rows)],
            (send if j % 2 else keep).at[j // 2, pl.ds(at * rows, rows)],
            sems.at[j],
        )
        for j in range(4)
    ]


def norm_rho(hidden):
    return lax.rsqrt(jnp.mean(hidden * hidden, axis=-1, keepdims=True) + 1e-06)


def norm_back(hidden, gain, upstream):
    rho = norm_rho(hidden)
    scaled = upstream * gain
    inner = jnp.mean(scaled * hidden, axis=-1, keepdims=True)
    grad = rho * scaled - hidden * (rho * rho * rho * inner)
    return grad, jnp.sum(upstream * hidden * rho, axis=0, keepdims=True)


def head_masks():
    lane = lax.broadcasted_iota(jnp.int32, (1, WIDE), 1) // DH
    return [(lane == h).astype(f32).astype(bf16) for h in range(QUAD)]


def stack_heads(values, masks):
    return jnp.concatenate([values * mask for mask in masks], axis=0)


def own_heads(mixed):
    rows = mixed.shape[1] // QUAD
    own = [mixed[h * DH : (h + 1) * DH, h * rows : (h + 1) * rows] for h in range(QUAD)]
    return jnp.concatenate(own, axis=0).T


def head_sums(product):
    high = product.astype(bf16)
    low = (product - high.astype(f32)).astype(bf16)
    ones = jnp.ones((8, WIDE), bf16)
    return (mm_nt(ones, high) + mm_nt(ones, low))[0:1]


def fold(values, op):
    return op(values.reshape(values.shape[0] // 8, 8, values.shape[1]), axis=0)


def quad_at(quad):
    return pl.ds(quad * WIDE, WIDE)


def copies_beside(meta, pieces, whole, sems, way):
    columns = pieces[0].shape[2]
    starts = piece_starts(meta, pieces, way)
    return [
        pltpu.make_async_copy(
            piece.at[j],
            whole.at[pl.ds(pl.multiple_of(start, 32), piece.shape[1]), pl.ds(j * columns, columns)],
            sems.at[j, i],
        )
        for j in range(2)
        for i, (piece, start) in enumerate(zip(pieces, starts))
    ]


def each_count(meta, slot, most, body):
    for n in range(1, most // CHUNK + 1):
        pl.when(meta[12 + slot] == n)(functools.partial(body, n * CHUNK))


def memory_kernel(meta, memory, *refs):
    pieces, (out, whole, sems) = refs[:6], refs[6:]
    slot = pl.program_id(0)

    @pl.when(slot == 0)
    def _():
        copies = copies_beside(meta, pieces, whole, sems, WAY_X)
        start_all(copies)
        wait_all(copies)

    def project(rows):
        out[0, :rows, :] = mm(memory[0, :rows, :], whole[...]).astype(bf16)

    each_count(meta, slot, memory.shape[1], project)


def self_kernel(meta, tokens, gains, bias, *refs):
    pieces = refs[:6]
    normed_out, q_out, k_out, v_out, mixed_out, lse_out, whole, sems = refs[6:]
    copies = copies_in(meta, pieces, whole, sems, WAY_Z)
    start_all(copies)
    hidden = tokens[...].astype(f32)
    normed = (hidden * norm_rho(hidden) * gains[0:1]).astype(bf16)
    normed_out[...] = normed
    wait_all(copies)
    q_out[...] = mm(normed, whole[0]).astype(bf16)
    k_out[...] = mm(normed, whole[1]).astype(bf16)
    v_out[...] = mm(normed, whole[2]).astype(bf16)
    length = bias.shape[1]
    masks = head_masks()
    key_at = lax.broadcasted_iota(jnp.int32, (length, QUAD * length), 0)
    query_at = lax.broadcasted_iota(jnp.int32, (length, QUAD * length), 1) % length
    for b in range(lse_out.shape[0]):
        rows = slice(b * length, (b + 1) * length)
        ok = (key_at <= query_at) & (key_at < meta[4 + b])
        for quad in range(QUADS):
            at = slice(quad * WIDE, (quad + 1) * WIDE)
            scores = mm_nt(k_out[rows, at], stack_heads(q_out[rows, at], masks)) + bias[quad]
            scores = jnp.where(ok, scores, MASKED)
            top = jnp.max(scores, axis=0, keepdims=True)
            raised = jnp.exp(scores - top)
            total = jnp.sum(raised, axis=0, keepdims=True)
            weights = (raised * (1.0 / total)).astype(bf16)
            mixed_out[rows, at] = own_heads(mm(v_out[rows, at].T, weights)).astype(bf16)
            lse_out[b, quad : quad + 1, :] = top + jnp.log(total)


def query_kernel(meta, tokens, mixed, gains, *refs):
    pieces, (h1_out, normed2_out, q2_out, whole, sems) = refs[:6], refs[6:]
    copies = copies_in(meta, pieces, whole, sems, WAY_X, pl.ds(0, 2))
    start_all(copies)
    wait_all(copies)
    first = tokens[...].astype(f32) + mm(mixed[...], whole[0])
    h1_out[...] = first
    normed2 = (first * norm_rho(first) * gains[1:2]).astype(bf16)
    normed2_out[...] = normed2
    q2_out[...] = mm(normed2, whole[1]).astype(bf16)


def cross_kernel(meta, queries, memory, mixed_out, lse_out):
    slot = pl.program_id(0)
    model = queries.shape[2]

    @pl.when(meta[12 + slot] == 0)
    def _():
        mixed_out[...] = jnp.zeros(mixed_out.shape, bf16)
        lse_out[...] = jnp.zeros(lse_out.shape, f32)

    def attend(rows):
        masks = head_masks()
        ok = lax.broadcasted_iota(jnp.int32, (rows, 1), 0) < meta[8 + slot]
        for quad in range(QUADS):
            at, at_v = slice(quad * WIDE, (quad + 1) * WIDE), slice(model + quad * WIDE, model + (quad + 1) * WIDE)
            stacked = stack_heads(queries[0, :, at], masks)
            scores = jnp.where(ok, mm_nt(memory[0, :rows, at], stacked), MASKED)
            top = jnp.max(scores, axis=0, keepdims=True)
            raised = jnp.exp(scores - top)
            total = jnp.sum(raised, axis=0, keepdims=True)
            mixed = mm(memory[0, :rows, at_v].T, raised.astype(bf16))
            mixed_out[0, :, at] = own_heads(mixed * (1.0 / total)).astype(bf16)
            lse_out[0, quad : quad + 1, :] = top + jnp.log(total)

    each_count(meta, slot, memory.shape[1], attend)


def gelu_both(values):
    scale = math.sqrt(2.0 / math.pi)
    square = values * values
    slope = jnp.tanh(scale * values * (1.0 + 0.044715 * square))
    half = 0.5 * (1.0 + slope)
    back = half + 0.5 * values * (1.0 - slope * slope) * (scale * (1.0 + 3 * 0.044715 * square))
    return values * half, back


def live_rows(meta, slots, length):
    positions = lax.broadcasted_iota(jnp.int32, (length, 1), 0)
    return jnp.concatenate(
        [((positions < meta[4 + b]) & (b < meta[2])).astype(f32) for b in range(slots)], axis=0
    )


def ff_kernel(meta, h1, mixed, cotangent, gains, *refs):
    square, wide, narrow, refs = refs[:6], refs[6:12], refs[12:18], refs[18:]
    (output, g2_out, ga2_out, gain_out, keep_n, send_n, keep_w, send_w, keep_o, send_o), refs = refs[:10], refs[10:]
    co, w_in, w_out, gf, normed, grad_n, grad_w, grad_o, second, third, back, in_sems, n_sems, w_sems, o_sems = refs
    model = h1.shape[1]
    rows = model // 4
    shard = meta[0]
    co_in = copies_in(meta, square, co, in_sems.at[0], WAY_X, pl.ds(2, 1))
    in_in = copies_in(meta, wide, w_in, in_sems.at[1], WAY_Z)
    out_in = copies_in(meta, narrow, w_out, in_sems.at[2], WAY_X)
    start_all(co_in)
    start_all(in_in)
    start_all(out_in)
    live = live_rows(meta, cotangent.shape[0], cotangent.shape[1])
    gf[...] = (cotangent[...].reshape(h1.shape).astype(f32) * live).astype(bf16)
    wait_all(co_in)
    second[...] = h1[...] + mm(mixed[...], co[0])
    hidden = second[...]
    normed[...] = (hidden * norm_rho(hidden) * gains[2:3]).astype(bf16)
    normed_t = normed[...].T
    wait_all(in_in)
    wait_all(out_in)
    waits = []
    for j in range(4):
        cols = pl.ds(pl.multiple_of((shard ^ j) * model, model), model)
        units, slope = gelu_both(mm(normed[...], w_in[0, :, cols]))
        low = units.astype(bf16)
        wide_out = mm(low, w_out[0, cols, :])
        grad_n[j] = mm_tn(low, gf[...]).astype(bf16)
        waits.append(pltpu.make_async_copy(grad_n.at[j], (send_n if j % 2 else keep_n).at[j // 2], n_sems.at[j]))
        waits[-1].start()
        grad_units = (mm_nt(gf[...], w_out[0, cols, :]) * slope).astype(bf16)
        grad_w[j] = mm(normed_t, grad_units).astype(bf16)
        at = pl.ds(pl.multiple_of((shard ^ j) * rows, 32), rows)
        for i in range(4):
            waits.append(
                pltpu.make_async_copy(
                    grad_w.at[j, pl.ds(pl.multiple_of((shard ^ i) * rows, 32), rows)],
                    (send_w if i % 2 else keep_w).at[i // 2, at],
                    w_sems.at[4 * j + i],
                )
            )
            waits[-1].start()
        grad_normed = mm_nt(grad_units, w_in[0, :, cols])
        if j == 0:
            third[...] = second[...] + wide_out
            back[...] = grad_normed
        else:
            third[...] += wide_out
            back[...] += grad_normed
    output[...] = (third[...] * live).astype(bf16)
    grad, gain = norm_back(second[...], gains[2:3], back[...])
    gain_out[...] = jnp.broadcast_to(gain, gain_out.shape)
    g2 = gf[...].astype(f32) + grad
    g2_out[...] = g2
    go2 = g2.astype(bf16)
    ga2_out[...] = mm_nt(go2, co[0]).astype(bf16)
    grad_o[...] = mm_tn(mixed[...], go2).astype(bf16)
    out = copies_out(meta, grad_o, keep_o, send_o, 0, o_sems)
    start_all(out)
    wait_all(waits)
    wait_all(out)


def cross_back_kernel(meta, queries, grads, mixed, lse, memory, gq_out, out):
    slot = pl.program_id(0)
    model = queries.shape[2]

    @pl.when(meta[12 + slot] == 0)
    def _():
        gq_out[...] = jnp.zeros(gq_out.shape, bf16)

    def attend(rows):
        masks = head_masks()
        ok = lax.broadcasted_iota(jnp.int32, (rows, 1), 0) < meta[8 + slot]
        for quad in range(QUADS):
            at, at_v = slice(quad * WIDE, (quad + 1) * WIDE), slice(model + quad * WIDE, model + (quad + 1) * WIDE)
            q_stack = stack_heads(queries[0, :, at], masks)
            g_stack = stack_heads(grads[0, :, at], masks)
            tiled = jnp.concatenate([mixed[0, :, at].astype(f32)] * QUAD, axis=0)
            delta = head_sums(g_stack.astype(f32) * tiled)
            block = memory[0, :rows, at]
            scores = jnp.where(ok, mm_nt(block, q_stack), MASKED)
            share = jnp.exp(scores - lse[0, quad : quad + 1, :])
            grad_share = mm_nt(memory[0, :rows, at_v], g_stack)
            grad_scores = (share * (grad_share - delta)).astype(bf16)
            out[0, :rows, at_v] = mm(share.astype(bf16), g_stack).astype(bf16)
            out[0, :rows, at] = mm(grad_scores, q_stack).astype(bf16)
            gq_out[0, :, at] = own_heads(mm(block.T, grad_scores)).astype(bf16)

    each_count(meta, slot, memory.shape[1], attend)


def table_grad(scores):
    length = scores.shape[1]
    key_at = lax.broadcasted_iota(jnp.int32, (length, length), 0)
    distance = jnp.maximum(lax.broadcasted_iota(jnp.int32, (length, length), 1) - key_at, 0)
    bucket = jnp.minimum(distance, 16)
    for edge in bucket_edges:
        bucket = bucket + (distance >= edge).astype(jnp.int32)
    bucket = jnp.concatenate([bucket] * QUAD, axis=1)
    head = lax.broadcasted_iota(jnp.int32, (QUAD * length, 128), 0) // length
    column = lax.broadcasted_iota(jnp.int32, (QUAD * length, 128), 1)
    table = jnp.zeros((BUCKETS, 128), f32)
    for quad in range(QUADS):
        values = scores[quad]
        sums = [jnp.sum(jnp.where(bucket == n, values, 0.0), axis=0, keepdims=True) for n in range(BUCKETS)]
        sums = jnp.concatenate(sums, axis=0)
        high = sums.astype(bf16)
        low = (sums - high.astype(f32)).astype(bf16)
        to_head = (column == head + quad * QUAD).astype(f32).astype(bf16)
        table = table + mm(high, to_head) + mm(low, to_head)
    return table


def self_back_kernel(
    meta, gq2, normed2, h1, g2, mixed, q, k, v, lse, normed, tokens, gains, bias, gain_three, keep_in, send_in, *refs
):
    query, pieces, refs = refs[:6], refs[6:12], refs[12:]
    (grad_out, tiny, keep, send, keep_s, send_s), refs = refs[:6], refs[6:]
    bias_out, square, whole, grads, ga1, gq, gk, gv, in_sems, sems = refs
    copies_q = copies_in(meta, query, square, in_sems.at[0], WAY_X, pl.ds(0, 2))
    copies = copies_in(meta, pieces, whole, in_sems.at[1], WAY_Z)
    start_all(copies_q)
    start_all(copies)
    outs = []

    def emit(index, value, *place):
        grads[index] = value.astype(bf16)
        outs.extend(copies_out(meta, grads.at[index], *place, sems.at[index]))
        start_all(outs[-4:])

    emit(0, mm_tn(normed2[...], gq2[...]), keep, send, 1)
    wait_all(copies_q)
    grad, gain_two = norm_back(h1[...], gains[1:2], mm_nt(gq2[...], square[1]))
    g1 = g2[...] + grad
    grad_out[...] = g1
    go1 = g1.astype(bf16)
    emit(1, mm_tn(mixed[...], go1), keep, send, 2)
    ga1[...] = mm_nt(go1, square[0]).astype(bf16)
    length = bias.shape[1]
    masks = head_masks()
    key_at = lax.broadcasted_iota(jnp.int32, (length, QUAD * length), 0)
    query_at = lax.broadcasted_iota(jnp.int32, (length, QUAD * length), 1) % length
    for b in range(lse.shape[0]):
        rows = slice(b * length, (b + 1) * length)
        ok = (key_at <= query_at) & (key_at < meta[4 + b])
        for quad in range(QUADS):
            at = slice(quad * WIDE, (quad + 1) * WIDE)
            q_stack = stack_heads(q[rows, at], masks)
            g_stack = stack_heads(ga1[rows, at], masks)
            tiled = jnp.concatenate([mixed[rows, at].astype(f32)] * QUAD, axis=0)
            delta = head_sums(g_stack.astype(f32) * tiled)
            block = k[rows, at]
            scores = jnp.where(ok, mm_nt(block, q_stack) + bias[quad], MASKED)
            share = jnp.exp(scores - lse[b, quad : quad + 1, :])
            grad_share = mm_nt(v[rows, at], g_stack)
            grad_scores = (share * (grad_share - delta)).astype(bf16)
            gv[rows, at] = mm(share.astype(bf16), g_stack).astype(bf16)
            gk[rows, at] = mm(grad_scores, q_stack).astype(bf16)
            gq[rows, at] = own_heads(mm(block.T, grad_scores)).astype(bf16)
            if b == 0:
                bias_out[quad] = grad_scores.astype(f32)
            else:
                bias_out[quad] += grad_scores.astype(f32)
    normed_t = normed[...].T
    emit(2, mm(normed_t, gq[...]), keep, send, 3)
    emit(3, mm(normed_t, gk[...]), keep_s, send_s, 0)
    emit(4, mm(normed_t, gv[...]), keep_s, send_s, 1)
    wait_all(copies)
    grad_normed = mm_nt(gq[...], whole[0]) + mm_nt(gk[...], whole[1]) + mm_nt(gv[...], whole[2])
    grad, gain_one = norm_back(tokens[...].astype(f32), gains[0:1], grad_normed)
    grad_out[...] += grad
    top = jnp.concatenate([gain_one, gain_two, gain_three[0:1], jnp.zeros((5, gain_one.shape[1]), f32)], axis=0)
    table = jnp.pad(table_grad(bias_out), ((0, 0), (0, gain_one.shape[1] - 128)))
    rest = jnp.zeros((tiny.shape[0] - 8 - table.shape[0], gain_one.shape[1]), f32)
    tiny[...] = jnp.concatenate([top, table, rest], axis=0).astype(bf16)
    wait_all(outs)


def memory_weight_kernel(meta, memory, grads, tiny, keep, send, total, low, sems):
    slot = pl.program_id(0)
    model = memory.shape[2]

    @pl.when(slot == 0)
    def _():
        total[...] = jnp.zeros(total.shape, f32)

    def add(rows):
        total[...] += mm(memory[0, :rows, :].T, grads[0, :rows, :])

    each_count(meta, slot, memory.shape[1], add)

    @pl.when(slot == pl.num_programs(0) - 1)
    def _():
        rows = model // 4
        outs = [
            pltpu.make_async_copy(
                tiny,
                (send if j % 2 else keep).at[j // 2, pl.ds(2 * rows, tiny.shape[0])],
                sems.at[2, j],
            )
            for j in range(4)
        ]
        start_all(outs)
        for i in range(2):
            low[i] = total[:, i * model : (i + 1) * model].astype(bf16)
            outs += copies_out(meta, low.at[i], keep, send, i, sems.at[i])
            start_all(outs[-4:])
        wait_all(outs)


def memory_grad_kernel(meta, grads, *refs):
    pieces, (out, whole, sems) = refs[:6], refs[6:]
    slot = pl.program_id(0)

    @pl.when(slot == 0)
    def _():
        copies = copies_beside(meta, pieces, whole, sems, WAY_X)
        start_all(copies)
        wait_all(copies)

    def fill(rows):
        if rows:
            out[0, :rows, :] = mm_nt(grads[0, :rows, :], whole[...])
        if rows < out.shape[1]:
            out[0, rows:, :] = jnp.zeros((out.shape[1] - rows, out.shape[2]), f32)

    pl.when(meta[12 + slot] == 0)(functools.partial(fill, 0))
    each_count(meta, slot, out.shape[1], fill)


VMEM = pl.BlockSpec(memory_space=pltpu.VMEM)
ANY = pl.BlockSpec(memory_space=pl.ANY)


def cost(flops, moved, raised=0):
    del flops, moved, raised
    return pl.CostEstimate(flops=1024, bytes_accessed=1024, transcendentals=0)


def shape(dims, dtype):
    return jax.ShapeDtypeStruct(tuple(dims), dtype)


def live_slot(b, meta):
    return jnp.where(meta[12 + b] > 0, b, jnp.maximum(meta[2] - 1, 0))


def by_slot(rows, model, held=False):
    if held:
        return pl.BlockSpec((1, rows, model), lambda b, meta: (live_slot(b, meta), 0, 0))
    return pl.BlockSpec((1, rows, model), lambda b, meta: (b, 0, 0))


class Steps:
    def __init__(self, meta):
        self.meta = meta
        self.token = meta
        self.marks = []
        self.last = None
        self.pending = []
        self.fresh = False

    def call(self, kernel, outs, in_specs, out_specs, scratch, estimate, operands, grid=(), aliases=None, after=None):
        count = len(outs)
        order = [self.token]
        if self.marks:
            order.extend(self.marks)
        first = 1 + len(order)

        def body(meta, *refs):
            refs = refs[len(order) :]
            ins, rest = refs[: len(operands)], refs[len(operands) :]
            kernel(meta, *ins, *rest[:count], *rest[count + 1 :])

        result = pl.pallas_call(
            body,
            out_shape=tuple(outs) + (shape((16, 128), f32),),
            grid_spec=pltpu.PrefetchScalarGridSpec(
                num_scalar_prefetch=1,
                grid=grid,
                in_specs=[ANY] * len(order) + list(in_specs),
                out_specs=tuple(out_specs) + (ANY,),
                scratch_shapes=scratch,
            ),
            input_output_aliases={first + i: o for i, o in (aliases or {}).items()},
            compiler_params=pltpu.CompilerParams(vmem_limit_bytes=56 * 1024 * 1024),
            cost_estimate=estimate,
        )(self.meta, *order, *operands)
        self.token, self.marks = result[-1], []
        return result[:-1]

    def mark(self, result):
        self.marks.append(result)

    def gate(self, *values):
        outs = self.call(
            lambda *refs: None,
            [shape(v.shape, v.dtype) for v in values],
            [ANY] * len(values),
            [ANY] * len(values),
            [],
            cost(0, 0),
            values,
            aliases={i: i for i in range(len(values))},
        )
        return outs


class Bundle:
    def __init__(self, own, place, bit):
        rows = own.shape[1] // 2
        self.own, self.bit = own, bit
        self.half = lax.dynamic_slice_in_dim(own, (place // bit) % 2 * rows, rows, 1)

    def send(self):
        self.direct = flip(self.half, "fsdp", 2)
        self.beside = flip(self.own, "fsdp", 1)

    def hand_on(self):
        self.passed = flip(self.direct, "dp", self.bit)
        self.direct_beside = flip(self.direct, "fsdp", 1)

    def end(self):
        self.passed_beside = flip(self.passed, "fsdp", 1)

    def pieces(self):
        return (self.own, self.beside, self.direct, self.passed, self.direct_beside, self.passed_beside)


class Piece:
    def __init__(self, steps, place, outs, blocks, tall=True):
        self.steps, self.outs, self.blocks = steps, outs, blocks
        self.place, self.tall = place, tall and lax.axis_size("dp") > 2

    def ready(self, keep, send):
        self.keep, self.send = keep, send
        self.steps.pending.append(self)

    def add(self, left, right):
        return (left.astype(f32) + right.astype(f32)).astype(bf16)

    def cut(self, which, axis):
        half = self.keep.shape[axis] // 2
        return [lax.dynamic_slice_in_dim(v, which * half, half, axis) for v in (self.keep, self.got)]

    def core(self):
        far = self.add(self.keep[1], self.got[1])
        self.keep, self.got = self.add(self.keep[0], self.got[0]), flip(far, "fsdp", 2)
        self.steps.mark(far)

    def halve(self, bit, axis):
        side = self.place // bit % 2
        send = self.add(*self.cut(1 - side, axis))
        self.keep, self.got = self.add(*self.cut(side, axis)), flip(send, "dp", bit)
        self.steps.mark(send)

    def y(self):
        self.halve(1, 1)

    def x(self):
        if self.tall:
            self.halve(2, 0)
        else:
            self.pass_on(2)

    def pass_on(self, bit):
        self.keep = self.add(self.keep, self.got)
        self.got = flip(self.keep, "dp", bit)
        self.steps.mark(self.keep)

    def z(self):
        bit = 4
        while bit < lax.axis_size("dp"):
            self.pass_on(bit)
            bit *= 2

    def w(self):
        self.pass_on(2 if self.tall else 1)

    def joined(self, axis, bit, dtype, rows=slice(None)):
        mine, other = self.keep[rows].astype(dtype), self.got[rows].astype(dtype)
        low = self.place // bit % 2 == 0
        return jnp.concatenate([jnp.where(low, mine, other), jnp.where(low, other, mine)], axis=axis)

    def v(self):
        self.keep = self.joined(0, 2, bf16)
        self.got = flip(self.keep, "dp", 1)
        self.steps.mark(self.keep)

    def end(self):
        at = 0
        parts = {}
        for which, _ in self.blocks:
            rows = self.outs[which][0]
            parts.setdefault(which, []).append(self.joined(1, 1, f32, slice(at, at + rows)))
            at += rows
        self.result = [jnp.concatenate(parts[which], axis=1) for which in range(len(self.outs))]
        self.steps.mark(self.result[0])


ORDER = (
    "!",
    ("W1.core",),
    ("W2.core",),
    "KE",
    ("W1.y",),
    "KF",
    ("W2.y", "W1.x"),
    "!",
    ("S1.core", "S2.core"),
    "KW",
    ("S1.y", "W2.x", "W1.z"),
    "!",
    ("M.core",),
    "KG",
    ("S2.y", "M.y", "S1.x", "W2.z", "W1.w"),
    ("W1.v", "S2.x"),
    ("S1.z", "W2.w", "M.x"),
    ("S2.z", "W1.end"),
    ("S1.w", "W2.v", "M.z"),
    ("S2.w", "S1.v"),
    ("M.w", "S2.v", "W2.end"),
    ("S1.end", "S2.end", "M.end"),
)


def on_device(
    tokens,
    memory,
    tgt_len,
    enc_len,
    ex_count,
    self_gain,
    self_q,
    self_k,
    self_v,
    self_out,
    rel_bias,
    cross_gain,
    cross_q,
    cross_k,
    cross_v,
    cross_out,
    ff_gain,
    ff_in,
    ff_out,
    cotangent,
):
    slots, length, model = tokens.shape
    enc = memory.shape[1]
    hidden = ff_in.shape[1]
    rows = self_q.shape[0]
    total = slots * length
    shard = lax.axis_index("fsdp")
    place = lax.axis_index("dp")
    live = jnp.arange(slots, dtype=jnp.int32) < ex_count[0]
    chunks = jnp.where(live, (enc_len + CHUNK - 1) // CHUNK, 0)
    first = jnp.stack([shard, place % 2, ex_count[0], place // 2 % 2])
    meta = jnp.concatenate([first, tgt_len, enc_len, chunks, place[None]])
    steps = Steps(meta)

    kv = Bundle(jnp.stack([cross_k, cross_v]), place, 1)
    qkv = Bundle(jnp.stack([self_q, self_k, self_v]), place, 2)
    outs = Bundle(jnp.stack([self_out, cross_q, cross_out]), place, 1)
    wide = Bundle(ff_in[None], place, 2)
    narrow = Bundle(ff_out[None], place, 1)
    packed = jnp.concatenate([self_gain, cross_gain, ff_gain, rel_bias.reshape(-1)])
    packed = jnp.pad(packed, (0, model - packed.shape[0]))[None]
    kv.send()
    qkv.send()
    kv.direct, outs.half, packed = steps.gate(kv.direct, outs.half, packed)
    kv.hand_on()
    outs.send()
    near = jnp.stack([packed] + [flip(packed, "fsdp", j) for j in (1, 2, 3)])
    small = jnp.concatenate([pick(near, shard ^ j) for j in range(4)], axis=0)
    gains = small[:, : 3 * rows].reshape(4, 3, rows).transpose(1, 0, 2).reshape(3, model).astype(f32)
    gains = jnp.pad(gains, ((0, 5), (0, 0)))
    table = small[:, 3 * rows : 3 * rows + rel_bias.size].reshape(-1, H)
    onehot = (bucket_ids(length)[:, :, None] == jnp.arange(table.shape[0], dtype=jnp.int32)).astype(f32)
    bias = jnp.einsum("ijn,nh->hij", onehot, table.astype(f32), precision=highest)
    bias = bias.reshape(QUADS, QUAD, length, length).transpose(0, 3, 1, 2).reshape(QUADS, length, QUAD * length)
    kv.passed, wide.half = steps.gate(kv.passed, wide.half)
    kv.end()
    wide.send()
    qkv.direct, narrow.half, gains, bias = steps.gate(qkv.direct, narrow.half, gains, bias)
    qkv.hand_on()
    narrow.send()
    stacked = QUAD * length
    slot_rows = by_slot(length, model)
    enc_rows = by_slot(enc, model, held=True)
    unit = 2 * total * model * model
    enc_unit = 2 * slots * enc * model * model
    attend_unit = 2 * slots * enc * length * model * QUAD
    flat = tokens.reshape(total, model)
    by_slots = (slots, length, model)
    low = shape((total, model), bf16)
    wide_f32 = shape((total, model), f32)
    lse_spec = by_slot(8, stacked)
    gain_shape = shape((8, model), f32)
    sems = pltpu.SemaphoreType.DMA

    enc_wide = by_slot(enc, 2 * model, held=True)
    both = shape((slots, enc, 2 * model), bf16)
    beside = [pltpu.VMEM((model, 2 * model), bf16), sems((2, 6))]
    (keys_values,) = steps.call(
        memory_kernel,
        [both],
        [enc_rows] + [ANY] * 6,
        [enc_wide],
        beside,
        cost(2 * enc_unit, 6 * memory.size),
        [memory, *kv.pieces()],
        grid=(slots,),
    )
    outs.direct, qkv.passed = steps.gate(outs.direct, qkv.passed)
    outs.hand_on()
    qkv.end()
    normed1, q1, k1, v1, a1, lse1 = steps.call(
        self_kernel,
        [low, low, low, low, low, shape((slots, 8, stacked), f32)],
        [VMEM] * 3 + [ANY] * 6,
        [VMEM] * 6,
        [pltpu.VMEM((3, model, model), bf16), sems((6,))],
        cost(3 * unit + attend_unit / 4, 12 * total * model, slots * H * length * length),
        [flat, gains, bias, *qkv.pieces()],
    )
    outs.passed, wide.direct = steps.gate(outs.passed, wide.direct)
    outs.end()
    wide.hand_on()
    (narrow.direct,) = steps.gate(narrow.direct)
    narrow.hand_on()
    h1, normed2, q2 = steps.call(
        query_kernel,
        [wide_f32, low, low],
        [VMEM] * 3 + [ANY] * 6,
        [VMEM] * 3,
        [pltpu.VMEM((2, model, model), bf16), sems((6,))],
        cost(2 * unit, 12 * total * model),
        [flat, a1, gains, *outs.pieces()],
    )
    a2, lse2 = steps.call(
        cross_kernel,
        [shape(by_slots, bf16), shape((slots, 8, stacked), f32)],
        [slot_rows, enc_wide],
        [slot_rows, lse_spec],
        [],
        cost(2 * attend_unit, 4 * memory.size, slots * H * length * enc),
        [q2.reshape(by_slots), keys_values],
        grid=(slots,),
    )
    wide.passed, narrow.passed = steps.gate(wide.passed, narrow.passed)
    wide.end()
    narrow.end()
    flat2 = a2.reshape(total, model)

    pair = [(rows, model)] * 2
    order = [(0, 0), (1, 0)]
    pieces = {
        "W1": Piece(steps, place, [(rows, hidden)], [(0, c * model) for c in range(4)]),
        "W2": Piece(steps, place, [(hidden // 4, model)], [(0, 0)]),
        "S1": Piece(steps, place, [(rows, model)] * 4, [(i, 0) for i in range(4)]),
        "S2": Piece(steps, place, pair, order),
        "M": Piece(steps, place, pair + [(TINY, model)], order + [(2, 0)], tall=False),
    }
    one = shape((2, 4 * rows, model), bf16)
    half = shape((2, 2 * rows, model), bf16)
    tall = pltpu.VMEM((total, model), f32)
    slim = pltpu.VMEM((total, model), bf16)
    output, g2, ga2, gain_three, keep_n, send_n, keep_w, send_w, keep_o, send_o = steps.call(
        ff_kernel,
        [low, wide_f32, low, gain_shape, one, one, one, one, one, one],
        [VMEM] * 4 + [ANY] * 18,
        [VMEM] * 4 + [ANY] * 6,
        [
            pltpu.VMEM((1, model, model), bf16),
            pltpu.VMEM((1, model, hidden), bf16),
            pltpu.VMEM((1, hidden, model), bf16),
            slim,
            slim,
            pltpu.VMEM((4, model, model), bf16),
            pltpu.VMEM((4, model, model), bf16),
            pltpu.VMEM((model, model), bf16),
            tall,
            tall,
            tall,
            sems((3, 6)),
            sems((4,)),
            sems((16,)),
            sems((4,)),
        ],
        after=0,
        estimate=cost(27 * unit, 40e6, total * hidden),
        operands=[h1, flat2, cotangent, gains, *outs.pieces(), *wide.pieces(), *narrow.pieces()],
    )
    pieces["W1"].ready(keep_w, send_w)
    pieces["W2"].ready(keep_n, send_n)
    got = {}

    def cross_back():
        got["gq2"], got["gkv"] = steps.call(
            cross_back_kernel,
            [shape(by_slots, bf16), both],
            [slot_rows, slot_rows, slot_rows, lse_spec, enc_wide],
            [slot_rows, enc_wide],
            [],
            after=0,
            estimate=cost(5 * attend_unit, 8 * memory.size, slots * H * length * enc),
            operands=[q2.reshape(by_slots), ga2.reshape(by_slots), a2, lse2, keys_values],
            grid=(slots,),
        )

    def self_back():
        got["tokens"], got["tiny"], keep, send, keep_s, send_s = steps.call(
            self_back_kernel,
            [wide_f32, shape((TINY, model), bf16), one, one, half, half],
            [VMEM] * 14 + [ANY] * 14,
            [VMEM] * 2 + [ANY] * 4,
            [
                pltpu.VMEM((QUADS, length, stacked), f32),
                pltpu.VMEM((2, model, model), bf16),
                pltpu.VMEM((3, model, model), bf16),
                pltpu.VMEM((5, model, model), bf16),
                slim,
                slim,
                slim,
                slim,
                sems((2, 6)),
                sems((5, 4)),
            ],
            cost(10 * unit + attend_unit, 40 * total * model, slots * H * length * length),
            [
                *(got["gq2"].reshape(total, model), normed2, h1, g2, a1, q1, k1, v1, lse1, normed1, flat),
                *(gains, bias, gain_three, keep_o, send_o, *outs.pieces(), *qkv.pieces()),
            ],
            aliases={14: 2, 15: 3},
            after=0,
        )
        pieces["S1"].ready(keep, send)
        pieces["S2"].ready(keep_s, send_s)

    def memory_weights():
        keep, send = steps.call(
            memory_weight_kernel,
            [shape((2, 2 * rows + TINY, model), bf16)] * 2,
            [enc_rows, enc_wide, pl.BlockSpec((TINY, model), lambda *_: (0, 0))],
            [ANY, ANY],
            [pltpu.VMEM((model, 2 * model), f32), pltpu.VMEM((2, model, model), bf16), sems((3, 4))],
            cost(2 * enc_unit, 6 * memory.size),
            [memory, got["gkv"], got["tiny"]],
            grid=(slots,),
            after=0,
        )
        pieces["M"].ready(keep, send)

    def memory_back():
        (got["memory"],) = steps.call(
            memory_grad_kernel,
            [shape(memory.shape, f32)],
            [enc_wide] + [ANY] * 6,
            [by_slot(enc, model)],
            beside,
            cost(2 * enc_unit, 8 * memory.size),
            [got["gkv"], *kv.pieces()],
            grid=(slots,),
            after=0,
        )

    kernels = {"KE": cross_back, "KF": self_back, "KW": memory_weights, "KG": memory_back}
    for group in ORDER:
        if group in kernels:
            kernels[group]()
            steps.fresh = True
        elif group == "!":
            steps.fresh = False
            waiting, steps.pending = steps.pending, []
            sends = steps.gate(*(piece.send for piece in waiting))
            for piece, send in zip(waiting, sends):
                piece.got = flip(send, "fsdp", 1)
        else:
            members = [step.split(".") for step in group]
            if steps.fresh:
                used = list(dict.fromkeys(name for name, _ in members))
                for name, value in zip(used, steps.gate(*(pieces[name].keep for name in used))):
                    pieces[name].keep = value
                steps.fresh = False
            for name, stage in members:
                getattr(pieces[name], stage)()

    sum_co, sum_cq, sum_so, sum_sq = pieces["S1"].result
    sum_sk, sum_sv = pieces["S2"].result
    sum_ck, sum_cv, tiny = pieces["M"].result
    ours = lax.dynamic_slice_in_dim(tiny[0:3], shard * rows, rows, 1)
    ours_table = lax.dynamic_slice_in_dim(tiny[8 : 8 + BUCKETS, :H], shard * rel_bias.shape[0], rel_bias.shape[0], 0)
    return (
        output.reshape(tokens.shape),
        got["tokens"].reshape(tokens.shape),
        got["memory"],
        ours[0],
        sum_sq,
        sum_sk,
        sum_sv,
        sum_so,
        ours_table,
        ours[1],
        sum_cq,
        sum_ck,
        sum_cv,
        sum_co,
        ours[2],
        pieces["W1"].result[0],
        pieces["W2"].result[0],
    )


def solution(mesh):
    in_specs = (
        P(("dp", "fsdp"), None, None),
        P(("dp", "fsdp"), None, None),
        P(("dp", "fsdp")),
        P(("dp", "fsdp")),
        P(("dp", "fsdp")),
        P("fsdp"),
        P("fsdp", None),
        P("fsdp", None),
        P("fsdp", None),
        P("fsdp", None),
        P("fsdp", None),
        P("fsdp"),
        P("fsdp", None),
        P("fsdp", None),
        P("fsdp", None),
        P("fsdp", None),
        P("fsdp"),
        P("fsdp", None),
        P("fsdp", None),
        P(("dp", "fsdp"), None, None),
    )
    out_specs = (
        P(("dp", "fsdp"), None, None),
        P(("dp", "fsdp"), None, None),
        P(("dp", "fsdp"), None, None),
        P("fsdp"),
        P("fsdp", None),
        P("fsdp", None),
        P("fsdp", None),
        P("fsdp", None),
        P("fsdp", None),
        P("fsdp"),
        P("fsdp", None),
        P("fsdp", None),
        P("fsdp", None),
        P("fsdp", None),
        P("fsdp"),
        P("fsdp", None),
        P("fsdp", None),
    )
    return jax.shard_map(
        on_device, mesh=mesh, in_specs=in_specs, out_specs=out_specs, check_vma=False
    )
```

```python
import functools
import math

import jax
import jax.numpy as jnp
from jax import lax
from jax.experimental import pallas as pl
from jax.experimental.pallas import tpu as pltpu
from jax.sharding import PartitionSpec as P

H = 12
DH = 64
QUAD = 4
QUADS = H // QUAD
WIDE = QUAD * DH
CHUNK = 256
MASKED = -1000000000.0
WAY_X, WAY_Z, PLACE = 1, 3, 16
BUCKETS = 32
TINY = 64

bucket_edges = [math.ceil(16 * 8 ** (exponent / 16)) for exponent in range(1, 16)]
f32 = jnp.float32
bf16 = jnp.bfloat16


def flip(values, axis, bit):
    size = lax.axis_size(axis)
    return lax.ppermute(values, axis, [(i, i ^ bit) for i in range(size)])


def pick(values, index):
    return lax.dynamic_index_in_dim(values, index, 0, keepdims=False)


def add_low(left, right):
    return (left.astype(f32) + right.astype(f32)).astype(bf16)


def mm(left, right):
    return jnp.dot(left, right, preferred_element_type=f32)


def mm_nt(left, right):
    return lax.dot_general(left, right, (((1,), (1,)), ((), ())), preferred_element_type=f32)


def mm_tn(left, right):
    return lax.dot_general(left, right, (((0,), (0,)), ((), ())), preferred_element_type=f32)


def piece_starts(meta, pieces, way):
    shard, side = meta[0], meta[way]
    rows = pieces[0].shape[1]
    half = rows // 2
    return (
        shard * rows,
        (shard ^ 1) * rows,
        (shard ^ 2) * rows + side * half,
        (shard ^ 2) * rows + (1 - side) * half,
        (shard ^ 3) * rows + side * half,
        (shard ^ 3) * rows + (1 - side) * half,
    )


def copies_in(meta, pieces, whole, sems, way, only=slice(None), cols=slice(None)):
    return [
        pltpu.make_async_copy(
            piece.at[only, :, cols],
            whole.at[:, pl.ds(pl.multiple_of(start, 32), piece.shape[1])],
            sems.at[i],
        )
        for i, (piece, start) in enumerate(zip(pieces, piece_starts(meta, pieces, way)))
    ]


def start_all(copies):
    for copy in copies:
        copy.start()


def wait_all(copies):
    for copy in copies:
        copy.wait()


def copies_out(meta, whole, keep, send, at, sems):
    shard = meta[0]
    rows = whole.shape[0] // 4
    return [
        pltpu.make_async_copy(
            whole.at[pl.ds(pl.multiple_of((shard ^ j) * rows, 32), rows)],
            (send if j % 2 else keep).at[j // 2, pl.ds(at * rows, rows)],
            sems.at[j],
        )
        for j in range(4)
    ]


def norm_rho(hidden):
    return lax.rsqrt(jnp.mean(hidden * hidden, axis=-1, keepdims=True) + 1e-06)


def norm_back(hidden, gain, upstream):
    rho = norm_rho(hidden)
    scaled = upstream * gain
    inner = jnp.mean(scaled * hidden, axis=-1, keepdims=True)
    grad = rho * scaled - hidden * (rho * rho * rho * inner)
    return grad, jnp.sum(upstream * hidden * rho, axis=0, keepdims=True)


def head_masks():
    lane = lax.broadcasted_iota(jnp.int32, (1, WIDE), 1) // DH
    return [(lane == h).astype(f32).astype(bf16) for h in range(QUAD)]


def stack_heads(values, masks):
    return jnp.concatenate([values * mask for mask in masks], axis=0)


def own_heads(mixed):
    rows = mixed.shape[1] // QUAD
    own = [mixed[h * DH : (h + 1) * DH, h * rows : (h + 1) * rows] for h in range(QUAD)]
    return jnp.concatenate(own, axis=0).T


def head_sums(product):
    high = product.astype(bf16)
    low = (product - high.astype(f32)).astype(bf16)
    ones = jnp.ones((8, WIDE), bf16)
    return (mm_nt(ones, high) + mm_nt(ones, low))[0:1]


def fold(values, op):
    return op(values.reshape(values.shape[0] // 8, 8, values.shape[1]), axis=0)


def quad_at(quad):
    return pl.ds(quad * WIDE, WIDE)


def copies_beside(meta, pieces, whole, sems, way):
    columns = pieces[0].shape[2]
    starts = piece_starts(meta, pieces, way)
    return [
        pltpu.make_async_copy(
            piece.at[j],
            whole.at[pl.ds(pl.multiple_of(start, 32), piece.shape[1]), pl.ds(j * columns, columns)],
            sems.at[j, i],
        )
        for j in range(2)
        for i, (piece, start) in enumerate(zip(pieces, starts))
    ]


def each_count(meta, slot, most, body):
    for n in range(1, most // CHUNK + 1):
        pl.when(meta[12 + slot] == n)(functools.partial(body, n * CHUNK))


def memory_kernel(meta, memory, *refs):
    pieces, (out, whole, sems) = refs[:6], refs[6:]
    slot = pl.program_id(0)

    @pl.when(slot == 0)
    def _():
        copies = copies_beside(meta, pieces, whole, sems, WAY_X)
        start_all(copies)
        wait_all(copies)

    def project(rows):
        out[0, :rows, :] = mm(memory[0, :rows, :], whole[...]).astype(bf16)

    each_count(meta, slot, memory.shape[1], project)


def buckets_of(length):
    key_at = lax.broadcasted_iota(jnp.int32, (length, length), 0)
    distance = jnp.maximum(lax.broadcasted_iota(jnp.int32, (length, length), 1) - key_at, 0)
    bucket = jnp.minimum(distance, 16)
    for edge in bucket_edges:
        bucket = bucket + (distance >= edge).astype(jnp.int32)
    return bucket


def self_kernel(meta, tokens, gains, table, *refs):
    pieces = refs[:6]
    bias, normed_out, q_out, k_out, v_out, mixed_out, lse_out, whole, sems = refs[6:]
    copies = copies_in(meta, pieces, whole, sems, WAY_Z)
    start_all(copies)
    hidden = tokens[...].astype(f32)
    normed = (hidden * norm_rho(hidden) * gains[0:1]).astype(bf16)
    normed_out[...] = normed
    length = bias.shape[1]
    bucket = buckets_of(length)
    for head in range(H):
        block = jnp.zeros((length, length), f32)
        for n in range(BUCKETS):
            block = jnp.where(bucket == n, table[n, head], block)
        at = head % QUAD * length
        bias[head // QUAD, :, at : at + length] = block
    wait_all(copies)
    q_out[...] = mm(normed, whole[0]).astype(bf16)
    k_out[...] = mm(normed, whole[1]).astype(bf16)
    v_out[...] = mm(normed, whole[2]).astype(bf16)
    length = bias.shape[1]
    masks = head_masks()
    key_at = lax.broadcasted_iota(jnp.int32, (length, QUAD * length), 0)
    query_at = lax.broadcasted_iota(jnp.int32, (length, QUAD * length), 1) % length
    for b in range(lse_out.shape[0]):
        rows = slice(b * length, (b + 1) * length)
        ok = (key_at <= query_at) & (key_at < meta[4 + b])
        for quad in range(QUADS):
            at = slice(quad * WIDE, (quad + 1) * WIDE)
            scores = mm_nt(k_out[rows, at], stack_heads(q_out[rows, at], masks)) + bias[quad]
            scores = jnp.where(ok, scores, MASKED)
            top = jnp.max(scores, axis=0, keepdims=True)
            raised = jnp.exp(scores - top)
            total = jnp.sum(raised, axis=0, keepdims=True)
            weights = (raised * (1.0 / total)).astype(bf16)
            mixed_out[rows, at] = own_heads(mm(v_out[rows, at].T, weights)).astype(bf16)
            lse_out[b, quad : quad + 1, :] = top + jnp.log(total)


def query_kernel(meta, tokens, mixed, gains, *refs):
    pieces, (h1_out, normed2_out, q2_out, whole, sems) = refs[:6], refs[6:]
    copies = copies_in(meta, pieces, whole, sems, WAY_X, pl.ds(0, 2))
    start_all(copies)
    wait_all(copies)
    first = tokens[...].astype(f32) + mm(mixed[...], whole[0])
    h1_out[...] = first
    normed2 = (first * norm_rho(first) * gains[1:2]).astype(bf16)
    normed2_out[...] = normed2
    q2_out[...] = mm(normed2, whole[1]).astype(bf16)


def cross_kernel(meta, queries, memory, mixed_out, lse_out):
    slot = pl.program_id(0)
    model = queries.shape[2]

    @pl.when(meta[12 + slot] == 0)
    def _():
        mixed_out[...] = jnp.zeros(mixed_out.shape, bf16)
        lse_out[...] = jnp.zeros(lse_out.shape, f32)

    def attend(rows):
        masks = head_masks()
        ok = lax.broadcasted_iota(jnp.int32, (rows, 1), 0) < meta[8 + slot]
        for quad in range(QUADS):
            at, at_v = slice(quad * WIDE, (quad + 1) * WIDE), slice(model + quad * WIDE, model + (quad + 1) * WIDE)
            stacked = stack_heads(queries[0, :, at], masks)
            scores = jnp.where(ok, mm_nt(memory[0, :rows, at], stacked), MASKED)
            top = jnp.max(scores, axis=0, keepdims=True)
            raised = jnp.exp(scores - top)
            total = jnp.sum(raised, axis=0, keepdims=True)
            mixed = mm(memory[0, :rows, at_v].T, raised.astype(bf16))
            mixed_out[0, :, at] = own_heads(mixed * (1.0 / total)).astype(bf16)
            lse_out[0, quad : quad + 1, :] = top + jnp.log(total)

    each_count(meta, slot, memory.shape[1], attend)


def gelu_both(values):
    scale = math.sqrt(2.0 / math.pi)
    square = values * values
    slope = jnp.tanh(scale * values * (1.0 + 0.044715 * square))
    half = 0.5 * (1.0 + slope)
    back = half + 0.5 * values * (1.0 - slope * slope) * (scale * (1.0 + 3 * 0.044715 * square))
    return values * half, back


def live_rows(meta, slots, length):
    positions = lax.broadcasted_iota(jnp.int32, (length, 1), 0)
    return jnp.concatenate(
        [((positions < meta[4 + b]) & (b < meta[2])).astype(f32) for b in range(slots)], axis=0
    )


def ff_kernel(meta, h1, mixed, cotangent, gains, *refs):
    square, wide, narrow, refs = refs[:6], refs[6:12], refs[12:18], refs[18:]
    (output, g2_out, ga2_out, gain_out, keep_n, send_n, keep_w, send_w, keep_o, send_o), refs = refs[:10], refs[10:]
    co, w_in, w_out, gf, normed, grad_n, grad_w, grad_o, second, third, back, in_sems, n_sems, w_sems, o_sems = refs
    model = h1.shape[1]
    rows = model // 4
    shard = meta[0]
    co_in = copies_in(meta, square, co, in_sems.at[0], WAY_X, pl.ds(2, 1))
    in_in = copies_in(meta, wide, w_in, in_sems.at[1], WAY_Z)
    out_in = copies_in(meta, narrow, w_out, in_sems.at[2], WAY_X)
    start_all(co_in)
    start_all(in_in)
    start_all(out_in)
    live = live_rows(meta, cotangent.shape[0], cotangent.shape[1])
    gf[...] = (cotangent[...].reshape(h1.shape).astype(f32) * live).astype(bf16)
    wait_all(co_in)
    second[...] = h1[...] + mm(mixed[...], co[0])
    hidden = second[...]
    normed[...] = (hidden * norm_rho(hidden) * gains[2:3]).astype(bf16)
    normed_t = normed[...].T
    wait_all(in_in)
    waits = []
    for j in range(4):
        cols = pl.ds(pl.multiple_of((shard ^ j) * model, model), model)
        units, slope = gelu_both(mm(normed[...], w_in[0, :, cols]))
        low = units.astype(bf16)
        if j == 0:
            wait_all(out_in)
        wide_out = mm(low, w_out[0, cols, :])
        grad_n[j] = mm_tn(low, gf[...]).astype(bf16)
        waits.append(pltpu.make_async_copy(grad_n.at[j], (send_n if j % 2 else keep_n).at[j // 2], n_sems.at[j]))
        waits[-1].start()
        grad_units = (mm_nt(gf[...], w_out[0, cols, :]) * slope).astype(bf16)
        grad_w[j] = mm(normed_t, grad_units).astype(bf16)
        at = pl.ds(pl.multiple_of((shard ^ j) * rows, 32), rows)
        for i in range(4):
            waits.append(
                pltpu.make_async_copy(
                    grad_w.at[j, pl.ds(pl.multiple_of((shard ^ i) * rows, 32), rows)],
                    (send_w if i % 2 else keep_w).at[i // 2, at],
                    w_sems.at[4 * j + i],
                )
            )
            waits[-1].start()
        grad_normed = mm_nt(grad_units, w_in[0, :, cols])
        if j == 0:
            third[...] = second[...] + wide_out
            back[...] = grad_normed
        else:
            third[...] += wide_out
            back[...] += grad_normed
    output[...] = (third[...] * live).astype(bf16)
    grad, gain = norm_back(second[...], gains[2:3], back[...])
    gain_out[...] = jnp.broadcast_to(gain, gain_out.shape)
    g2 = gf[...].astype(f32) + grad
    g2_out[...] = g2
    go2 = g2.astype(bf16)
    ga2_out[...] = mm_nt(go2, co[0]).astype(bf16)
    grad_o[...] = mm_tn(mixed[...], go2).astype(bf16)
    out = copies_out(meta, grad_o, keep_o, send_o, 0, o_sems)
    start_all(out)
    wait_all(waits)
    wait_all(out)


def cross_back_kernel(meta, queries, grads, mixed, lse, memory, gq_out, out):
    slot = pl.program_id(0)
    model = queries.shape[2]

    @pl.when(meta[12 + slot] == 0)
    def _():
        gq_out[...] = jnp.zeros(gq_out.shape, bf16)

    def attend(rows):
        masks = head_masks()
        ok = lax.broadcasted_iota(jnp.int32, (rows, 1), 0) < meta[8 + slot]
        for quad in range(QUADS):
            at, at_v = slice(quad * WIDE, (quad + 1) * WIDE), slice(model + quad * WIDE, model + (quad + 1) * WIDE)
            q_stack = stack_heads(queries[0, :, at], masks)
            g_stack = stack_heads(grads[0, :, at], masks)
            tiled = jnp.concatenate([mixed[0, :, at].astype(f32)] * QUAD, axis=0)
            delta = head_sums(g_stack.astype(f32) * tiled)
            block = memory[0, :rows, at]
            scores = jnp.where(ok, mm_nt(block, q_stack), MASKED)
            share = jnp.exp(scores - lse[0, quad : quad + 1, :])
            grad_share = mm_nt(memory[0, :rows, at_v], g_stack)
            grad_scores = (share * (grad_share - delta)).astype(bf16)
            out[0, :rows, at_v] = mm(share.astype(bf16), g_stack).astype(bf16)
            out[0, :rows, at] = mm(grad_scores, q_stack).astype(bf16)
            gq_out[0, :, at] = own_heads(mm(block.T, grad_scores)).astype(bf16)

    each_count(meta, slot, memory.shape[1], attend)


def table_grad(scores):
    length = scores.shape[1]
    bucket = jnp.concatenate([buckets_of(length)] * QUAD, axis=1)
    head = lax.broadcasted_iota(jnp.int32, (QUAD * length, 128), 0) // length
    column = lax.broadcasted_iota(jnp.int32, (QUAD * length, 128), 1)
    table = jnp.zeros((BUCKETS, 128), f32)
    for quad in range(QUADS):
        values = scores[quad]
        sums = [jnp.sum(jnp.where(bucket == n, values, 0.0), axis=0, keepdims=True) for n in range(BUCKETS)]
        sums = jnp.concatenate(sums, axis=0)
        high = sums.astype(bf16)
        low = (sums - high.astype(f32)).astype(bf16)
        to_head = (column == head + quad * QUAD).astype(f32).astype(bf16)
        table = table + mm(high, to_head) + mm(low, to_head)
    return table


def self_back_kernel(
    meta, gq2, normed2, h1, g2, mixed, q, k, v, lse, normed, tokens, gains, bias, keep_in, send_in, *refs
):
    query, pieces, refs = refs[:6], refs[6:12], refs[12:]
    (grad_out, gain_out, bias_out, keep, send, keep_s, send_s), refs = refs[:7], refs[7:]
    square, whole, grads, ga1, gq, gk, gv, in_sems, sems = refs
    copies_q = copies_in(meta, query, square, in_sems.at[0], WAY_X, pl.ds(0, 2))
    copies = copies_in(meta, pieces, whole, in_sems.at[1], WAY_Z)
    start_all(copies_q)
    start_all(copies)
    outs = []

    def emit(index, value, *place):
        grads[index] = value.astype(bf16)
        outs.extend(copies_out(meta, grads.at[index], *place, sems.at[index]))
        start_all(outs[-4:])

    emit(0, mm_tn(normed2[...], gq2[...]), keep, send, 1)
    wait_all(copies_q)
    grad, gain_two = norm_back(h1[...], gains[1:2], mm_nt(gq2[...], square[1]))
    g1 = g2[...] + grad
    grad_out[...] = g1
    go1 = g1.astype(bf16)
    emit(1, mm_tn(mixed[...], go1), keep, send, 2)
    ga1[...] = mm_nt(go1, square[0]).astype(bf16)
    length = bias.shape[1]
    masks = head_masks()
    key_at = lax.broadcasted_iota(jnp.int32, (length, QUAD * length), 0)
    query_at = lax.broadcasted_iota(jnp.int32, (length, QUAD * length), 1) % length
    for b in range(lse.shape[0]):
        rows = slice(b * length, (b + 1) * length)
        ok = (key_at <= query_at) & (key_at < meta[4 + b])
        for quad in range(QUADS):
            at = slice(quad * WIDE, (quad + 1) * WIDE)
            q_stack = stack_heads(q[rows, at], masks)
            g_stack = stack_heads(ga1[rows, at], masks)
            tiled = jnp.concatenate([mixed[rows, at].astype(f32)] * QUAD, axis=0)
            delta = head_sums(g_stack.astype(f32) * tiled)
            block = k[rows, at]
            scores = jnp.where(ok, mm_nt(block, q_stack) + bias[quad], MASKED)
            share = jnp.exp(scores - lse[b, quad : quad + 1, :])
            grad_share = mm_nt(v[rows, at], g_stack)
            grad_scores = (share * (grad_share - delta)).astype(bf16)
            gv[rows, at] = mm(share.astype(bf16), g_stack).astype(bf16)
            gk[rows, at] = mm(grad_scores, q_stack).astype(bf16)
            gq[rows, at] = own_heads(mm(block.T, grad_scores)).astype(bf16)
            if b == 0:
                bias_out[quad] = grad_scores.astype(f32)
            else:
                bias_out[quad] += grad_scores.astype(f32)
    normed_t = normed[...].T
    emit(2, mm(normed_t, gq[...]), keep, send, 3)
    emit(3, mm(normed_t, gk[...]), keep_s, send_s, 0)
    emit(4, mm(normed_t, gv[...]), keep_s, send_s, 1)
    wait_all(copies)
    grad_normed = mm_nt(gq[...], whole[0]) + mm_nt(gk[...], whole[1]) + mm_nt(gv[...], whole[2])
    grad, gain_one = norm_back(tokens[...].astype(f32), gains[0:1], grad_normed)
    grad_out[...] += grad
    gain_out[...] = jnp.concatenate([gain_one, gain_two, jnp.zeros((6, gain_one.shape[1]), f32)], axis=0)
    wait_all(outs)


def memory_weight_kernel(meta, memory, grads, gain_low, gain_three, scores, keep, send, total, low, tiny, sems):
    slot = pl.program_id(0)
    model = memory.shape[2]

    @pl.when(slot == 0)
    def _():
        total[...] = jnp.zeros(total.shape, f32)
        top = jnp.concatenate([gain_low[0:2], gain_three[0:1], jnp.zeros((5, model), f32)], axis=0)
        table = jnp.pad(table_grad(scores), ((0, 0), (0, model - 128)))
        rest = jnp.zeros((TINY - 8 - BUCKETS, model), f32)
        tiny[...] = jnp.concatenate([top, table, rest], axis=0).astype(bf16)

    def add(rows):
        total[...] += mm(memory[0, :rows, :].T, grads[0, :rows, :])

    each_count(meta, slot, memory.shape[1], add)

    @pl.when(slot == pl.num_programs(0) - 1)
    def _():
        rows = model // 4
        outs = [
            pltpu.make_async_copy(
                tiny,
                (send if j % 2 else keep).at[j // 2, pl.ds(2 * rows, tiny.shape[0])],
                sems.at[2, j],
            )
            for j in range(4)
        ]
        start_all(outs)
        for i in range(2):
            low[i] = total[:, i * model : (i + 1) * model].astype(bf16)
            outs += copies_out(meta, low.at[i], keep, send, i, sems.at[i])
            start_all(outs[-4:])
        wait_all(outs)


def memory_grad_kernel(meta, grads, *refs):
    pieces, (out, whole, sems) = refs[:6], refs[6:]
    slot = pl.program_id(0)

    @pl.when(slot == 0)
    def _():
        copies = copies_beside(meta, pieces, whole, sems, WAY_X)
        start_all(copies)
        wait_all(copies)

    def fill(rows):
        if rows:
            out[0, :rows, :] = mm_nt(grads[0, :rows, :], whole[...])
        if rows < out.shape[1]:
            out[0, rows:, :] = jnp.zeros((out.shape[1] - rows, out.shape[2]), f32)

    pl.when(meta[12 + slot] == 0)(functools.partial(fill, 0))
    each_count(meta, slot, out.shape[1], fill)


VMEM = pl.BlockSpec(memory_space=pltpu.VMEM)
ANY = pl.BlockSpec(memory_space=pl.ANY)


def cost(flops, moved, raised=0):
    del flops, moved, raised
    return pl.CostEstimate(flops=1024, bytes_accessed=1024, transcendentals=0)


def shape(dims, dtype):
    return jax.ShapeDtypeStruct(tuple(dims), dtype)


def live_slot(b, meta):
    return jnp.where(meta[12 + b] > 0, b, jnp.maximum(meta[2] - 1, 0))


def by_slot(rows, model, held=False):
    if held:
        return pl.BlockSpec((1, rows, model), lambda b, meta: (live_slot(b, meta), 0, 0))
    return pl.BlockSpec((1, rows, model), lambda b, meta: (b, 0, 0))


class Steps:
    def __init__(self, meta):
        self.meta = meta
        self.token = meta
        self.marks = []
        self.last = None
        self.pending = []
        self.fresh = False

    def call(self, kernel, outs, in_specs, out_specs, scratch, estimate, operands, grid=(), aliases=None, after=None):
        count = len(outs)
        order = [self.token]
        if self.marks:
            order.extend(self.marks)
        first = 1 + len(order)

        def body(meta, *refs):
            refs = refs[len(order) :]
            ins, rest = refs[: len(operands)], refs[len(operands) :]
            kernel(meta, *ins, *rest[:count], *rest[count + 1 :])

        result = pl.pallas_call(
            body,
            out_shape=tuple(outs) + (shape((16, 128), f32),),
            grid_spec=pltpu.PrefetchScalarGridSpec(
                num_scalar_prefetch=1,
                grid=grid,
                in_specs=[ANY] * len(order) + list(in_specs),
                out_specs=tuple(out_specs) + (ANY,),
                scratch_shapes=scratch,
            ),
            input_output_aliases={first + i: o for i, o in (aliases or {}).items()},
            compiler_params=pltpu.CompilerParams(vmem_limit_bytes=56 * 1024 * 1024),
            cost_estimate=estimate,
        )(self.meta, *order, *operands)
        self.token, self.marks = result[-1], []
        return result[:-1]

    def mark(self, result):
        self.marks.append(result)

    def gate(self, *values):
        outs = self.call(
            lambda *refs: None,
            [shape(v.shape, v.dtype) for v in values],
            [ANY] * len(values),
            [ANY] * len(values),
            [],
            cost(0, 0),
            values,
            aliases={i: i for i in range(len(values))},
        )
        return outs


class Bundle:
    def __init__(self, own, place, bit):
        rows = own.shape[1] // 2
        self.own, self.bit = own, bit
        self.half = lax.dynamic_slice_in_dim(own, (place // bit) % 2 * rows, rows, 1)

    def send(self):
        self.direct = flip(self.half, "fsdp", 2)
        self.beside = flip(self.own, "fsdp", 1)

    def hand_on(self):
        self.passed = flip(self.direct, "dp", self.bit)
        self.direct_beside = flip(self.direct, "fsdp", 1)

    def end(self):
        self.passed_beside = flip(self.passed, "fsdp", 1)

    def pieces(self):
        return (self.own, self.beside, self.direct, self.passed, self.direct_beside, self.passed_beside)


class Piece:
    def __init__(self, steps, place, outs, blocks, tall=True):
        self.steps, self.outs, self.blocks = steps, outs, blocks
        self.place, self.tall = place, tall and lax.axis_size("dp") > 2

    def ready(self, keep, send):
        self.keep, self.send = keep, send
        self.steps.pending.append(self)

    def add(self, left, right):
        return (left.astype(f32) + right.astype(f32)).astype(bf16)

    def cut(self, which, axis):
        half = self.keep.shape[axis] // 2
        return [lax.dynamic_slice_in_dim(v, which * half, half, axis) for v in (self.keep, self.got)]

    def core(self):
        far = self.add(self.keep[1], self.got[1])
        self.keep, self.got = self.add(self.keep[0], self.got[0]), flip(far, "fsdp", 2)
        self.steps.mark(far)

    def halve(self, bit, axis):
        side = self.place // bit % 2
        send = self.add(*self.cut(1 - side, axis))
        self.keep, self.got = self.add(*self.cut(side, axis)), flip(send, "dp", bit)
        self.steps.mark(send)

    def y(self):
        self.halve(1, 1)

    def x(self):
        if self.tall:
            self.halve(2, 0)
        else:
            self.pass_on(2)

    def pass_on(self, bit):
        self.keep = self.add(self.keep, self.got)
        self.got = flip(self.keep, "dp", bit)
        self.steps.mark(self.keep)

    def z(self):
        bit = 4
        while bit < lax.axis_size("dp"):
            self.pass_on(bit)
            bit *= 2

    def w(self):
        self.pass_on(2 if self.tall else 1)

    def joined(self, axis, bit, dtype, rows=slice(None)):
        mine, other = self.keep[rows].astype(dtype), self.got[rows].astype(dtype)
        low = self.place // bit % 2 == 0
        return jnp.concatenate([jnp.where(low, mine, other), jnp.where(low, other, mine)], axis=axis)

    def v(self):
        self.keep = self.joined(0, 2, bf16)
        self.got = flip(self.keep, "dp", 1)
        self.steps.mark(self.keep)

    def end(self):
        at = 0
        parts = {}
        for which, _ in self.blocks:
            rows = self.outs[which][0]
            parts.setdefault(which, []).append(self.joined(1, 1, f32, slice(at, at + rows)))
            at += rows
        self.result = [jnp.concatenate(parts[which], axis=1) for which in range(len(self.outs))]
        self.steps.mark(self.result[0])


ORDER = (
    "!",
    ("W1.core",),
    ("W2.core",),
    "KE",
    ("W1.y",),
    "KF",
    ("W2.y", "W1.x"),
    "!",
    ("S1.core", "S2.core"),
    "KW",
    ("S1.y", "W2.x", "W1.z"),
    "!",
    ("M.core",),
    "KG",
    ("S1.x", "W2.z", "W1.w", "S2.y"),
    ("M.y",),
    "|",
    ("W2.w", "S2.x", "S1.z", "W1.v"),
    "|",
    ("M.x", "S2.z"),
    ("S1.w", "W2.v"),
    "|",
    ("M.z", "S1.v", "S2.w"),
    "|",
    ("M.w", "S2.v"),
    ("W1.end", "W2.end", "S1.end", "S2.end", "M.end"),
)


def on_device(
    tokens,
    memory,
    tgt_len,
    enc_len,
    ex_count,
    self_gain,
    self_q,
    self_k,
    self_v,
    self_out,
    rel_bias,
    cross_gain,
    cross_q,
    cross_k,
    cross_v,
    cross_out,
    ff_gain,
    ff_in,
    ff_out,
    cotangent,
):
    slots, length, model = tokens.shape
    enc = memory.shape[1]
    hidden = ff_in.shape[1]
    rows = self_q.shape[0]
    total = slots * length
    shard = lax.axis_index("fsdp")
    place = lax.axis_index("dp")
    live = jnp.arange(slots, dtype=jnp.int32) < ex_count[0]
    chunks = jnp.where(live, (enc_len + CHUNK - 1) // CHUNK, 0)
    first = jnp.stack([shard, place % 2, ex_count[0], place // 2 % 2])
    meta = jnp.concatenate([first, tgt_len, enc_len, chunks, place[None]])
    steps = Steps(meta)

    kv = Bundle(jnp.stack([cross_k, cross_v]), place, 1)
    qkv = Bundle(jnp.stack([self_q, self_k, self_v]), place, 2)
    outs = Bundle(jnp.stack([self_out, cross_q, cross_out]), place, 1)
    wide = Bundle(ff_in[None], place, 2)
    narrow = Bundle(ff_out[None], place, 1)
    packed = jnp.concatenate([self_gain, cross_gain, ff_gain, rel_bias.reshape(-1)])
    packed = jnp.pad(packed, (0, model - packed.shape[0]))[None]
    kv.send()
    qkv.send()
    kv.direct, outs.half = steps.gate(kv.direct, outs.half)
    kv.hand_on()
    outs.send()
    kv.passed, qkv.direct, wide.half, narrow.half, packed = steps.gate(
        kv.passed, qkv.direct, wide.half, narrow.half, packed
    )
    kv.end()
    qkv.hand_on()
    wide.send()
    narrow.send()
    near = jnp.stack([packed] + [flip(packed, "fsdp", j) for j in (1, 2, 3)])
    small = jnp.concatenate([pick(near, shard ^ j) for j in range(4)], axis=0)
    gains = small[:, : 3 * rows].reshape(4, 3, rows).transpose(1, 0, 2).reshape(3, model).astype(f32)
    gains = jnp.pad(gains, ((0, 5), (0, 0)))
    table = small[:, 3 * rows : 3 * rows + rel_bias.size].reshape(-1, H).astype(f32)
    stacked = QUAD * length
    slot_rows = by_slot(length, model)
    enc_rows = by_slot(enc, model, held=True)
    unit = 2 * total * model * model
    enc_unit = 2 * slots * enc * model * model
    attend_unit = 2 * slots * enc * length * model * QUAD
    flat = tokens.reshape(total, model)
    by_slots = (slots, length, model)
    low = shape((total, model), bf16)
    wide_f32 = shape((total, model), f32)
    lse_spec = by_slot(8, stacked)
    gain_shape = shape((8, model), f32)
    sems = pltpu.SemaphoreType.DMA

    enc_wide = by_slot(enc, 2 * model, held=True)
    both = shape((slots, enc, 2 * model), bf16)
    beside = [pltpu.VMEM((model, 2 * model), bf16), sems((2, 6))]
    (keys_values,) = steps.call(
        memory_kernel,
        [both],
        [enc_rows] + [ANY] * 6,
        [enc_wide],
        beside,
        cost(2 * enc_unit, 6 * memory.size),
        [memory, *kv.pieces()],
        grid=(slots,),
    )
    outs.direct, qkv.passed = steps.gate(outs.direct, qkv.passed)
    outs.hand_on()
    qkv.end()
    bias, normed1, q1, k1, v1, a1, lse1 = steps.call(
        self_kernel,
        [shape((QUADS, length, stacked), f32), low, low, low, low, low, shape((slots, 8, stacked), f32)],
        [VMEM] * 2 + [pl.BlockSpec(memory_space=pltpu.SMEM)] + [ANY] * 6,
        [VMEM] * 7,
        [pltpu.VMEM((3, model, model), bf16), sems((6,))],
        cost(3 * unit + attend_unit / 4, 12 * total * model, slots * H * length * length),
        [flat, gains, table, *qkv.pieces()],
    )
    outs.passed, wide.direct = steps.gate(outs.passed, wide.direct)
    outs.end()
    wide.hand_on()
    (narrow.direct,) = steps.gate(narrow.direct)
    narrow.hand_on()
    h1, normed2, q2 = steps.call(
        query_kernel,
        [wide_f32, low, low],
        [VMEM] * 3 + [ANY] * 6,
        [VMEM] * 3,
        [pltpu.VMEM((2, model, model), bf16), sems((6,))],
        cost(2 * unit, 12 * total * model),
        [flat, a1, gains, *outs.pieces()],
    )
    a2, lse2 = steps.call(
        cross_kernel,
        [shape(by_slots, bf16), shape((slots, 8, stacked), f32)],
        [slot_rows, enc_wide],
        [slot_rows, lse_spec],
        [],
        cost(2 * attend_unit, 4 * memory.size, slots * H * length * enc),
        [q2.reshape(by_slots), keys_values],
        grid=(slots,),
    )
    wide.passed, narrow.passed = steps.gate(wide.passed, narrow.passed)
    wide.end()
    narrow.end()
    flat2 = a2.reshape(total, model)

    pair = [(rows, model)] * 2
    order = [(0, 0), (1, 0)]
    pieces = {
        "W1": Piece(steps, place, [(rows, hidden)], [(0, c * model) for c in range(4)]),
        "W2": Piece(steps, place, [(hidden // 4, model)], [(0, 0)]),
        "S1": Piece(steps, place, [(rows, model)] * 4, [(i, 0) for i in range(4)]),
        "S2": Piece(steps, place, pair, order),
        "M": Piece(steps, place, pair + [(TINY, model)], order + [(2, 0)], tall=False),
    }
    one = shape((2, 4 * rows, model), bf16)
    half = shape((2, 2 * rows, model), bf16)
    tall = pltpu.VMEM((total, model), f32)
    slim = pltpu.VMEM((total, model), bf16)
    output, g2, ga2, gain_three, keep_n, send_n, keep_w, send_w, keep_o, send_o = steps.call(
        ff_kernel,
        [low, wide_f32, low, gain_shape, one, one, one, one, one, one],
        [VMEM] * 4 + [ANY] * 18,
        [VMEM] * 4 + [ANY] * 6,
        [
            pltpu.VMEM((1, model, model), bf16),
            pltpu.VMEM((1, model, hidden), bf16),
            pltpu.VMEM((1, hidden, model), bf16),
            slim,
            slim,
            pltpu.VMEM((4, model, model), bf16),
            pltpu.VMEM((4, model, model), bf16),
            pltpu.VMEM((model, model), bf16),
            tall,
            tall,
            tall,
            sems((3, 6)),
            sems((4,)),
            sems((16,)),
            sems((4,)),
        ],
        after=0,
        estimate=cost(27 * unit, 40e6, total * hidden),
        operands=[h1, flat2, cotangent, gains, *outs.pieces(), *wide.pieces(), *narrow.pieces()],
    )
    pieces["W1"].ready(keep_w, send_w)
    pieces["W2"].ready(keep_n, send_n)
    got = {}

    def cross_back():
        got["gq2"], got["gkv"] = steps.call(
            cross_back_kernel,
            [shape(by_slots, bf16), both],
            [slot_rows, slot_rows, slot_rows, lse_spec, enc_wide],
            [slot_rows, enc_wide],
            [],
            after=0,
            estimate=cost(5 * attend_unit, 8 * memory.size, slots * H * length * enc),
            operands=[q2.reshape(by_slots), ga2.reshape(by_slots), a2, lse2, keys_values],
            grid=(slots,),
        )

    def self_back():
        got["tokens"], got["gain"], got["scores"], keep, send, keep_s, send_s = steps.call(
            self_back_kernel,
            [wide_f32, gain_shape, shape((QUADS, length, stacked), f32), one, one, half, half],
            [VMEM] * 13 + [ANY] * 14,
            [VMEM] * 3 + [ANY] * 4,
            [
                pltpu.VMEM((2, model, model), bf16),
                pltpu.VMEM((3, model, model), bf16),
                pltpu.VMEM((5, model, model), bf16),
                slim,
                slim,
                slim,
                slim,
                sems((2, 6)),
                sems((5, 4)),
            ],
            cost(10 * unit + attend_unit, 40 * total * model, slots * H * length * length),
            [
                *(got["gq2"].reshape(total, model), normed2, h1, g2, a1, q1, k1, v1, lse1, normed1, flat),
                *(gains, bias, keep_o, send_o, *outs.pieces(), *qkv.pieces()),
            ],
            aliases={13: 3, 14: 4},
            after=0,
        )
        pieces["S1"].ready(keep, send)
        pieces["S2"].ready(keep_s, send_s)

    def memory_weights():
        keep, send = steps.call(
            memory_weight_kernel,
            [shape((2, 2 * rows + TINY, model), bf16)] * 2,
            [
                enc_rows,
                enc_wide,
                pl.BlockSpec((8, model), lambda *_: (0, 0)),
                pl.BlockSpec((8, model), lambda *_: (0, 0)),
                pl.BlockSpec((QUADS, length, stacked), lambda *_: (0, 0, 0)),
            ],
            [ANY, ANY],
            [
                pltpu.VMEM((model, 2 * model), f32),
                pltpu.VMEM((2, model, model), bf16),
                pltpu.VMEM((TINY, model), bf16),
                sems((3, 4)),
            ],
            cost(2 * enc_unit, 6 * memory.size),
            [memory, got["gkv"], got["gain"], gain_three, got["scores"]],
            grid=(slots,),
            after=0,
        )
        pieces["M"].ready(keep, send)

    def memory_back():
        (got["memory"],) = steps.call(
            memory_grad_kernel,
            [shape(memory.shape, f32)],
            [enc_wide] + [ANY] * 6,
            [by_slot(enc, model)],
            beside,
            cost(2 * enc_unit, 8 * memory.size),
            [got["gkv"], *kv.pieces()],
            grid=(slots,),
            after=0,
        )

    kernels = {"KE": cross_back, "KF": self_back, "KW": memory_weights, "KG": memory_back}
    for group in ORDER:
        if group in kernels:
            kernels[group]()
            steps.fresh = True
        elif group == "|":
            steps.fresh = True
        elif group == "!":
            steps.fresh = False
            waiting, steps.pending = steps.pending, []
            sends = steps.gate(*(piece.send for piece in waiting))
            for piece, send in zip(waiting, sends):
                piece.got = flip(send, "fsdp", 1)
        else:
            members = [step.split(".") for step in group]
            if steps.fresh:
                used = list(dict.fromkeys(name for name, _ in members))
                for name, value in zip(used, steps.gate(*(pieces[name].keep for name in used))):
                    pieces[name].keep = value
                steps.fresh = False
            for name, stage in members:
                getattr(pieces[name], stage)()

    sum_co, sum_cq, sum_so, sum_sq = pieces["S1"].result
    sum_sk, sum_sv = pieces["S2"].result
    sum_ck, sum_cv, tiny = pieces["M"].result
    ours = lax.dynamic_slice_in_dim(tiny[0:3], shard * rows, rows, 1)
    ours_table = lax.dynamic_slice_in_dim(tiny[8 : 8 + BUCKETS, :H], shard * rel_bias.shape[0], rel_bias.shape[0], 0)
    return (
        output.reshape(tokens.shape),
        got["tokens"].reshape(tokens.shape),
        got["memory"],
        ours[0],
        sum_sq,
        sum_sk,
        sum_sv,
        sum_so,
        ours_table,
        ours[1],
        sum_cq,
        sum_ck,
        sum_cv,
        sum_co,
        ours[2],
        pieces["W1"].result[0],
        pieces["W2"].result[0],
    )


def solution(mesh):
    in_specs = (
        P(("dp", "fsdp"), None, None),
        P(("dp", "fsdp"), None, None),
        P(("dp", "fsdp")),
        P(("dp", "fsdp")),
        P(("dp", "fsdp")),
        P("fsdp"),
        P("fsdp", None),
        P("fsdp", None),
        P("fsdp", None),
        P("fsdp", None),
        P("fsdp", None),
        P("fsdp"),
        P("fsdp", None),
        P("fsdp", None),
        P("fsdp", None),
        P("fsdp", None),
        P("fsdp"),
        P("fsdp", None),
        P("fsdp", None),
        P(("dp", "fsdp"), None, None),
    )
    out_specs = (
        P(("dp", "fsdp"), None, None),
        P(("dp", "fsdp"), None, None),
        P(("dp", "fsdp"), None, None),
        P("fsdp"),
        P("fsdp", None),
        P("fsdp", None),
        P("fsdp", None),
        P("fsdp", None),
        P("fsdp", None),
        P("fsdp"),
        P("fsdp", None),
        P("fsdp", None),
        P("fsdp", None),
        P("fsdp", None),
        P("fsdp"),
        P("fsdp", None),
        P("fsdp", None),
    )
    return jax.shard_map(
        on_device, mesh=mesh, in_specs=in_specs, out_specs=out_specs, check_vma=False
    )
```

```python
import functools
import math

import jax
import jax.numpy as jnp
from jax import lax
from jax.experimental import pallas as pl
from jax.experimental.pallas import tpu as pltpu
from jax.sharding import PartitionSpec as P

H = 12
DH = 64
QUAD = 4
QUADS = H // QUAD
WIDE = QUAD * DH
CHUNK = 256
MASKED = -1000000000.0
WAY_X, WAY_Z, PLACE = 1, 3, 16
BUCKETS = 32
TINY = 64

bucket_edges = [math.ceil(16 * 8 ** (exponent / 16)) for exponent in range(1, 16)]
f32 = jnp.float32
bf16 = jnp.bfloat16


def flip(values, axis, bit):
    size = lax.axis_size(axis)
    return lax.ppermute(values, axis, [(i, i ^ bit) for i in range(size)])


def pick(values, index):
    return lax.dynamic_index_in_dim(values, index, 0, keepdims=False)


def add_low(left, right):
    return (left.astype(f32) + right.astype(f32)).astype(bf16)


def mm(left, right):
    return jnp.dot(left, right, preferred_element_type=f32)


def mm_nt(left, right):
    return lax.dot_general(left, right, (((1,), (1,)), ((), ())), preferred_element_type=f32)


def mm_tn(left, right):
    return lax.dot_general(left, right, (((0,), (0,)), ((), ())), preferred_element_type=f32)


def piece_starts(meta, pieces, way):
    shard, side = meta[0], meta[way]
    rows = pieces[0].shape[1]
    half = rows // 2
    return (
        shard * rows,
        (shard ^ 1) * rows,
        (shard ^ 2) * rows + side * half,
        (shard ^ 2) * rows + (1 - side) * half,
        (shard ^ 3) * rows + side * half,
        (shard ^ 3) * rows + (1 - side) * half,
    )


def copies_in(meta, pieces, whole, sems, way, only=slice(None), cols=slice(None)):
    return [
        pltpu.make_async_copy(
            piece.at[only, :, cols],
            whole.at[:, pl.ds(pl.multiple_of(start, 32), piece.shape[1])],
            sems.at[i],
        )
        for i, (piece, start) in enumerate(zip(pieces, piece_starts(meta, pieces, way)))
    ]


def start_all(copies):
    for copy in copies:
        copy.start()


def wait_all(copies):
    for copy in copies:
        copy.wait()


def copies_out(meta, whole, keep, send, at, sems):
    shard = meta[0]
    rows = whole.shape[0] // 4
    return [
        pltpu.make_async_copy(
            whole.at[pl.ds(pl.multiple_of((shard ^ j) * rows, 32), rows)],
            (send if j % 2 else keep).at[j // 2, pl.ds(at * rows, rows)],
            sems.at[j],
        )
        for j in range(4)
    ]


def norm_rho(hidden):
    return lax.rsqrt(jnp.mean(hidden * hidden, axis=-1, keepdims=True) + 1e-06)


def norm_back(hidden, gain, upstream):
    rho = norm_rho(hidden)
    scaled = upstream * gain
    inner = jnp.mean(scaled * hidden, axis=-1, keepdims=True)
    grad = rho * scaled - hidden * (rho * rho * rho * inner)
    return grad, jnp.sum(upstream * hidden * rho, axis=0, keepdims=True)


def head_masks():
    lane = lax.broadcasted_iota(jnp.int32, (1, WIDE), 1) // DH
    return [(lane == h).astype(f32).astype(bf16) for h in range(QUAD)]


def stack_heads(values, masks):
    return jnp.concatenate([values * mask for mask in masks], axis=0)


def own_heads(mixed):
    rows = mixed.shape[1] // QUAD
    own = [mixed[h * DH : (h + 1) * DH, h * rows : (h + 1) * rows] for h in range(QUAD)]
    return jnp.concatenate(own, axis=0).T


def head_sums(product):
    high = product.astype(bf16)
    low = (product - high.astype(f32)).astype(bf16)
    ones = jnp.ones((8, WIDE), bf16)
    return (mm_nt(ones, high) + mm_nt(ones, low))[0:1]


def fold(values, op):
    return op(values.reshape(values.shape[0] // 8, 8, values.shape[1]), axis=0)


def quad_at(quad):
    return pl.ds(quad * WIDE, WIDE)


def copies_beside(meta, pieces, whole, sems, way):
    columns = pieces[0].shape[2]
    starts = piece_starts(meta, pieces, way)
    return [
        pltpu.make_async_copy(
            piece.at[j],
            whole.at[pl.ds(pl.multiple_of(start, 32), piece.shape[1]), pl.ds(j * columns, columns)],
            sems.at[j, i],
        )
        for j in range(2)
        for i, (piece, start) in enumerate(zip(pieces, starts))
    ]


def each_count(meta, slot, most, body):
    for n in range(1, most // CHUNK + 1):
        pl.when(meta[12 + slot] == n)(functools.partial(body, n * CHUNK))


def memory_kernel(meta, memory, *refs):
    pieces, (out, whole, sems) = refs[:6], refs[6:]
    slot = pl.program_id(0)

    @pl.when(slot == 0)
    def _():
        copies = copies_beside(meta, pieces, whole, sems, WAY_X)
        start_all(copies)
        wait_all(copies)

    def project(rows):
        out[0, :rows, :] = mm(memory[0, :rows, :], whole[...]).astype(bf16)

    each_count(meta, slot, memory.shape[1], project)


def buckets_of(length):
    key_at = lax.broadcasted_iota(jnp.int32, (length, length), 0)
    distance = jnp.maximum(lax.broadcasted_iota(jnp.int32, (length, length), 1) - key_at, 0)
    bucket = jnp.minimum(distance, 16)
    for edge in bucket_edges:
        bucket = bucket + (distance >= edge).astype(jnp.int32)
    return bucket


def self_kernel(meta, tokens, gains, table, *refs):
    pieces = refs[:6]
    bias, normed_out, q_out, k_out, v_out, mixed_out, lse_out, whole, sems = refs[6:]
    copies = copies_in(meta, pieces, whole, sems, WAY_Z)
    start_all(copies)
    hidden = tokens[...].astype(f32)
    normed = (hidden * norm_rho(hidden) * gains[0:1]).astype(bf16)
    normed_out[...] = normed
    length = bias.shape[1]
    bucket = buckets_of(length)
    for head in range(H):
        block = jnp.zeros((length, length), f32)
        for n in range(BUCKETS):
            block = jnp.where(bucket == n, table[n, head], block)
        at = head % QUAD * length
        bias[head // QUAD, :, at : at + length] = block
    wait_all(copies)
    q_out[...] = mm(normed, whole[0]).astype(bf16)
    k_out[...] = mm(normed, whole[1]).astype(bf16)
    v_out[...] = mm(normed, whole[2]).astype(bf16)
    length = bias.shape[1]
    masks = head_masks()
    key_at = lax.broadcasted_iota(jnp.int32, (length, QUAD * length), 0)
    query_at = lax.broadcasted_iota(jnp.int32, (length, QUAD * length), 1) % length
    for b in range(lse_out.shape[0]):
        rows = slice(b * length, (b + 1) * length)
        ok = (key_at <= query_at) & (key_at < meta[4 + b])
        for quad in range(QUADS):
            at = slice(quad * WIDE, (quad + 1) * WIDE)
            scores = mm_nt(k_out[rows, at], stack_heads(q_out[rows, at], masks)) + bias[quad]
            scores = jnp.where(ok, scores, MASKED)
            top = jnp.max(scores, axis=0, keepdims=True)
            raised = jnp.exp(scores - top)
            total = jnp.sum(raised, axis=0, keepdims=True)
            weights = (raised * (1.0 / total)).astype(bf16)
            mixed_out[rows, at] = own_heads(mm(v_out[rows, at].T, weights)).astype(bf16)
            lse_out[b, quad : quad + 1, :] = top + jnp.log(total)


def query_kernel(meta, tokens, mixed, gains, *refs):
    pieces, (h1_out, normed2_out, q2_out, whole, sems) = refs[:6], refs[6:]
    copies = copies_in(meta, pieces, whole, sems, WAY_X, pl.ds(0, 2))
    start_all(copies)
    wait_all(copies)
    first = tokens[...].astype(f32) + mm(mixed[...], whole[0])
    h1_out[...] = first
    normed2 = (first * norm_rho(first) * gains[1:2]).astype(bf16)
    normed2_out[...] = normed2
    q2_out[...] = mm(normed2, whole[1]).astype(bf16)


def cross_kernel(meta, queries, memory, mixed_out, lse_out):
    slot = pl.program_id(0)
    model = queries.shape[2]

    @pl.when(meta[12 + slot] == 0)
    def _():
        mixed_out[...] = jnp.zeros(mixed_out.shape, bf16)
        lse_out[...] = jnp.zeros(lse_out.shape, f32)

    def attend(rows):
        masks = head_masks()
        ok = lax.broadcasted_iota(jnp.int32, (rows, 1), 0) < meta[8 + slot]
        for quad in range(QUADS):
            at, at_v = slice(quad * WIDE, (quad + 1) * WIDE), slice(model + quad * WIDE, model + (quad + 1) * WIDE)
            stacked = stack_heads(queries[0, :, at], masks)
            scores = jnp.where(ok, mm_nt(memory[0, :rows, at], stacked), MASKED)
            top = jnp.max(scores, axis=0, keepdims=True)
            raised = jnp.exp(scores - top)
            total = jnp.sum(raised, axis=0, keepdims=True)
            mixed = mm(memory[0, :rows, at_v].T, raised.astype(bf16))
            mixed_out[0, :, at] = own_heads(mixed * (1.0 / total)).astype(bf16)
            lse_out[0, quad : quad + 1, :] = top + jnp.log(total)

    each_count(meta, slot, memory.shape[1], attend)


def gelu_both(values):
    scale = math.sqrt(2.0 / math.pi)
    square = values * values
    slope = jnp.tanh(scale * values * (1.0 + 0.044715 * square))
    half = 0.5 * (1.0 + slope)
    back = half + 0.5 * values * (1.0 - slope * slope) * (scale * (1.0 + 3 * 0.044715 * square))
    return values * half, back


def live_rows(meta, slots, length):
    positions = lax.broadcasted_iota(jnp.int32, (length, 1), 0)
    return jnp.concatenate(
        [((positions < meta[4 + b]) & (b < meta[2])).astype(f32) for b in range(slots)], axis=0
    )


def ff_kernel(meta, h1, mixed, cotangent, gains, *refs):
    square, wide, narrow, refs = refs[:6], refs[6:12], refs[12:18], refs[18:]
    (output, g2_out, ga2_out, gain_out, keep_n, send_n, keep_w, send_w, keep_o, send_o), refs = refs[:10], refs[10:]
    co, w_in, w_out, gf, normed, grad_n, grad_w, grad_o, second, third, back, in_sems, n_sems, w_sems, o_sems = refs
    model = h1.shape[1]
    rows = model // 4
    shard = meta[0]
    co_in = copies_in(meta, square, co, in_sems.at[0], WAY_X, pl.ds(2, 1))
    in_in = copies_in(meta, wide, w_in, in_sems.at[1], WAY_Z)
    out_in = copies_in(meta, narrow, w_out, in_sems.at[2], WAY_X)
    start_all(co_in)
    start_all(in_in)
    start_all(out_in)
    live = live_rows(meta, cotangent.shape[0], cotangent.shape[1])
    gf[...] = (cotangent[...].reshape(h1.shape).astype(f32) * live).astype(bf16)
    wait_all(co_in)
    second[...] = h1[...] + mm(mixed[...], co[0])
    hidden = second[...]
    normed[...] = (hidden * norm_rho(hidden) * gains[2:3]).astype(bf16)
    normed_t = normed[...].T
    wait_all(in_in)
    waits = []
    for j in range(4):
        cols = pl.ds(pl.multiple_of((shard ^ j) * model, model), model)
        units, slope = gelu_both(mm(normed[...], w_in[0, :, cols]))
        low = units.astype(bf16)
        if j == 0:
            wait_all(out_in)
        wide_out = mm(low, w_out[0, cols, :])
        grad_n[j] = mm_tn(low, gf[...]).astype(bf16)
        waits.append(pltpu.make_async_copy(grad_n.at[j], (send_n if j % 2 else keep_n).at[j // 2], n_sems.at[j]))
        waits[-1].start()
        grad_units = (mm_nt(gf[...], w_out[0, cols, :]) * slope).astype(bf16)
        grad_w[j] = mm(normed_t, grad_units).astype(bf16)
        at = pl.ds(pl.multiple_of((shard ^ j) * rows, 32), rows)
        for i in range(4):
            waits.append(
                pltpu.make_async_copy(
                    grad_w.at[j, pl.ds(pl.multiple_of((shard ^ i) * rows, 32), rows)],
                    (send_w if i % 2 else keep_w).at[i // 2, at],
                    w_sems.at[4 * j + i],
                )
            )
            waits[-1].start()
        grad_normed = mm_nt(grad_units, w_in[0, :, cols])
        if j == 0:
            third[...] = second[...] + wide_out
            back[...] = grad_normed
        else:
            third[...] += wide_out
            back[...] += grad_normed
    output[...] = (third[...] * live).astype(bf16)
    grad, gain = norm_back(second[...], gains[2:3], back[...])
    gain_out[...] = jnp.broadcast_to(gain, gain_out.shape)
    g2 = gf[...].astype(f32) + grad
    g2_out[...] = g2
    go2 = g2.astype(bf16)
    ga2_out[...] = mm_nt(go2, co[0]).astype(bf16)
    grad_o[...] = mm_tn(mixed[...], go2).astype(bf16)
    out = copies_out(meta, grad_o, keep_o, send_o, 0, o_sems)
    start_all(out)
    wait_all(waits)
    wait_all(out)


def cross_back_kernel(meta, queries, grads, mixed, lse, memory, gq_out, out):
    slot = pl.program_id(0)
    model = queries.shape[2]

    @pl.when(meta[12 + slot] == 0)
    def _():
        gq_out[...] = jnp.zeros(gq_out.shape, bf16)

    def attend(rows):
        masks = head_masks()
        ok = lax.broadcasted_iota(jnp.int32, (rows, 1), 0) < meta[8 + slot]
        for quad in range(QUADS):
            at, at_v = slice(quad * WIDE, (quad + 1) * WIDE), slice(model + quad * WIDE, model + (quad + 1) * WIDE)
            q_stack = stack_heads(queries[0, :, at], masks)
            g_stack = stack_heads(grads[0, :, at], masks)
            tiled = jnp.concatenate([mixed[0, :, at].astype(f32)] * QUAD, axis=0)
            delta = head_sums(g_stack.astype(f32) * tiled)
            block = memory[0, :rows, at]
            scores = jnp.where(ok, mm_nt(block, q_stack), MASKED)
            share = jnp.exp(scores - lse[0, quad : quad + 1, :])
            grad_share = mm_nt(memory[0, :rows, at_v], g_stack)
            grad_scores = (share * (grad_share - delta)).astype(bf16)
            out[0, :rows, at_v] = mm(share.astype(bf16), g_stack).astype(bf16)
            out[0, :rows, at] = mm(grad_scores, q_stack).astype(bf16)
            gq_out[0, :, at] = own_heads(mm(block.T, grad_scores)).astype(bf16)

    each_count(meta, slot, memory.shape[1], attend)


def table_grad(scores):
    length = scores.shape[1]
    bucket = jnp.concatenate([buckets_of(length)] * QUAD, axis=1)
    head = lax.broadcasted_iota(jnp.int32, (QUAD * length, 128), 0) // length
    column = lax.broadcasted_iota(jnp.int32, (QUAD * length, 128), 1)
    table = jnp.zeros((BUCKETS, 128), f32)
    for quad in range(QUADS):
        values = scores[quad]
        sums = [jnp.sum(jnp.where(bucket == n, values, 0.0), axis=0, keepdims=True) for n in range(BUCKETS)]
        sums = jnp.concatenate(sums, axis=0)
        high = sums.astype(bf16)
        low = (sums - high.astype(f32)).astype(bf16)
        to_head = (column == head + quad * QUAD).astype(f32).astype(bf16)
        table = table + mm(high, to_head) + mm(low, to_head)
    return table


def self_back_kernel(
    meta, gq2, normed2, h1, g2, mixed, q, k, v, lse, normed, tokens, gains, bias, keep_in, send_in, *refs
):
    query, pieces, refs = refs[:6], refs[6:12], refs[12:]
    (grad_out, gain_out, bias_out, keep, send, keep_s, send_s), refs = refs[:7], refs[7:]
    square, whole, grads, ga1, gq, gk, gv, in_sems, sems = refs
    copies_q = copies_in(meta, query, square, in_sems.at[0], WAY_X, pl.ds(0, 2))
    copies = copies_in(meta, pieces, whole, in_sems.at[1], WAY_Z)
    start_all(copies_q)
    start_all(copies)
    outs = []

    def emit(index, value, *place):
        grads[index] = value.astype(bf16)
        outs.extend(copies_out(meta, grads.at[index], *place, sems.at[index]))
        start_all(outs[-4:])

    emit(0, mm_tn(normed2[...], gq2[...]), keep, send, 1)
    wait_all(copies_q)
    grad, gain_two = norm_back(h1[...], gains[1:2], mm_nt(gq2[...], square[1]))
    g1 = g2[...] + grad
    grad_out[...] = g1
    go1 = g1.astype(bf16)
    emit(1, mm_tn(mixed[...], go1), keep, send, 2)
    ga1[...] = mm_nt(go1, square[0]).astype(bf16)
    length = bias.shape[1]
    masks = head_masks()
    key_at = lax.broadcasted_iota(jnp.int32, (length, QUAD * length), 0)
    query_at = lax.broadcasted_iota(jnp.int32, (length, QUAD * length), 1) % length
    for b in range(lse.shape[0]):
        rows = slice(b * length, (b + 1) * length)
        ok = (key_at <= query_at) & (key_at < meta[4 + b])
        for quad in range(QUADS):
            at = slice(quad * WIDE, (quad + 1) * WIDE)
            q_stack = stack_heads(q[rows, at], masks)
            g_stack = stack_heads(ga1[rows, at], masks)
            tiled = jnp.concatenate([mixed[rows, at].astype(f32)] * QUAD, axis=0)
            delta = head_sums(g_stack.astype(f32) * tiled)
            block = k[rows, at]
            scores = jnp.where(ok, mm_nt(block, q_stack) + bias[quad], MASKED)
            share = jnp.exp(scores - lse[b, quad : quad + 1, :])
            grad_share = mm_nt(v[rows, at], g_stack)
            grad_scores = (share * (grad_share - delta)).astype(bf16)
            gv[rows, at] = mm(share.astype(bf16), g_stack).astype(bf16)
            gk[rows, at] = mm(grad_scores, q_stack).astype(bf16)
            gq[rows, at] = own_heads(mm(block.T, grad_scores)).astype(bf16)
            if b == 0:
                bias_out[quad] = grad_scores.astype(f32)
            else:
                bias_out[quad] += grad_scores.astype(f32)
    normed_t = normed[...].T
    emit(2, mm(normed_t, gq[...]), keep, send, 3)
    emit(3, mm(normed_t, gk[...]), keep_s, send_s, 0)
    emit(4, mm(normed_t, gv[...]), keep_s, send_s, 1)
    wait_all(copies)
    grad_normed = mm_nt(gq[...], whole[0]) + mm_nt(gk[...], whole[1]) + mm_nt(gv[...], whole[2])
    grad, gain_one = norm_back(tokens[...].astype(f32), gains[0:1], grad_normed)
    grad_out[...] += grad
    gain_out[...] = jnp.concatenate([gain_one, gain_two, jnp.zeros((6, gain_one.shape[1]), f32)], axis=0)
    wait_all(outs)


def memory_weight_kernel(meta, memory, grads, gain_low, gain_three, scores, keep, send, total, low, tiny, sems):
    slot = pl.program_id(0)
    model = memory.shape[2]

    @pl.when(slot == 0)
    def _():
        total[...] = jnp.zeros(total.shape, f32)
        top = jnp.concatenate([gain_low[0:2], gain_three[0:1], jnp.zeros((5, model), f32)], axis=0)
        table = jnp.pad(table_grad(scores), ((0, 0), (0, model - 128)))
        rest = jnp.zeros((TINY - 8 - BUCKETS, model), f32)
        tiny[...] = jnp.concatenate([top, table, rest], axis=0).astype(bf16)

    def add(rows):
        total[...] += mm(memory[0, :rows, :].T, grads[0, :rows, :])

    each_count(meta, slot, memory.shape[1], add)

    @pl.when(slot == pl.num_programs(0) - 1)
    def _():
        rows = model // 4
        outs = [
            pltpu.make_async_copy(
                tiny,
                (send if j % 2 else keep).at[j // 2, pl.ds(2 * rows, tiny.shape[0])],
                sems.at[2, j],
            )
            for j in range(4)
        ]
        start_all(outs)
        for i in range(2):
            low[i] = total[:, i * model : (i + 1) * model].astype(bf16)
            outs += copies_out(meta, low.at[i], keep, send, i, sems.at[i])
            start_all(outs[-4:])
        wait_all(outs)


def memory_grad_kernel(meta, grads, *refs):
    pieces, (out, whole, sems) = refs[:6], refs[6:]
    slot = pl.program_id(0)

    @pl.when(slot == 0)
    def _():
        copies = copies_beside(meta, pieces, whole, sems, WAY_X)
        start_all(copies)
        wait_all(copies)

    def fill(rows):
        if rows:
            out[0, :rows, :] = mm_nt(grads[0, :rows, :], whole[...])
        if rows < out.shape[1]:
            out[0, rows:, :] = jnp.zeros((out.shape[1] - rows, out.shape[2]), f32)

    pl.when(meta[12 + slot] == 0)(functools.partial(fill, 0))
    each_count(meta, slot, out.shape[1], fill)


VMEM = pl.BlockSpec(memory_space=pltpu.VMEM)
ANY = pl.BlockSpec(memory_space=pl.ANY)


def cost(flops, moved, raised=0):
    del flops, moved, raised
    return pl.CostEstimate(flops=1024, bytes_accessed=1024, transcendentals=0)


def shape(dims, dtype):
    return jax.ShapeDtypeStruct(tuple(dims), dtype)


def live_slot(b, meta):
    return jnp.where(meta[12 + b] > 0, b, jnp.maximum(meta[2] - 1, 0))


def by_slot(rows, model, held=False):
    if held:
        return pl.BlockSpec((1, rows, model), lambda b, meta: (live_slot(b, meta), 0, 0))
    return pl.BlockSpec((1, rows, model), lambda b, meta: (b, 0, 0))


class Steps:
    def __init__(self, meta):
        self.meta = meta
        self.token = meta
        self.marks = []
        self.last = None
        self.pending = []
        self.fresh = False

    def call(self, kernel, outs, in_specs, out_specs, scratch, estimate, operands, grid=(), aliases=None, after=None):
        count = len(outs)
        order = [self.token]
        if self.marks:
            order.extend(self.marks)
        first = 1 + len(order)

        def body(meta, *refs):
            refs = refs[len(order) :]
            ins, rest = refs[: len(operands)], refs[len(operands) :]
            kernel(meta, *ins, *rest[:count], *rest[count + 1 :])

        result = pl.pallas_call(
            body,
            out_shape=tuple(outs) + (shape((16, 128), f32),),
            grid_spec=pltpu.PrefetchScalarGridSpec(
                num_scalar_prefetch=1,
                grid=grid,
                in_specs=[ANY] * len(order) + list(in_specs),
                out_specs=tuple(out_specs) + (ANY,),
                scratch_shapes=scratch,
            ),
            input_output_aliases={first + i: o for i, o in (aliases or {}).items()},
            compiler_params=pltpu.CompilerParams(vmem_limit_bytes=56 * 1024 * 1024),
            cost_estimate=estimate,
        )(self.meta, *order, *operands)
        self.token, self.marks = result[-1], []
        return result[:-1]

    def mark(self, result):
        self.marks.append(result)

    def gate(self, *values):
        outs = self.call(
            lambda *refs: None,
            [shape(v.shape, v.dtype) for v in values],
            [ANY] * len(values),
            [ANY] * len(values),
            [],
            cost(0, 0),
            values,
            aliases={i: i for i in range(len(values))},
        )
        return outs


class Bundle:
    def __init__(self, own, place, bit):
        rows = own.shape[1] // 2
        self.own, self.bit = own, bit
        self.half = lax.dynamic_slice_in_dim(own, (place // bit) % 2 * rows, rows, 1)

    def send(self):
        self.direct = flip(self.half, "fsdp", 2)
        self.beside = flip(self.own, "fsdp", 1)

    def hand_on(self):
        self.passed = flip(self.direct, "dp", self.bit)
        self.direct_beside = flip(self.direct, "fsdp", 1)

    def end(self):
        self.passed_beside = flip(self.passed, "fsdp", 1)

    def pieces(self):
        return (self.own, self.beside, self.direct, self.passed, self.direct_beside, self.passed_beside)


class Piece:
    def __init__(self, steps, place, outs, blocks, tall=True):
        self.steps, self.outs, self.blocks = steps, outs, blocks
        self.place, self.tall = place, tall and lax.axis_size("dp") > 2

    def ready(self, keep, send):
        self.keep, self.send = keep, send
        self.steps.pending.append(self)

    def add(self, left, right):
        return (left.astype(f32) + right.astype(f32)).astype(bf16)

    def cut(self, which, axis):
        half = self.keep.shape[axis] // 2
        return [lax.dynamic_slice_in_dim(v, which * half, half, axis) for v in (self.keep, self.got)]

    def core(self):
        far = self.add(self.keep[1], self.got[1])
        self.keep, self.got = self.add(self.keep[0], self.got[0]), flip(far, "fsdp", 2)
        self.steps.mark(far)

    def halve(self, bit, axis):
        side = self.place // bit % 2
        send = self.add(*self.cut(1 - side, axis))
        self.keep, self.got = self.add(*self.cut(side, axis)), flip(send, "dp", bit)
        self.steps.mark(send)

    def y(self):
        self.halve(1, 1)

    def x(self):
        if self.tall:
            self.halve(2, 0)
        else:
            self.pass_on(2)

    def pass_on(self, bit):
        self.keep = self.add(self.keep, self.got)
        self.got = flip(self.keep, "dp", bit)
        self.steps.mark(self.keep)

    def z(self):
        bit = 4
        while bit < lax.axis_size("dp"):
            self.pass_on(bit)
            bit *= 2

    def w(self):
        self.pass_on(2 if self.tall else 1)

    def joined(self, axis, bit, dtype, rows=slice(None)):
        mine, other = self.keep[rows].astype(dtype), self.got[rows].astype(dtype)
        low = self.place // bit % 2 == 0
        return jnp.concatenate([jnp.where(low, mine, other), jnp.where(low, other, mine)], axis=axis)

    def v(self):
        self.keep = self.joined(0, 2, bf16)
        self.got = flip(self.keep, "dp", 1)
        self.steps.mark(self.keep)

    def end(self):
        at = 0
        parts = {}
        for which, _ in self.blocks:
            rows = self.outs[which][0]
            parts.setdefault(which, []).append(self.joined(1, 1, f32, slice(at, at + rows)))
            at += rows
        self.result = [jnp.concatenate(parts[which], axis=1) for which in range(len(self.outs))]
        self.steps.mark(self.result[0])


ORDER = (
    "!",
    ("W1.core",),
    ("W2.core",),
    "KE",
    ("W1.y",),
    "KF",
    ("W2.y", "W1.x"),
    "!",
    ("S1.core", "S2.core"),
    "KW",
    ("S1.y", "W2.x", "W1.z"),
    "!",
    ("M.core",),
    "KG",
    ("S1.x", "W2.z", "W1.w", "S2.y"),
    ("M.y",),
    "|",
    ("W2.w", "S2.x", "S1.z", "W1.v"),
    "|",
    ("M.x",),
    "|",
    ("S2.z", "S1.w"),
    ("W2.v",),
    ("M.z",),
    "|",
    ("S1.v", "S2.w", "M.w"),
    ("S2.v",),
    ("M.v",),
    ("W1.end", "W2.end", "S1.end", "S2.end", "M.end"),
)


def on_device(
    tokens,
    memory,
    tgt_len,
    enc_len,
    ex_count,
    self_gain,
    self_q,
    self_k,
    self_v,
    self_out,
    rel_bias,
    cross_gain,
    cross_q,
    cross_k,
    cross_v,
    cross_out,
    ff_gain,
    ff_in,
    ff_out,
    cotangent,
):
    slots, length, model = tokens.shape
    enc = memory.shape[1]
    hidden = ff_in.shape[1]
    rows = self_q.shape[0]
    total = slots * length
    shard = lax.axis_index("fsdp")
    place = lax.axis_index("dp")
    live = jnp.arange(slots, dtype=jnp.int32) < ex_count[0]
    chunks = jnp.where(live, (enc_len + CHUNK - 1) // CHUNK, 0)
    first = jnp.stack([shard, place % 2, ex_count[0], place // 2 % 2])
    meta = jnp.concatenate([first, tgt_len, enc_len, chunks, place[None]])
    steps = Steps(meta)

    kv = Bundle(jnp.stack([cross_k, cross_v]), place, 1)
    qkv = Bundle(jnp.stack([self_q, self_k, self_v]), place, 2)
    outs = Bundle(jnp.stack([self_out, cross_q, cross_out]), place, 1)
    wide = Bundle(ff_in[None], place, 2)
    narrow = Bundle(ff_out[None], place, 1)
    packed = jnp.concatenate([self_gain, cross_gain, ff_gain, rel_bias.reshape(-1)])
    packed = jnp.pad(packed, (0, model - packed.shape[0]))[None]
    kv.send()
    qkv.send()
    kv.direct, outs.half, packed, far = steps.gate(kv.direct, outs.half, packed, flip(packed, "fsdp", 2))
    kv.hand_on()
    outs.send()
    pair = jnp.concatenate([packed, far], axis=0)
    beside = flip(pair, "fsdp", 1)
    kv.passed, qkv.direct, wide.half, narrow.half, beside = steps.gate(
        kv.passed, qkv.direct, wide.half, narrow.half, beside
    )
    near = jnp.stack([pair[0:1], beside[0:1], pair[1:2], beside[1:2]])
    kv.end()
    qkv.hand_on()
    wide.send()
    narrow.send()
    small = jnp.concatenate([pick(near, shard ^ j) for j in range(4)], axis=0)
    gains = small[:, : 3 * rows].reshape(4, 3, rows).transpose(1, 0, 2).reshape(3, model).astype(f32)
    gains = jnp.pad(gains, ((0, 5), (0, 0)))
    table = small[:, 3 * rows : 3 * rows + rel_bias.size].reshape(-1, H).astype(f32)
    kv.passed_beside, gains, table = steps.gate(kv.passed_beside, gains, table)
    stacked = QUAD * length
    slot_rows = by_slot(length, model)
    enc_rows = by_slot(enc, model, held=True)
    unit = 2 * total * model * model
    enc_unit = 2 * slots * enc * model * model
    attend_unit = 2 * slots * enc * length * model * QUAD
    flat = tokens.reshape(total, model)
    by_slots = (slots, length, model)
    low = shape((total, model), bf16)
    wide_f32 = shape((total, model), f32)
    lse_spec = by_slot(8, stacked)
    gain_shape = shape((8, model), f32)
    sems = pltpu.SemaphoreType.DMA

    enc_wide = by_slot(enc, 2 * model, held=True)
    both = shape((slots, enc, 2 * model), bf16)
    beside = [pltpu.VMEM((model, 2 * model), bf16), sems((2, 6))]
    (keys_values,) = steps.call(
        memory_kernel,
        [both],
        [enc_rows] + [ANY] * 6,
        [enc_wide],
        beside,
        cost(2 * enc_unit, 6 * memory.size),
        [memory, *kv.pieces()],
        grid=(slots,),
    )
    qkv.passed, outs.direct = steps.gate(qkv.passed, outs.direct)
    outs.hand_on()
    qkv.end()
    bias, normed1, q1, k1, v1, a1, lse1 = steps.call(
        self_kernel,
        [shape((QUADS, length, stacked), f32), low, low, low, low, low, shape((slots, 8, stacked), f32)],
        [VMEM] * 2 + [pl.BlockSpec(memory_space=pltpu.SMEM)] + [ANY] * 6,
        [VMEM] * 7,
        [pltpu.VMEM((3, model, model), bf16), sems((6,))],
        cost(3 * unit + attend_unit / 4, 12 * total * model, slots * H * length * length),
        [flat, gains, table, *qkv.pieces()],
    )
    outs.passed, wide.direct = steps.gate(outs.passed, wide.direct)
    outs.end()
    wide.hand_on()
    h1, normed2, q2 = steps.call(
        query_kernel,
        [wide_f32, low, low],
        [VMEM] * 3 + [ANY] * 6,
        [VMEM] * 3,
        [pltpu.VMEM((2, model, model), bf16), sems((6,))],
        cost(2 * unit, 12 * total * model),
        [flat, a1, gains, *outs.pieces()],
    )
    (narrow.direct,) = steps.gate(narrow.direct)
    narrow.hand_on()
    a2, lse2 = steps.call(
        cross_kernel,
        [shape(by_slots, bf16), shape((slots, 8, stacked), f32)],
        [slot_rows, enc_wide],
        [slot_rows, lse_spec],
        [],
        cost(2 * attend_unit, 4 * memory.size, slots * H * length * enc),
        [q2.reshape(by_slots), keys_values],
        grid=(slots,),
    )
    wide.passed, narrow.passed = steps.gate(wide.passed, narrow.passed)
    wide.end()
    narrow.end()
    flat2 = a2.reshape(total, model)

    pair = [(rows, model)] * 2
    order = [(0, 0), (1, 0)]
    pieces = {
        "W1": Piece(steps, place, [(rows, hidden)], [(0, c * model) for c in range(4)]),
        "W2": Piece(steps, place, [(hidden // 4, model)], [(0, 0)]),
        "S1": Piece(steps, place, [(rows, model)] * 4, [(i, 0) for i in range(4)]),
        "S2": Piece(steps, place, pair, order),
        "M": Piece(steps, place, pair + [(TINY, model)], order + [(2, 0)]),
    }
    one = shape((2, 4 * rows, model), bf16)
    half = shape((2, 2 * rows, model), bf16)
    tall = pltpu.VMEM((total, model), f32)
    slim = pltpu.VMEM((total, model), bf16)
    output, g2, ga2, gain_three, keep_n, send_n, keep_w, send_w, keep_o, send_o = steps.call(
        ff_kernel,
        [low, wide_f32, low, gain_shape, one, one, one, one, one, one],
        [VMEM] * 4 + [ANY] * 18,
        [VMEM] * 4 + [ANY] * 6,
        [
            pltpu.VMEM((1, model, model), bf16),
            pltpu.VMEM((1, model, hidden), bf16),
            pltpu.VMEM((1, hidden, model), bf16),
            slim,
            slim,
            pltpu.VMEM((4, model, model), bf16),
            pltpu.VMEM((4, model, model), bf16),
            pltpu.VMEM((model, model), bf16),
            tall,
            tall,
            tall,
            sems((3, 6)),
            sems((4,)),
            sems((16,)),
            sems((4,)),
        ],
        after=0,
        estimate=cost(27 * unit, 40e6, total * hidden),
        operands=[h1, flat2, cotangent, gains, *outs.pieces(), *wide.pieces(), *narrow.pieces()],
    )
    pieces["W1"].ready(keep_w, send_w)
    pieces["W2"].ready(keep_n, send_n)
    got = {}

    def cross_back():
        got["gq2"], got["gkv"] = steps.call(
            cross_back_kernel,
            [shape(by_slots, bf16), both],
            [slot_rows, slot_rows, slot_rows, lse_spec, enc_wide],
            [slot_rows, enc_wide],
            [],
            after=0,
            estimate=cost(5 * attend_unit, 8 * memory.size, slots * H * length * enc),
            operands=[q2.reshape(by_slots), ga2.reshape(by_slots), a2, lse2, keys_values],
            grid=(slots,),
        )

    def self_back():
        got["tokens"], got["gain"], got["scores"], keep, send, keep_s, send_s = steps.call(
            self_back_kernel,
            [wide_f32, gain_shape, shape((QUADS, length, stacked), f32), one, one, half, half],
            [VMEM] * 13 + [ANY] * 14,
            [VMEM] * 3 + [ANY] * 4,
            [
                pltpu.VMEM((2, model, model), bf16),
                pltpu.VMEM((3, model, model), bf16),
                pltpu.VMEM((5, model, model), bf16),
                slim,
                slim,
                slim,
                slim,
                sems((2, 6)),
                sems((5, 4)),
            ],
            cost(10 * unit + attend_unit, 40 * total * model, slots * H * length * length),
            [
                *(got["gq2"].reshape(total, model), normed2, h1, g2, a1, q1, k1, v1, lse1, normed1, flat),
                *(gains, bias, keep_o, send_o, *outs.pieces(), *qkv.pieces()),
            ],
            aliases={13: 3, 14: 4},
            after=0,
        )
        pieces["S1"].ready(keep, send)
        pieces["S2"].ready(keep_s, send_s)

    def memory_weights():
        keep, send = steps.call(
            memory_weight_kernel,
            [shape((2, 2 * rows + TINY, model), bf16)] * 2,
            [
                enc_rows,
                enc_wide,
                pl.BlockSpec((8, model), lambda *_: (0, 0)),
                pl.BlockSpec((8, model), lambda *_: (0, 0)),
                pl.BlockSpec((QUADS, length, stacked), lambda *_: (0, 0, 0)),
            ],
            [ANY, ANY],
            [
                pltpu.VMEM((model, 2 * model), f32),
                pltpu.VMEM((2, model, model), bf16),
                pltpu.VMEM((TINY, model), bf16),
                sems((3, 4)),
            ],
            cost(2 * enc_unit, 6 * memory.size),
            [memory, got["gkv"], got["gain"], gain_three, got["scores"]],
            grid=(slots,),
            after=0,
        )
        pieces["M"].ready(keep, send)

    def memory_back():
        (got["memory"],) = steps.call(
            memory_grad_kernel,
            [shape(memory.shape, f32)],
            [enc_wide] + [ANY] * 6,
            [by_slot(enc, model)],
            beside,
            cost(2 * enc_unit, 8 * memory.size),
            [got["gkv"], *kv.pieces()],
            grid=(slots,),
            after=0,
        )

    kernels = {"KE": cross_back, "KF": self_back, "KW": memory_weights, "KG": memory_back}
    for group in ORDER:
        if group in kernels:
            kernels[group]()
            steps.fresh = True
        elif group == "|":
            steps.fresh = True
        elif group == "!":
            steps.fresh = False
            waiting, steps.pending = steps.pending, []
            sends = steps.gate(*(piece.send for piece in waiting))
            for piece, send in zip(waiting, sends):
                piece.got = flip(send, "fsdp", 1)
        else:
            members = [step.split(".") for step in group]
            if steps.fresh:
                used = list(dict.fromkeys(name for name, _ in members))
                for name, value in zip(used, steps.gate(*(pieces[name].keep for name in used))):
                    pieces[name].keep = value
                steps.fresh = False
            for name, stage in members:
                getattr(pieces[name], stage)()

    sum_co, sum_cq, sum_so, sum_sq = pieces["S1"].result
    sum_sk, sum_sv = pieces["S2"].result
    sum_ck, sum_cv, tiny = pieces["M"].result
    ours = lax.dynamic_slice_in_dim(tiny[0:3], shard * rows, rows, 1)
    ours_table = lax.dynamic_slice_in_dim(tiny[8 : 8 + BUCKETS, :H], shard * rel_bias.shape[0], rel_bias.shape[0], 0)
    return (
        output.reshape(tokens.shape),
        got["tokens"].reshape(tokens.shape),
        got["memory"],
        ours[0],
        sum_sq,
        sum_sk,
        sum_sv,
        sum_so,
        ours_table,
        ours[1],
        sum_cq,
        sum_ck,
        sum_cv,
        sum_co,
        ours[2],
        pieces["W1"].result[0],
        pieces["W2"].result[0],
    )


def solution(mesh):
    in_specs = (
        P(("dp", "fsdp"), None, None),
        P(("dp", "fsdp"), None, None),
        P(("dp", "fsdp")),
        P(("dp", "fsdp")),
        P(("dp", "fsdp")),
        P("fsdp"),
        P("fsdp", None),
        P("fsdp", None),
        P("fsdp", None),
        P("fsdp", None),
        P("fsdp", None),
        P("fsdp"),
        P("fsdp", None),
        P("fsdp", None),
        P("fsdp", None),
        P("fsdp", None),
        P("fsdp"),
        P("fsdp", None),
        P("fsdp", None),
        P(("dp", "fsdp"), None, None),
    )
    out_specs = (
        P(("dp", "fsdp"), None, None),
        P(("dp", "fsdp"), None, None),
        P(("dp", "fsdp"), None, None),
        P("fsdp"),
        P("fsdp", None),
        P("fsdp", None),
        P("fsdp", None),
        P("fsdp", None),
        P("fsdp", None),
        P("fsdp"),
        P("fsdp", None),
        P("fsdp", None),
        P("fsdp", None),
        P("fsdp", None),
        P("fsdp"),
        P("fsdp", None),
        P("fsdp", None),
    )
    return jax.shard_map(
        on_device, mesh=mesh, in_specs=in_specs, out_specs=out_specs, check_vma=False
    )
```

```python
import functools
import math

import jax
import jax.numpy as jnp
from jax import lax
from jax.experimental import pallas as pl
from jax.experimental.pallas import tpu as pltpu
from jax.sharding import PartitionSpec as P

H = 12
DH = 64
QUAD = 4
QUADS = H // QUAD
WIDE = QUAD * DH
CHUNK = 256
MASKED = -1000000000.0
WAY_X, WAY_Z, PLACE = 1, 3, 16
BUCKETS = 32
TINY = 64

bucket_edges = [math.ceil(16 * 8 ** (exponent / 16)) for exponent in range(1, 16)]
f32 = jnp.float32
bf16 = jnp.bfloat16


def flip(values, axis, bit):
    size = lax.axis_size(axis)
    return lax.ppermute(values, axis, [(i, i ^ bit) for i in range(size)])


def pick(values, index):
    return lax.dynamic_index_in_dim(values, index, 0, keepdims=False)


def add_low(left, right):
    return (left.astype(f32) + right.astype(f32)).astype(bf16)


def mm(left, right):
    return jnp.dot(left, right, preferred_element_type=f32)


def mm_nt(left, right):
    return lax.dot_general(left, right, (((1,), (1,)), ((), ())), preferred_element_type=f32)


def mm_tn(left, right):
    return lax.dot_general(left, right, (((0,), (0,)), ((), ())), preferred_element_type=f32)


def piece_starts(meta, pieces, way):
    shard, side = meta[0], meta[way]
    rows = pieces[0].shape[1]
    half = rows // 2
    return (
        shard * rows,
        (shard ^ 1) * rows,
        (shard ^ 2) * rows + side * half,
        (shard ^ 2) * rows + (1 - side) * half,
        (shard ^ 3) * rows + side * half,
        (shard ^ 3) * rows + (1 - side) * half,
    )


def copies_in(meta, pieces, whole, sems, way, only=slice(None), cols=slice(None)):
    return [
        pltpu.make_async_copy(
            piece.at[only, :, cols],
            whole.at[:, pl.ds(pl.multiple_of(start, 32), piece.shape[1])],
            sems.at[i],
        )
        for i, (piece, start) in enumerate(zip(pieces, piece_starts(meta, pieces, way)))
    ]


def start_all(copies):
    for copy in copies:
        copy.start()


def wait_all(copies):
    for copy in copies:
        copy.wait()


def copies_out(meta, whole, keep, send, at, sems):
    shard = meta[0]
    rows = whole.shape[0] // 4
    return [
        pltpu.make_async_copy(
            whole.at[pl.ds(pl.multiple_of((shard ^ j) * rows, 32), rows)],
            (send if j % 2 else keep).at[j // 2, pl.ds(at * rows, rows)],
            sems.at[j],
        )
        for j in range(4)
    ]


def norm_rho(hidden):
    return lax.rsqrt(jnp.mean(hidden * hidden, axis=-1, keepdims=True) + 1e-06)


def norm_back(hidden, gain, upstream):
    rho = norm_rho(hidden)
    scaled = upstream * gain
    inner = jnp.mean(scaled * hidden, axis=-1, keepdims=True)
    grad = rho * scaled - hidden * (rho * rho * rho * inner)
    return grad, jnp.sum(upstream * hidden * rho, axis=0, keepdims=True)


def head_masks():
    lane = lax.broadcasted_iota(jnp.int32, (1, WIDE), 1) // DH
    return [(lane == h).astype(f32).astype(bf16) for h in range(QUAD)]


def stack_heads(values, masks):
    return jnp.concatenate([values * mask for mask in masks], axis=0)


def own_heads(mixed):
    rows = mixed.shape[1] // QUAD
    own = [mixed[h * DH : (h + 1) * DH, h * rows : (h + 1) * rows] for h in range(QUAD)]
    return jnp.concatenate(own, axis=0).T


def head_sums(product):
    high = product.astype(bf16)
    low = (product - high.astype(f32)).astype(bf16)
    ones = jnp.ones((8, WIDE), bf16)
    return (mm_nt(ones, high) + mm_nt(ones, low))[0:1]


def fold(values, op):
    return op(values.reshape(values.shape[0] // 8, 8, values.shape[1]), axis=0)


def quad_at(quad):
    return pl.ds(quad * WIDE, WIDE)


def copies_beside(meta, pieces, whole, sems, way):
    columns = pieces[0].shape[2]
    starts = piece_starts(meta, pieces, way)
    return [
        pltpu.make_async_copy(
            piece.at[j],
            whole.at[pl.ds(pl.multiple_of(start, 32), piece.shape[1]), pl.ds(j * columns, columns)],
            sems.at[j, i],
        )
        for j in range(2)
        for i, (piece, start) in enumerate(zip(pieces, starts))
    ]


def each_count(meta, slot, most, body):
    for n in range(1, most // CHUNK + 1):
        pl.when(meta[12 + slot] == n)(functools.partial(body, n * CHUNK))


def memory_kernel(meta, memory, *refs):
    pieces, (out, whole, sems) = refs[:6], refs[6:]
    slot = pl.program_id(0)

    @pl.when(slot == 0)
    def _():
        copies = copies_beside(meta, pieces, whole, sems, WAY_X)
        start_all(copies)
        wait_all(copies)

    def project(rows):
        out[0, :rows, :] = mm(memory[0, :rows, :], whole[...]).astype(bf16)

    each_count(meta, slot, memory.shape[1], project)


def buckets_of(length):
    key_at = lax.broadcasted_iota(jnp.int32, (length, length), 0)
    distance = jnp.maximum(lax.broadcasted_iota(jnp.int32, (length, length), 1) - key_at, 0)
    bucket = jnp.minimum(distance, 16)
    for edge in bucket_edges:
        bucket = bucket + (distance >= edge).astype(jnp.int32)
    return bucket


def self_kernel(meta, tokens, gains, table, *refs):
    pieces = refs[:6]
    bias, normed_out, q_out, k_out, v_out, mixed_out, lse_out, whole, sems = refs[6:]
    copies = copies_in(meta, pieces, whole, sems, WAY_Z)
    start_all(copies)
    hidden = tokens[...].astype(f32)
    normed = (hidden * norm_rho(hidden) * gains[0:1]).astype(bf16)
    normed_out[...] = normed
    length = bias.shape[1]
    bucket = buckets_of(length)
    for head in range(H):
        block = jnp.zeros((length, length), f32)
        for n in range(BUCKETS):
            block = jnp.where(bucket == n, table[n, head], block)
        at = head % QUAD * length
        bias[head // QUAD, :, at : at + length] = block
    wait_all(copies)
    q_out[...] = mm(normed, whole[0]).astype(bf16)
    k_out[...] = mm(normed, whole[1]).astype(bf16)
    v_out[...] = mm(normed, whole[2]).astype(bf16)
    length = bias.shape[1]
    masks = head_masks()
    key_at = lax.broadcasted_iota(jnp.int32, (length, QUAD * length), 0)
    query_at = lax.broadcasted_iota(jnp.int32, (length, QUAD * length), 1) % length
    for b in range(lse_out.shape[0]):
        rows = slice(b * length, (b + 1) * length)
        ok = (key_at <= query_at) & (key_at < meta[4 + b])
        for quad in range(QUADS):
            at = slice(quad * WIDE, (quad + 1) * WIDE)
            scores = mm_nt(k_out[rows, at], stack_heads(q_out[rows, at], masks)) + bias[quad]
            scores = jnp.where(ok, scores, MASKED)
            top = jnp.max(scores, axis=0, keepdims=True)
            raised = jnp.exp(scores - top)
            total = jnp.sum(raised, axis=0, keepdims=True)
            weights = (raised * (1.0 / total)).astype(bf16)
            mixed_out[rows, at] = own_heads(mm(v_out[rows, at].T, weights)).astype(bf16)
            lse_out[b, quad : quad + 1, :] = top + jnp.log(total)


def query_kernel(meta, tokens, mixed, gains, *refs):
    pieces, (h1_out, normed2_out, q2_out, whole, sems) = refs[:6], refs[6:]
    copies = copies_in(meta, pieces, whole, sems, WAY_X, pl.ds(0, 2))
    start_all(copies)
    wait_all(copies)
    first = tokens[...].astype(f32) + mm(mixed[...], whole[0])
    h1_out[...] = first
    normed2 = (first * norm_rho(first) * gains[1:2]).astype(bf16)
    normed2_out[...] = normed2
    q2_out[...] = mm(normed2, whole[1]).astype(bf16)


def mask_last(scores, ok):
    last = scores.shape[0] - CHUNK
    masked = jnp.where(ok, scores[last:], MASKED)
    return jnp.concatenate([scores[:last], masked], axis=0) if last else masked


def cross_kernel(meta, queries, memory, mixed_out, lse_out):
    slot = pl.program_id(0)
    model = queries.shape[2]

    @pl.when(meta[12 + slot] == 0)
    def _():
        mixed_out[...] = jnp.zeros(mixed_out.shape, bf16)
        lse_out[...] = jnp.zeros(lse_out.shape, f32)

    def attend(rows):
        masks = head_masks()
        ok = lax.broadcasted_iota(jnp.int32, (CHUNK, 1), 0) + (rows - CHUNK) < meta[8 + slot]
        for quad in range(QUADS):
            at, at_v = slice(quad * WIDE, (quad + 1) * WIDE), slice(model + quad * WIDE, model + (quad + 1) * WIDE)
            stacked = stack_heads(queries[0, :, at], masks)
            scores = mask_last(mm_nt(memory[0, :rows, at], stacked), ok)
            top = jnp.max(scores, axis=0, keepdims=True)
            raised = jnp.exp(scores - top)
            total = jnp.sum(raised, axis=0, keepdims=True)
            mixed = mm(memory[0, :rows, at_v].T, raised.astype(bf16))
            mixed_out[0, :, at] = own_heads(mixed * (1.0 / total)).astype(bf16)
            lse_out[0, quad : quad + 1, :] = top + jnp.log(total)

    each_count(meta, slot, memory.shape[1], attend)


def gelu_both(values):
    scale = math.sqrt(2.0 / math.pi)
    square = values * values
    slope = jnp.tanh(scale * values * (1.0 + 0.044715 * square))
    half = 0.5 * (1.0 + slope)
    back = half + 0.5 * values * (1.0 - slope * slope) * (scale * (1.0 + 3 * 0.044715 * square))
    return values * half, back


def live_rows(meta, slots, length):
    positions = lax.broadcasted_iota(jnp.int32, (length, 1), 0)
    return jnp.concatenate(
        [((positions < meta[4 + b]) & (b < meta[2])).astype(f32) for b in range(slots)], axis=0
    )


def ff_kernel(meta, h1, mixed, cotangent, gains, *refs):
    square, wide, narrow, refs = refs[:6], refs[6:12], refs[12:18], refs[18:]
    (output, g2_out, ga2_out, gain_out, keep_n, send_n, keep_w, send_w, keep_o, send_o), refs = refs[:10], refs[10:]
    co, w_in, w_out, gf, normed, grad_n, grad_w, grad_o, second, third, back, in_sems, n_sems, w_sems, o_sems = refs
    model = h1.shape[1]
    rows = model // 4
    shard = meta[0]
    co_in = copies_in(meta, square, co, in_sems.at[0], WAY_X, pl.ds(2, 1))
    in_in = copies_in(meta, wide, w_in, in_sems.at[1], WAY_Z)
    out_in = copies_in(meta, narrow, w_out, in_sems.at[2], WAY_X)
    start_all(co_in)
    start_all(in_in)
    start_all(out_in)
    live = live_rows(meta, cotangent.shape[0], cotangent.shape[1])
    gf[...] = (cotangent[...].reshape(h1.shape).astype(f32) * live).astype(bf16)
    wait_all(co_in)
    second[...] = h1[...] + mm(mixed[...], co[0])
    hidden = second[...]
    normed[...] = (hidden * norm_rho(hidden) * gains[2:3]).astype(bf16)
    normed_t = normed[...].T
    wait_all(in_in)
    waits = []
    for j in range(4):
        cols = pl.ds(pl.multiple_of((shard ^ j) * model, model), model)
        units, slope = gelu_both(mm(normed[...], w_in[0, :, cols]))
        low = units.astype(bf16)
        if j == 0:
            wait_all(out_in)
        wide_out = mm(low, w_out[0, cols, :])
        grad_n[j] = mm_tn(low, gf[...]).astype(bf16)
        waits.append(pltpu.make_async_copy(grad_n.at[j], (send_n if j % 2 else keep_n).at[j // 2], n_sems.at[j]))
        waits[-1].start()
        grad_units = (mm_nt(gf[...], w_out[0, cols, :]) * slope).astype(bf16)
        grad_w[j] = mm(normed_t, grad_units).astype(bf16)
        at = pl.ds(pl.multiple_of((shard ^ j) * rows, 32), rows)
        for i in range(4):
            waits.append(
                pltpu.make_async_copy(
                    grad_w.at[j, pl.ds(pl.multiple_of((shard ^ i) * rows, 32), rows)],
                    (send_w if i % 2 else keep_w).at[i // 2, at],
                    w_sems.at[4 * j + i],
                )
            )
            waits[-1].start()
        grad_normed = mm_nt(grad_units, w_in[0, :, cols])
        if j == 0:
            third[...] = second[...] + wide_out
            back[...] = grad_normed
        else:
            third[...] += wide_out
            back[...] += grad_normed
    output[...] = (third[...] * live).astype(bf16)
    grad, gain = norm_back(second[...], gains[2:3], back[...])
    gain_out[...] = jnp.broadcast_to(gain, gain_out.shape)
    g2 = gf[...].astype(f32) + grad
    g2_out[...] = g2
    go2 = g2.astype(bf16)
    ga2_out[...] = mm_nt(go2, co[0]).astype(bf16)
    grad_o[...] = mm_tn(mixed[...], go2).astype(bf16)
    out = copies_out(meta, grad_o, keep_o, send_o, 0, o_sems)
    start_all(out)
    wait_all(waits)
    wait_all(out)


def cross_back_kernel(meta, queries, grads, mixed, lse, memory, gq_out, out):
    slot = pl.program_id(0)
    model = queries.shape[2]

    @pl.when(meta[12 + slot] == 0)
    def _():
        gq_out[...] = jnp.zeros(gq_out.shape, bf16)

    def attend(rows):
        masks = head_masks()
        ok = lax.broadcasted_iota(jnp.int32, (CHUNK, 1), 0) + (rows - CHUNK) < meta[8 + slot]
        for quad in range(QUADS):
            at, at_v = slice(quad * WIDE, (quad + 1) * WIDE), slice(model + quad * WIDE, model + (quad + 1) * WIDE)
            q_stack = stack_heads(queries[0, :, at], masks)
            g_stack = stack_heads(grads[0, :, at], masks)
            tiled = jnp.concatenate([mixed[0, :, at].astype(f32)] * QUAD, axis=0)
            delta = head_sums(g_stack.astype(f32) * tiled)
            block = memory[0, :rows, at]
            scores = mask_last(mm_nt(block, q_stack), ok)
            share = jnp.exp(scores - lse[0, quad : quad + 1, :])
            grad_share = mm_nt(memory[0, :rows, at_v], g_stack)
            grad_scores = (share * (grad_share - delta)).astype(bf16)
            out[0, :rows, at_v] = mm(share.astype(bf16), g_stack).astype(bf16)
            out[0, :rows, at] = mm(grad_scores, q_stack).astype(bf16)
            gq_out[0, :, at] = own_heads(mm(block.T, grad_scores)).astype(bf16)

    each_count(meta, slot, memory.shape[1], attend)


def table_grad(scores):
    length = scores.shape[1]
    bucket = jnp.concatenate([buckets_of(length)] * QUAD, axis=1)
    head = lax.broadcasted_iota(jnp.int32, (QUAD * length, 128), 0) // length
    column = lax.broadcasted_iota(jnp.int32, (QUAD * length, 128), 1)
    table = jnp.zeros((BUCKETS, 128), f32)
    for quad in range(QUADS):
        values = scores[quad]
        sums = [jnp.sum(jnp.where(bucket == n, values, 0.0), axis=0, keepdims=True) for n in range(BUCKETS)]
        sums = jnp.concatenate(sums, axis=0)
        high = sums.astype(bf16)
        low = (sums - high.astype(f32)).astype(bf16)
        to_head = (column == head + quad * QUAD).astype(f32).astype(bf16)
        table = table + mm(high, to_head) + mm(low, to_head)
    return table


def self_back_kernel(
    meta, gq2, normed2, h1, g2, mixed, q, k, v, lse, normed, tokens, gains, bias, keep_in, send_in, *refs
):
    query, pieces, refs = refs[:6], refs[6:12], refs[12:]
    (grad_out, gain_out, bias_out, keep, send, keep_s, send_s), refs = refs[:7], refs[7:]
    square, whole, grads, ga1, gq, gk, gv, in_sems, sems = refs
    copies_q = copies_in(meta, query, square, in_sems.at[0], WAY_X, pl.ds(0, 2))
    copies = copies_in(meta, pieces, whole, in_sems.at[1], WAY_Z)
    start_all(copies_q)
    start_all(copies)
    outs = []

    def emit(index, value, *place):
        grads[index] = value.astype(bf16)
        outs.extend(copies_out(meta, grads.at[index], *place, sems.at[index]))
        start_all(outs[-4:])

    emit(0, mm_tn(normed2[...], gq2[...]), keep, send, 1)
    wait_all(copies_q)
    grad, gain_two = norm_back(h1[...], gains[1:2], mm_nt(gq2[...], square[1]))
    g1 = g2[...] + grad
    grad_out[...] = g1
    go1 = g1.astype(bf16)
    emit(1, mm_tn(mixed[...], go1), keep, send, 2)
    ga1[...] = mm_nt(go1, square[0]).astype(bf16)
    length = bias.shape[1]
    masks = head_masks()
    key_at = lax.broadcasted_iota(jnp.int32, (length, QUAD * length), 0)
    query_at = lax.broadcasted_iota(jnp.int32, (length, QUAD * length), 1) % length
    for b in range(lse.shape[0]):
        rows = slice(b * length, (b + 1) * length)
        ok = (key_at <= query_at) & (key_at < meta[4 + b])
        for quad in range(QUADS):
            at = slice(quad * WIDE, (quad + 1) * WIDE)
            q_stack = stack_heads(q[rows, at], masks)
            g_stack = stack_heads(ga1[rows, at], masks)
            tiled = jnp.concatenate([mixed[rows, at].astype(f32)] * QUAD, axis=0)
            delta = head_sums(g_stack.astype(f32) * tiled)
            block = k[rows, at]
            scores = jnp.where(ok, mm_nt(block, q_stack) + bias[quad], MASKED)
            share = jnp.exp(scores - lse[b, quad : quad + 1, :])
            grad_share = mm_nt(v[rows, at], g_stack)
            grad_scores = (share * (grad_share - delta)).astype(bf16)
            gv[rows, at] = mm(share.astype(bf16), g_stack).astype(bf16)
            gk[rows, at] = mm(grad_scores, q_stack).astype(bf16)
            gq[rows, at] = own_heads(mm(block.T, grad_scores)).astype(bf16)
            if b == 0:
                bias_out[quad] = grad_scores.astype(f32)
            else:
                bias_out[quad] += grad_scores.astype(f32)
    normed_t = normed[...].T
    emit(2, mm(normed_t, gq[...]), keep, send, 3)
    emit(3, mm(normed_t, gk[...]), keep_s, send_s, 0)
    emit(4, mm(normed_t, gv[...]), keep_s, send_s, 1)
    wait_all(copies)
    grad_normed = mm_nt(gq[...], whole[0]) + mm_nt(gk[...], whole[1]) + mm_nt(gv[...], whole[2])
    grad, gain_one = norm_back(tokens[...].astype(f32), gains[0:1], grad_normed)
    grad_out[...] += grad
    gain_out[...] = jnp.concatenate([gain_one, gain_two, jnp.zeros((6, gain_one.shape[1]), f32)], axis=0)
    wait_all(outs)


def memory_weight_kernel(meta, memory, grads, gain_low, gain_three, scores, keep, send, total, low, tiny, sems):
    slot = pl.program_id(0)
    model = memory.shape[2]

    @pl.when(slot == 0)
    def _():
        total[...] = jnp.zeros(total.shape, f32)
        top = jnp.concatenate([gain_low[0:2], gain_three[0:1], jnp.zeros((5, model), f32)], axis=0)
        table = jnp.pad(table_grad(scores), ((0, 0), (0, model - 128)))
        rest = jnp.zeros((TINY - 8 - BUCKETS, model), f32)
        tiny[...] = jnp.concatenate([top, table, rest], axis=0).astype(bf16)

    def add(rows):
        total[...] += mm(memory[0, :rows, :].T, grads[0, :rows, :])

    each_count(meta, slot, memory.shape[1], add)

    @pl.when(slot == pl.num_programs(0) - 1)
    def _():
        rows = model // 4
        outs = [
            pltpu.make_async_copy(
                tiny,
                (send if j % 2 else keep).at[j // 2, pl.ds(2 * rows, tiny.shape[0])],
                sems.at[2, j],
            )
            for j in range(4)
        ]
        start_all(outs)
        for i in range(2):
            low[i] = total[:, i * model : (i + 1) * model].astype(bf16)
            outs += copies_out(meta, low.at[i], keep, send, i, sems.at[i])
            start_all(outs[-4:])
        wait_all(outs)


def memory_grad_kernel(meta, grads, *refs):
    pieces, (out, whole, sems) = refs[:6], refs[6:]
    slot = pl.program_id(0)

    @pl.when(slot == 0)
    def _():
        copies = copies_beside(meta, pieces, whole, sems, WAY_X)
        start_all(copies)
        wait_all(copies)

    def fill(rows):
        if rows:
            out[0, :rows, :] = mm_nt(grads[0, :rows, :], whole[...])
        if rows < out.shape[1]:
            out[0, rows:, :] = jnp.zeros((out.shape[1] - rows, out.shape[2]), f32)

    pl.when(meta[12 + slot] == 0)(functools.partial(fill, 0))
    each_count(meta, slot, out.shape[1], fill)


VMEM = pl.BlockSpec(memory_space=pltpu.VMEM)
ANY = pl.BlockSpec(memory_space=pl.ANY)


def cost(flops, moved, raised=0):
    del flops, moved, raised
    return pl.CostEstimate(flops=1024, bytes_accessed=1024, transcendentals=0)


def shape(dims, dtype):
    return jax.ShapeDtypeStruct(tuple(dims), dtype)


def live_slot(b, meta):
    return jnp.where(meta[12 + b] > 0, b, jnp.maximum(meta[2] - 1, 0))


def by_slot(rows, model, held=False):
    if held:
        return pl.BlockSpec((1, rows, model), lambda b, meta: (live_slot(b, meta), 0, 0))
    return pl.BlockSpec((1, rows, model), lambda b, meta: (b, 0, 0))


class Steps:
    def __init__(self, meta):
        self.meta = meta
        self.token = meta
        self.marks = []
        self.last = None
        self.pending = []
        self.fresh = False

    def call(self, kernel, outs, in_specs, out_specs, scratch, estimate, operands, grid=(), aliases=None, after=None):
        count = len(outs)
        order = [self.token]
        if self.marks:
            order.extend(self.marks)
        first = 1 + len(order)

        def body(meta, *refs):
            refs = refs[len(order) :]
            ins, rest = refs[: len(operands)], refs[len(operands) :]
            kernel(meta, *ins, *rest[:count], *rest[count + 1 :])

        result = pl.pallas_call(
            body,
            out_shape=tuple(outs) + (shape((16, 128), f32),),
            grid_spec=pltpu.PrefetchScalarGridSpec(
                num_scalar_prefetch=1,
                grid=grid,
                in_specs=[ANY] * len(order) + list(in_specs),
                out_specs=tuple(out_specs) + (ANY,),
                scratch_shapes=scratch,
            ),
            input_output_aliases={first + i: o for i, o in (aliases or {}).items()},
            compiler_params=pltpu.CompilerParams(vmem_limit_bytes=56 * 1024 * 1024),
            cost_estimate=estimate,
        )(self.meta, *order, *operands)
        self.token, self.marks = result[-1], []
        return result[:-1]

    def mark(self, result):
        self.marks.append(result)

    def gate(self, *values):
        outs = self.call(
            lambda *refs: None,
            [shape(v.shape, v.dtype) for v in values],
            [ANY] * len(values),
            [ANY] * len(values),
            [],
            cost(0, 0),
            values,
            aliases={i: i for i in range(len(values))},
        )
        return outs


class Bundle:
    def __init__(self, own, place, bit):
        rows = own.shape[1] // 2
        self.own, self.bit = own, bit
        self.half = lax.dynamic_slice_in_dim(own, (place // bit) % 2 * rows, rows, 1)

    def send(self):
        self.direct = flip(self.half, "fsdp", 2)
        self.beside = flip(self.own, "fsdp", 1)

    def hand_on(self):
        self.passed = flip(self.direct, "dp", self.bit)
        self.direct_beside = flip(self.direct, "fsdp", 1)

    def end(self):
        self.passed_beside = flip(self.passed, "fsdp", 1)

    def pieces(self):
        return (self.own, self.beside, self.direct, self.passed, self.direct_beside, self.passed_beside)


class Piece:
    def __init__(self, steps, place, outs, blocks, tall=True):
        self.steps, self.outs, self.blocks = steps, outs, blocks
        self.place, self.tall = place, tall and lax.axis_size("dp") > 2

    def ready(self, keep, send):
        self.keep, self.send = keep, send
        self.steps.pending.append(self)

    def add(self, left, right):
        return (left.astype(f32) + right.astype(f32)).astype(bf16)

    def cut(self, which, axis):
        half = self.keep.shape[axis] // 2
        return [lax.dynamic_slice_in_dim(v, which * half, half, axis) for v in (self.keep, self.got)]

    def core(self):
        far = self.add(self.keep[1], self.got[1])
        self.keep, self.got = self.add(self.keep[0], self.got[0]), flip(far, "fsdp", 2)
        self.steps.mark(far)

    def halve(self, bit, axis):
        side = self.place // bit % 2
        send = self.add(*self.cut(1 - side, axis))
        self.keep, self.got = self.add(*self.cut(side, axis)), flip(send, "dp", bit)
        self.steps.mark(send)

    def y(self):
        self.halve(1, 1)

    def x(self):
        if self.tall:
            self.halve(2, 0)
        else:
            self.pass_on(2)

    def pass_on(self, bit):
        self.keep = self.add(self.keep, self.got)
        self.got = flip(self.keep, "dp", bit)
        self.steps.mark(self.keep)

    def z(self):
        bit = 4
        while bit < lax.axis_size("dp"):
            self.pass_on(bit)
            bit *= 2

    def w(self):
        self.pass_on(2 if self.tall else 1)

    def joined(self, axis, bit, dtype, rows=slice(None)):
        mine, other = self.keep[rows].astype(dtype), self.got[rows].astype(dtype)
        low = self.place // bit % 2 == 0
        return jnp.concatenate([jnp.where(low, mine, other), jnp.where(low, other, mine)], axis=axis)

    def v(self):
        self.keep = self.joined(0, 2, bf16)
        self.got = flip(self.keep, "dp", 1)
        self.steps.mark(self.keep)

    def end(self):
        at = 0
        parts = {}
        for which, _ in self.blocks:
            rows = self.outs[which][0]
            parts.setdefault(which, []).append(self.joined(1, 1, f32, slice(at, at + rows)))
            at += rows
        self.result = [jnp.concatenate(parts[which], axis=1) for which in range(len(self.outs))]
        self.steps.mark(self.result[0])


ORDER = (
    "!",
    ("W1.core",),
    ("W2.core",),
    "KE",
    ("W1.y",),
    "KF",
    ("W2.y", "W1.x"),
    "!",
    ("S1.core", "S2.core"),
    "KW",
    ("S1.y", "W2.x", "W1.z"),
    "!",
    ("M.core",),
    "KG",
    ("S1.x", "W2.z", "W1.w", "S2.y"),
    ("M.y",),
    "|",
    ("W2.w", "S2.x", "S1.z", "W1.v"),
    "|",
    ("M.x",),
    "|",
    ("S2.z", "S1.w"),
    ("W2.v",),
    ("M.z",),
    "|",
    ("S1.v", "S2.w", "M.w"),
    ("S2.v",),
    ("M.v",),
    ("W1.end", "W2.end", "S1.end", "S2.end", "M.end"),
)


def on_device(
    tokens,
    memory,
    tgt_len,
    enc_len,
    ex_count,
    self_gain,
    self_q,
    self_k,
    self_v,
    self_out,
    rel_bias,
    cross_gain,
    cross_q,
    cross_k,
    cross_v,
    cross_out,
    ff_gain,
    ff_in,
    ff_out,
    cotangent,
):
    slots, length, model = tokens.shape
    enc = memory.shape[1]
    hidden = ff_in.shape[1]
    rows = self_q.shape[0]
    total = slots * length
    shard = lax.axis_index("fsdp")
    place = lax.axis_index("dp")
    live = jnp.arange(slots, dtype=jnp.int32) < ex_count[0]
    chunks = jnp.where(live, (enc_len + CHUNK - 1) // CHUNK, 0)
    first = jnp.stack([shard, place % 2, ex_count[0], place // 2 % 2])
    meta = jnp.concatenate([first, tgt_len, enc_len, chunks, place[None]])
    steps = Steps(meta)

    kv = Bundle(jnp.stack([cross_k, cross_v]), place, 1)
    qkv = Bundle(jnp.stack([self_q, self_k, self_v]), place, 2)
    outs = Bundle(jnp.stack([self_out, cross_q, cross_out]), place, 1)
    wide = Bundle(ff_in[None], place, 2)
    narrow = Bundle(ff_out[None], place, 1)
    packed = jnp.concatenate([self_gain, cross_gain, ff_gain, rel_bias.reshape(-1)])
    packed = jnp.pad(packed, (0, model - packed.shape[0]))[None]
    kv.send()
    qkv.send()
    kv.direct, outs.half, packed, far = steps.gate(kv.direct, outs.half, packed, flip(packed, "fsdp", 2))
    kv.hand_on()
    outs.send()
    pair = jnp.concatenate([packed, far], axis=0)
    beside = flip(pair, "fsdp", 1)
    kv.passed, qkv.direct, wide.half, narrow.half, beside = steps.gate(
        kv.passed, qkv.direct, wide.half, narrow.half, beside
    )
    near = jnp.stack([pair[0:1], beside[0:1], pair[1:2], beside[1:2]])
    kv.end()
    qkv.hand_on()
    wide.send()
    narrow.send()
    small = jnp.concatenate([pick(near, shard ^ j) for j in range(4)], axis=0)
    gains = small[:, : 3 * rows].reshape(4, 3, rows).transpose(1, 0, 2).reshape(3, model).astype(f32)
    gains = jnp.pad(gains, ((0, 5), (0, 0)))
    table = small[:, 3 * rows : 3 * rows + rel_bias.size].reshape(-1, H).astype(f32)
    kv.passed_beside, gains, table = steps.gate(kv.passed_beside, gains, table)
    stacked = QUAD * length
    slot_rows = by_slot(length, model)
    enc_rows = by_slot(enc, model, held=True)
    unit = 2 * total * model * model
    enc_unit = 2 * slots * enc * model * model
    attend_unit = 2 * slots * enc * length * model * QUAD
    flat = tokens.reshape(total, model)
    by_slots = (slots, length, model)
    low = shape((total, model), bf16)
    wide_f32 = shape((total, model), f32)
    lse_spec = by_slot(8, stacked)
    gain_shape = shape((8, model), f32)
    sems = pltpu.SemaphoreType.DMA

    enc_wide = by_slot(enc, 2 * model, held=True)
    both = shape((slots, enc, 2 * model), bf16)
    beside = [pltpu.VMEM((model, 2 * model), bf16), sems((2, 6))]
    (keys_values,) = steps.call(
        memory_kernel,
        [both],
        [enc_rows] + [ANY] * 6,
        [enc_wide],
        beside,
        cost(2 * enc_unit, 6 * memory.size),
        [memory, *kv.pieces()],
        grid=(slots,),
    )
    qkv.passed, outs.direct = steps.gate(qkv.passed, outs.direct)
    outs.hand_on()
    qkv.end()
    bias, normed1, q1, k1, v1, a1, lse1 = steps.call(
        self_kernel,
        [shape((QUADS, length, stacked), f32), low, low, low, low, low, shape((slots, 8, stacked), f32)],
        [VMEM] * 2 + [pl.BlockSpec(memory_space=pltpu.SMEM)] + [ANY] * 6,
        [VMEM] * 7,
        [pltpu.VMEM((3, model, model), bf16), sems((6,))],
        cost(3 * unit + attend_unit / 4, 12 * total * model, slots * H * length * length),
        [flat, gains, table, *qkv.pieces()],
    )
    outs.passed, wide.direct = steps.gate(outs.passed, wide.direct)
    outs.end()
    wide.hand_on()
    h1, normed2, q2 = steps.call(
        query_kernel,
        [wide_f32, low, low],
        [VMEM] * 3 + [ANY] * 6,
        [VMEM] * 3,
        [pltpu.VMEM((2, model, model), bf16), sems((6,))],
        cost(2 * unit, 12 * total * model),
        [flat, a1, gains, *outs.pieces()],
    )
    (narrow.direct,) = steps.gate(narrow.direct)
    narrow.hand_on()
    a2, lse2 = steps.call(
        cross_kernel,
        [shape(by_slots, bf16), shape((slots, 8, stacked), f32)],
        [slot_rows, enc_wide],
        [slot_rows, lse_spec],
        [],
        cost(2 * attend_unit, 4 * memory.size, slots * H * length * enc),
        [q2.reshape(by_slots), keys_values],
        grid=(slots,),
    )
    wide.passed, narrow.passed = steps.gate(wide.passed, narrow.passed)
    wide.end()
    narrow.end()
    flat2 = a2.reshape(total, model)

    pair = [(rows, model)] * 2
    order = [(0, 0), (1, 0)]
    pieces = {
        "W1": Piece(steps, place, [(rows, hidden)], [(0, c * model) for c in range(4)]),
        "W2": Piece(steps, place, [(hidden // 4, model)], [(0, 0)]),
        "S1": Piece(steps, place, [(rows, model)] * 4, [(i, 0) for i in range(4)]),
        "S2": Piece(steps, place, pair, order),
        "M": Piece(steps, place, pair + [(TINY, model)], order + [(2, 0)]),
    }
    one = shape((2, 4 * rows, model), bf16)
    half = shape((2, 2 * rows, model), bf16)
    tall = pltpu.VMEM((total, model), f32)
    slim = pltpu.VMEM((total, model), bf16)
    output, g2, ga2, gain_three, keep_n, send_n, keep_w, send_w, keep_o, send_o = steps.call(
        ff_kernel,
        [low, wide_f32, low, gain_shape, one, one, one, one, one, one],
        [VMEM] * 4 + [ANY] * 18,
        [VMEM] * 4 + [ANY] * 6,
        [
            pltpu.VMEM((1, model, model), bf16),
            pltpu.VMEM((1, model, hidden), bf16),
            pltpu.VMEM((1, hidden, model), bf16),
            slim,
            slim,
            pltpu.VMEM((4, model, model), bf16),
            pltpu.VMEM((4, model, model), bf16),
            pltpu.VMEM((model, model), bf16),
            tall,
            tall,
            tall,
            sems((3, 6)),
            sems((4,)),
            sems((16,)),
            sems((4,)),
        ],
        after=0,
        estimate=cost(27 * unit, 40e6, total * hidden),
        operands=[h1, flat2, cotangent, gains, *outs.pieces(), *wide.pieces(), *narrow.pieces()],
    )
    pieces["W1"].ready(keep_w, send_w)
    pieces["W2"].ready(keep_n, send_n)
    got = {}

    def cross_back():
        got["gq2"], got["gkv"] = steps.call(
            cross_back_kernel,
            [shape(by_slots, bf16), both],
            [slot_rows, slot_rows, slot_rows, lse_spec, enc_wide],
            [slot_rows, enc_wide],
            [],
            after=0,
            estimate=cost(5 * attend_unit, 8 * memory.size, slots * H * length * enc),
            operands=[q2.reshape(by_slots), ga2.reshape(by_slots), a2, lse2, keys_values],
            grid=(slots,),
        )

    def self_back():
        got["tokens"], got["gain"], got["scores"], keep, send, keep_s, send_s = steps.call(
            self_back_kernel,
            [wide_f32, gain_shape, shape((QUADS, length, stacked), f32), one, one, half, half],
            [VMEM] * 13 + [ANY] * 14,
            [VMEM] * 3 + [ANY] * 4,
            [
                pltpu.VMEM((2, model, model), bf16),
                pltpu.VMEM((3, model, model), bf16),
                pltpu.VMEM((5, model, model), bf16),
                slim,
                slim,
                slim,
                slim,
                sems((2, 6)),
                sems((5, 4)),
            ],
            cost(10 * unit + attend_unit, 40 * total * model, slots * H * length * length),
            [
                *(got["gq2"].reshape(total, model), normed2, h1, g2, a1, q1, k1, v1, lse1, normed1, flat),
                *(gains, bias, keep_o, send_o, *outs.pieces(), *qkv.pieces()),
            ],
            aliases={13: 3, 14: 4},
            after=0,
        )
        pieces["S1"].ready(keep, send)
        pieces["S2"].ready(keep_s, send_s)

    def memory_weights():
        keep, send = steps.call(
            memory_weight_kernel,
            [shape((2, 2 * rows + TINY, model), bf16)] * 2,
            [
                enc_rows,
                enc_wide,
                pl.BlockSpec((8, model), lambda *_: (0, 0)),
                pl.BlockSpec((8, model), lambda *_: (0, 0)),
                pl.BlockSpec((QUADS, length, stacked), lambda *_: (0, 0, 0)),
            ],
            [ANY, ANY],
            [
                pltpu.VMEM((model, 2 * model), f32),
                pltpu.VMEM((2, model, model), bf16),
                pltpu.VMEM((TINY, model), bf16),
                sems((3, 4)),
            ],
            cost(2 * enc_unit, 6 * memory.size),
            [memory, got["gkv"], got["gain"], gain_three, got["scores"]],
            grid=(slots,),
            after=0,
        )
        pieces["M"].ready(keep, send)

    def memory_back():
        (got["memory"],) = steps.call(
            memory_grad_kernel,
            [shape(memory.shape, f32)],
            [enc_wide] + [ANY] * 6,
            [by_slot(enc, model)],
            beside,
            cost(2 * enc_unit, 8 * memory.size),
            [got["gkv"], *kv.pieces()],
            grid=(slots,),
            after=0,
        )

    kernels = {"KE": cross_back, "KF": self_back, "KW": memory_weights, "KG": memory_back}
    for group in ORDER:
        if group in kernels:
            kernels[group]()
            steps.fresh = True
        elif group == "|":
            steps.fresh = True
        elif group == "!":
            steps.fresh = False
            waiting, steps.pending = steps.pending, []
            sends = steps.gate(*(piece.send for piece in waiting))
            for piece, send in zip(waiting, sends):
                piece.got = flip(send, "fsdp", 1)
        else:
            members = [step.split(".") for step in group]
            if steps.fresh:
                used = list(dict.fromkeys(name for name, _ in members))
                for name, value in zip(used, steps.gate(*(pieces[name].keep for name in used))):
                    pieces[name].keep = value
                steps.fresh = False
            for name, stage in members:
                getattr(pieces[name], stage)()

    sum_co, sum_cq, sum_so, sum_sq = pieces["S1"].result
    sum_sk, sum_sv = pieces["S2"].result
    sum_ck, sum_cv, tiny = pieces["M"].result
    ours = lax.dynamic_slice_in_dim(tiny[0:3], shard * rows, rows, 1)
    ours_table = lax.dynamic_slice_in_dim(tiny[8 : 8 + BUCKETS, :H], shard * rel_bias.shape[0], rel_bias.shape[0], 0)
    return (
        output.reshape(tokens.shape),
        got["tokens"].reshape(tokens.shape),
        got["memory"],
        ours[0],
        sum_sq,
        sum_sk,
        sum_sv,
        sum_so,
        ours_table,
        ours[1],
        sum_cq,
        sum_ck,
        sum_cv,
        sum_co,
        ours[2],
        pieces["W1"].result[0],
        pieces["W2"].result[0],
    )


def solution(mesh):
    in_specs = (
        P(("dp", "fsdp"), None, None),
        P(("dp", "fsdp"), None, None),
        P(("dp", "fsdp")),
        P(("dp", "fsdp")),
        P(("dp", "fsdp")),
        P("fsdp"),
        P("fsdp", None),
        P("fsdp", None),
        P("fsdp", None),
        P("fsdp", None),
        P("fsdp", None),
        P("fsdp"),
        P("fsdp", None),
        P("fsdp", None),
        P("fsdp", None),
        P("fsdp", None),
        P("fsdp"),
        P("fsdp", None),
        P("fsdp", None),
        P(("dp", "fsdp"), None, None),
    )
    out_specs = (
        P(("dp", "fsdp"), None, None),
        P(("dp", "fsdp"), None, None),
        P(("dp", "fsdp"), None, None),
        P("fsdp"),
        P("fsdp", None),
        P("fsdp", None),
        P("fsdp", None),
        P("fsdp", None),
        P("fsdp", None),
        P("fsdp"),
        P("fsdp", None),
        P("fsdp", None),
        P("fsdp", None),
        P("fsdp", None),
        P("fsdp"),
        P("fsdp", None),
        P("fsdp", None),
    )
    return jax.shard_map(
        on_device, mesh=mesh, in_specs=in_specs, out_specs=out_specs, check_vma=False
    )
```
